32 devices in a mesh: box: 8 (over z, y), panel: 4 (over x, core).
Axes of the slice: x: 2, y: 2, z: 4, core: 2. Of those that a mesh axis runs over, the one named last changes fastest.
Arguments:
- field_start: float32 [2048, 2048], P('box', 'panel'), may hold values from -6 to 6
- fluid_mask: int32 [2048, 2048], P('box', 'panel'), may hold values 0 or 1
- base_visc: float32 [2048, 2048], P('box', 'panel'), may hold values from 0.02 to 0.1
- panel_cell: int32 [4096], P(('box', 'panel')), may hold values from 0 to 131071
- amplitude: bfloat16 [4096, 4096], P('box', 'panel'), may hold values from 0.049804688 to 0.5
- delay_bin: int32 [4096, 4096], P('box', 'panel'), may hold values from 0 to 2044
Outputs:
- field_end: float32 [2048, 2048], P('box', 'panel')
- signals: float32 [4096, 2048], P('panel', 'box')
The draws below stay inside these ranges and needn't reach their ends.
Inputs may be any that keep to these rules, and one draw needn't show every extreme that they name: `panel_cell`: an index, row-major, into the 256 x 512 block of the device that owns the panel.
All inputs are finite; a program needn't handle non-finite values. No bound on the sum of `fluid_mask` on one device may be relied on, other than what follows from the above.
Results may differ from the reference program's by a relative error of at most 0.0029.
Values may be sent and summed in bfloat16 or wider, within the bound.
No kernel may reach another device: no remote copies, remote signals or barrier semaphores. Data moves between devices by JAX's collectives and lax.ppermute only.
A program may use at most 64 MiB of HBM per device.

```python
import math
import jax
import jax.numpy as jnp
from jax import lax

CX = 256
CY = 512
PPD = 128
STEPS = 4
OBS = 4096
NB = 2048
NX = 2048
NY = 2048
PANELS = 4096
N_PANEL = 4


def place_ends(array, rng, low, top_value):
    longest = array.shape.index(max(array.shape))
    spots = []
    for shift in (0, 1):
        where = [jax.random.randint(jax.random.fold_in(rng, axis), (), 0, length) for axis, length in enumerate(array.shape)]
        where[longest] = (where[longest] + shift) % array.shape[longest]
        spots.append(tuple(where))
    return array.at[spots[0]].set(low).at[spots[1]].set(top_value)


def level_of(own_key, extent, pieces, least, top_value):
    loudness = 1.0
    for position, shards_of in pieces:
        heights = jax.random.uniform(jax.random.fold_in(jax.random.fold_in(own_key, 6), position), (shards_of,), jnp.float32, least / len(pieces), top_value / len(pieces))
        loudness = loudness * jnp.repeat(jnp.exp(heights), extent[position] // shards_of).reshape((-1,) + (1,) * (len(extent) - 1 - position))
    return loudness


def noise(stream_key, dims, width, most, split=(), kind=jnp.bfloat16):
    drawn = width * jax.random.normal(stream_key, dims, jnp.float32)
    if split:
        drawn = drawn * level_of(stream_key, dims, split, -0.22, 0.18)
    return jnp.clip(drawn, -most, most).astype(kind)


def setup_inputs(seed: int = 0) -> dict:
    seeds = jax.random.split(jax.random.key(seed), 7)
    field_start = noise(seeds[0], (NX, NY), 1.0, 6.0, ((0, 8), (1, 4)), jnp.float32)
    fluid_mask = place_ends((jax.random.randint(seeds[1], (NX, NY), 0, 8) < 7).astype(jnp.int32), jax.random.fold_in(seeds[1], 1), 0, 1)
    base_visc = jnp.clip(jnp.exp(math.log(0.1) - 1.609438 * jax.random.uniform(seeds[2], (NX, NY), jnp.float32) ** level_of(seeds[2], (NX, NY), ((0, 8), (1, 4)), -0.2, 0.2)), 0.02, 0.1)
    panel_cell = place_ends(jax.random.randint(seeds[3], (PANELS,), 0, CX * CY), jax.random.fold_in(seeds[3], 1), 0, (CX * CY) - 1).astype(jnp.int32)
    amplitude = jnp.clip(jnp.exp(math.log(0.5) - 2.306499 * jax.random.uniform(seeds[4], (PANELS, OBS), jnp.float32) ** level_of(seeds[4], (PANELS, OBS), ((0, 8), (1, 4)), -0.2, 0.2)), 0.049804688, 0.5).astype(jnp.bfloat16)
    delay_bin = place_ends(jax.random.randint(seeds[5], (PANELS, OBS), 0, NB - STEPS + 1), jax.random.fold_in(seeds[5], 1), 0, NB - STEPS).astype(jnp.int32)
    return dict(field_start=field_start, fluid_mask=fluid_mask, base_visc=base_visc, panel_cell=panel_cell, amplitude=amplitude, delay_bin=delay_bin)


def advance(ext, mask_c, base_c):
    center = ext[1:-1, 1:-1]
    west = ext[:-2, 1:-1]
    east = ext[2:, 1:-1]
    south = ext[1:-1, :-2]
    north = ext[1:-1, 2:]
    grad_x = 0.5 * (east - west)
    grad_y = 0.5 * (north - south)
    grad_norm = jnp.sqrt(grad_x * grad_x + grad_y * grad_y)
    viscosity = base_c + 0.05 * grad_norm / (1.0 + grad_norm)
    update = center + viscosity * (east + west + north + south - 4.0 * center)
    update = update - 0.15 * (center - west) - 0.1 * (center - south)
    return mask_c * update

def reference(field_start, fluid_mask, base_visc, panel_cell, amplitude, delay_bin):
    owner = (jnp.arange(PANELS, dtype=jnp.int32) // PPD).astype(jnp.int32)
    rows = (owner // N_PANEL * CX + panel_cell // CY).astype(jnp.int32)
    cols = (owner % N_PANEL * CY + panel_cell % CY).astype(jnp.int32)
    maskf = fluid_mask.astype(jnp.float32)
    field = field_start
    taken = []
    for step in range(STEPS):
        field = advance(jnp.pad(field, 1), maskf, base_visc)
        taken.append(field[rows, cols])
    sample = jnp.stack(taken)
    observer_base = (jnp.arange(OBS, dtype=jnp.int32) * NB).astype(jnp.int32)

    def add_block(total, block):
        start = (block * PPD).astype(jnp.int32)
        amp_rows = lax.dynamic_slice_in_dim(amplitude, start, PPD, 0).astype(jnp.float32)
        bin_rows = lax.dynamic_slice_in_dim(delay_bin, start, PPD, 0)
        samp_rows = lax.dynamic_slice_in_dim(sample, start, PPD, 1)
        weight = (amp_rows[None, :, :] * samp_rows[:, :, None]).astype(jnp.bfloat16)
        weight = lax.optimization_barrier(weight).astype(jnp.float32)
        for step in range(STEPS):
            index = (observer_base[None, :] + bin_rows + step).astype(jnp.int32)
            total = total.at[index.reshape(-1)].add(weight[step].reshape(-1))
        return (total, None)
    flat = jnp.zeros((OBS * NB,), jnp.float32)
    flat, unused = lax.scan(add_block, flat, jnp.arange(PANELS // PPD, dtype=jnp.int32))
    return (field, flat.reshape(OBS, NB))
```

```python
import functools

import jax
import jax.numpy as jnp
from jax import lax
from jax.experimental import pallas as pl
from jax.experimental.pallas import tpu as pltpu
from jax.sharding import PartitionSpec as P

F32 = jnp.float32
BF16 = jnp.bfloat16
STEPS = 4
NB = 2048
LOW = 32
LANES = 128
EDGE = 2 * STEPS
PAD = 16
AMP_SCALE = 4096.0
CHUNKS = 2
UNROLL = 4
VMEM = pl.BlockSpec(memory_space=pltpu.VMEM)
SMEM = pl.BlockSpec(memory_space=pltpu.SMEM)


def params(mib):
    return pltpu.CompilerParams(vmem_limit_bytes=mib << 20)


def cost(flops, size):
    return pl.CostEstimate(flops=flops, bytes_accessed=size, transcendentals=0)


def pack_kernel(amp_ref, bin_ref, *outs):
    scaled = (amp_ref[...].astype(F32) * AMP_SCALE).astype(jnp.int32)
    word = jnp.transpose((scaled << 16) | bin_ref[...])
    peers, width, rows = outs[0].shape
    for dest in range(peers):
        for c, out in enumerate(outs):
            first = (dest * len(outs) + c) * width
            out[dest] = word[first : first + width]


def pack(amplitude, delay_bin, peers, chunks):
    panels, observers = amplitude.shape
    width = observers // peers // chunks
    block = pl.BlockSpec((LANES, observers), lambda i: (i, 0))
    out = jax.ShapeDtypeStruct((peers, width, panels), jnp.int32)
    return pl.pallas_call(
        pack_kernel,
        grid=(panels // LANES,),
        in_specs=[block, block],
        out_specs=[pl.BlockSpec((peers, width, LANES), lambda i: (0, 0, i))] * chunks,
        out_shape=[out] * chunks,
        compiler_params=params(32),
        cost_estimate=cost(panels * observers, 10 * panels * observers),
    )(amplitude, delay_bin)


def rows_kernel(field_ref, mask_ref, visc_ref, coded_ref, first_ref, last_ref):
    length = field_ref.shape[0]
    coded = jnp.where(mask_ref[...] != 0, visc_ref[...], 0.0)
    coded_ref[...] = coded
    first_ref[:STEPS] = field_ref[:STEPS]
    first_ref[STEPS:] = coded[:STEPS]
    last_ref[:STEPS] = field_ref[length - STEPS :]
    last_ref[STEPS:] = coded[length - STEPS :]


def columns_kernel(field_ref, coded_ref, before_ref, after_ref, first_ref, last_ref, tall):
    rows, cols = field_ref.shape
    tall[...] = jnp.zeros_like(tall)
    for part, ref in enumerate((field_ref, coded_ref)):
        halo = slice(part * STEPS, (part + 1) * STEPS)
        for start, low, out in ((0, 0, first_ref), (cols - LANES, LANES - STEPS, last_ref)):
            lanes = slice(start, start + LANES)
            tall[:rows] = ref[:, lanes]
            tall[rows : rows + STEPS] = after_ref[halo, lanes]
            tall[rows + STEPS : rows + EDGE] = before_ref[halo, lanes]
            out[halo] = jnp.transpose(tall[...])[low : low + STEPS]


def step_kernel(
    cell_smem,
    cell_ref,
    field_ref,
    coded_ref,
    before_ref,
    after_ref,
    south_ref,
    north_ref,
    end_ref,
    sample_ref,
    fields,
    visc,
    wide,
    picked,
):
    rows, cols = field_ref.shape
    panels = cell_ref.shape[1]
    height, width = visc.shape
    wide[...] = jnp.zeros_like(wide)
    blank = jnp.zeros((PAD, width), F32)
    for part, (ref, buf) in enumerate(((field_ref, fields.at[0]), (coded_ref, visc))):
        halo = slice(part * STEPS, (part + 1) * STEPS)
        wide[:STEPS] = north_ref[halo]
        wide[LANES - STEPS :] = south_ref[halo]
        side = jnp.transpose(wide[...])
        buf[:PAD] = blank
        buf[PAD + rows :] = blank
        buf[PAD : PAD + rows, :cols] = ref[...]
        buf[PAD + rows : PAD + rows + STEPS, :cols] = after_ref[halo]
        buf[PAD - STEPS : PAD, :cols] = before_ref[halo]
        buf[PAD : PAD + rows, cols:] = side[:rows]
        buf[PAD + rows : PAD + rows + STEPS, cols:] = side[rows : rows + STEPS]
        buf[PAD - STEPS : PAD, cols:] = side[rows + STEPS : rows + EDGE]

    strip = 16
    for step in range(STEPS):
        old, new = fields.at[step], fields.at[step + 1]
        new[:8] = jnp.zeros((8, width), F32)
        new[height - 8 :] = jnp.zeros((8, width), F32)

        def one_strip(i, carry):
            top = pl.multiple_of(i * strip, 8)
            window = old[pl.ds(top, strip + 16), :]
            base = visc[pl.ds(top + 8, strip), :]
            center = window[8 : 8 + strip]
            west = window[7 : 7 + strip]
            east = window[9 : 9 + strip]
            south = pltpu.roll(center, 1, 1)
            north = pltpu.roll(center, width - 1, 1)
            grad_x = 0.5 * (east - west)
            grad_y = 0.5 * (north - south)
            grad_norm = jnp.sqrt(grad_x * grad_x + grad_y * grad_y)
            viscosity = base + 0.05 * grad_norm / (1.0 + grad_norm)
            update = center + viscosity * (east + west + north + south - 4.0 * center)
            update = update - 0.15 * (center - west) - 0.1 * (center - south)
            new[pl.ds(top + 8, strip), :] = jnp.where(base > 0.0, update, 0.0)
            return carry

        lax.fori_loop(0, (height - 16) // strip, one_strip, 0)
    end_ref[...] = fields[STEPS, PAD : PAD + rows, :cols]

    def one_panel(k, carry):
        cell = cell_smem[0, k]
        row = cell // cols + PAD
        for step in range(STEPS):
            picked[step, pl.ds(k, 1), :] = fields[step + 1, pl.ds(row, 1), :cols]
        return carry

    lax.fori_loop(0, panels, one_panel, 0, unroll=4)
    column = lax.rem(cell_ref[...], cols)
    chosen = lax.broadcasted_iota(jnp.int32, (cols, panels), 0) == column
    for step in range(STEPS):
        turned = jnp.transpose(picked[step])
        value = jnp.sum(jnp.where(chosen, turned, 0.0), axis=0, keepdims=True)
        sample_ref[:, step, :] = jnp.broadcast_to(value, (sample_ref.shape[0], panels))


def field_window(field, mask, visc, panel_cell):
    rows, cols = field.shape
    tall = -(-(rows + EDGE) // LANES) * LANES
    edge_rows = jax.ShapeDtypeStruct((EDGE, cols), F32)
    edge_cols = jax.ShapeDtypeStruct((EDGE, tall), F32)

    def shifted(axis, first, last):
        peers = lax.axis_size(axis)
        up = [(i, i + 1) for i in range(peers - 1)]
        down = [(i + 1, i) for i in range(peers - 1)]
        return lax.ppermute(last, axis, up), lax.ppermute(first, axis, down)

    coded, first, last = pl.pallas_call(
        rows_kernel,
        in_specs=[VMEM] * 3,
        out_specs=[VMEM] * 3,
        out_shape=[jax.ShapeDtypeStruct((rows, cols), F32), edge_rows, edge_rows],
        compiler_params=params(16),
        cost_estimate=cost(rows * cols, 16 * rows * cols),
    )(field, mask, visc)
    before, after = shifted("box", first, last)
    first, last = pl.pallas_call(
        columns_kernel,
        in_specs=[VMEM] * 4,
        out_specs=[VMEM] * 2,
        out_shape=[edge_cols, edge_cols],
        scratch_shapes=[pltpu.VMEM((tall, LANES), F32)],
        compiler_params=params(16),
        cost_estimate=cost(rows * cols, 4 * rows * cols),
    )(field, coded, before, after)
    south, north = shifted("panel", first, last)
    devices = lax.axis_size("box") * lax.axis_size("panel")
    panels = panel_cell.shape[0]
    cells = panel_cell.reshape(1, panels)
    height, width = rows + 2 * PAD, cols + LANES
    return pl.pallas_call(
        step_kernel,
        in_specs=[SMEM] + [VMEM] * 7,
        out_specs=[VMEM] * 2,
        out_shape=[
            jax.ShapeDtypeStruct((rows, cols), F32),
            jax.ShapeDtypeStruct((devices, STEPS, panels), F32),
        ],
        scratch_shapes=[
            pltpu.VMEM((STEPS + 1, height, width), F32),
            pltpu.VMEM((height, width), F32),
            pltpu.VMEM((LANES, tall), F32),
            pltpu.VMEM((STEPS, panels, cols), F32),
        ],
        compiler_params=params(24),
        cost_estimate=cost(100 * rows * cols, 80 * rows * cols),
    )(cells, cells, field, coded, before, after, south, north)


def bin_kernel(word_ref, sample_ref, out_ref, low_s, high_s, weight_s, acc_s, sig_s):
    sources, block, local = word_ref.shape
    parts = local // LANES
    high = NB // LOW
    span = LOW + 16
    depth = 2 * LANES
    shift = LOW.bit_length() - 1
    for s in range(sources):
        for j in range(parts):
            word = word_ref[s, :, j * LANES : (j + 1) * LANES]
            at = slice((s * parts + j) * LANES, (s * parts + j + 1) * LANES)
            low_s[:, at] = (word & (LOW - 1)).astype(F32)
            high_s[:, at] = ((word >> shift) & (high - 1)).astype(F32)
            amp = (word >> 16).astype(F32) * (1.0 / AMP_SCALE)
            for t in range(STEPS):
                weight_s[t, :, at] = amp * sample_ref[s * parts + j, t : t + 1, :]

    one = jnp.ones((), BF16)
    zero = jnp.zeros((), BF16)
    high_ids = lax.broadcasted_iota(jnp.int32, (high, depth), 0).astype(F32).astype(BF16)
    low_ids = [
        (lax.broadcasted_iota(jnp.int32, (span, depth), 0) - t).astype(F32).astype(BF16)
        for t in range(STEPS)
    ]
    lane = lax.broadcasted_iota(jnp.int32, (NB // LANES, LANES), 1)
    acc_s[...] = jnp.zeros_like(acc_s)

    def spread(row):
        return jnp.broadcast_to(row, (16, depth)).astype(BF16)

    def one_observer(o, u):
        acc = None
        for c in range(sources * local // depth):
            at = slice(c * depth, (c + 1) * depth)
            low_row = spread(low_s[pl.ds(o, 1), at])
            high_row = spread(high_s[pl.ds(o, 1), at])
            weights = [spread(weight_s[t, pl.ds(o, 1), at]) for t in range(STEPS)]
            left = jnp.concatenate(
                [jnp.where(high_ids[k : k + 16] == high_row, one, zero) for k in range(0, high, 16)]
            )
            right = []
            for k in range(0, span, 16):
                placed = zero
                for t in range(1 if k >= LOW else 0, STEPS):
                    placed = jnp.where(low_ids[t][k : k + 16] == low_row, weights[t], placed)
                right.append(placed)
            term = lax.dot_general(
                left, jnp.concatenate(right), (((1,), (1,)), ((), ())), preferred_element_type=F32
            )
            acc = term if acc is None else acc + term
        acc_s[u, :, :span] = acc
        per_row = LANES // LOW
        total = None
        for j in range(per_row):
            x = acc_s[u, pl.ds(j, NB // LANES, stride=per_row), :]
            if j:
                x = pltpu.roll(x, LOW * j, 1)
            if j == per_row - 1:
                x = jnp.where(lane < 16, pltpu.roll(x, 1, 0), x)
            total = x if total is None else total + x
        sig_s[:, pl.ds(o, 1), :] = total[:, None, :]

    unroll = acc_s.shape[0]

    def some_observers(i, carry):
        for u in range(unroll):
            one_observer(i * unroll + u, u)
        return carry

    lax.fori_loop(0, block // unroll, some_observers, 0)
    owners, _, bins = out_ref.shape
    for d in range(owners):
        for r in range(bins // LANES):
            out_ref[d, :, r * LANES : (r + 1) * LANES] = sig_s[d * (bins // LANES) + r].astype(BF16)


def binned(words, samples, owners):
    sources, observers, local = words.shape
    block = 16
    panels = sources * local
    return pl.pallas_call(
        bin_kernel,
        grid=(observers // block,),
        in_specs=[
            pl.BlockSpec((sources, block, local), lambda i: (0, i, 0)),
            pl.BlockSpec(samples.shape, lambda i: (0, 0, 0)),
        ],
        out_specs=pl.BlockSpec((owners, block, NB // owners), lambda i: (0, i, 0)),
        out_shape=jax.ShapeDtypeStruct((owners, observers, NB // owners), BF16),
        scratch_shapes=[
            pltpu.VMEM((block, panels), F32),
            pltpu.VMEM((block, panels), F32),
            pltpu.VMEM((STEPS, block, panels), F32),
            pltpu.VMEM((UNROLL, NB // LOW, LANES), F32),
            pltpu.VMEM((NB // LANES, block, LANES), F32),
        ],
        compiler_params=params(40),
        cost_estimate=cost(65536 * observers * panels, 8 * observers * panels),
    )(words, samples)


def on_device(field_start, fluid_mask, base_visc, panel_cell, amplitude, delay_bin):
    peers = lax.axis_size("box")
    swap = functools.partial(
        lax.all_to_all, axis_name="box", split_axis=0, concat_axis=0, tiled=True
    )
    packed = pack(amplitude, delay_bin, peers, CHUNKS)
    packed, field_start = lax.optimization_barrier((packed, field_start))
    words = [swap(w) for w in packed]
    field, sample = field_window(field_start, fluid_mask, base_visc, panel_cell)
    words[0], sample = lax.optimization_barrier((words[0], sample))
    samples = lax.all_to_all(sample, ("box", "panel"), split_axis=0, concat_axis=0, tiled=True)
    finished = [swap(binned(w, samples, peers)) for w in words]
    signals = jnp.concatenate(finished, axis=1).astype(F32)
    return (field, signals.reshape(-1, signals.shape[-1]))


def solution(mesh):
    placed = (
        P("box", "panel"),
        P("box", "panel"),
        P("box", "panel"),
        P(("box", "panel")),
        P("box", "panel"),
        P("box", "panel"),
    )
    return jax.shard_map(
        on_device,
        mesh=mesh,
        in_specs=placed,
        out_specs=(P("box", "panel"), P("panel", "box")),
        check_vma=False,
    )
```

```python
import functools

import jax
import jax.numpy as jnp
from jax import lax
from jax.experimental import pallas as pl
from jax.experimental.pallas import tpu as pltpu
from jax.sharding import PartitionSpec as P

F32 = jnp.float32
BF16 = jnp.bfloat16
STEPS = 4
NB = 2048
LOW = 32
LANES = 128
EDGE = 2 * STEPS
PAD = 16
AMP_SCALE = 4096.0
LAST = 6
UNROLL = 4
VMEM = pl.BlockSpec(memory_space=pltpu.VMEM)
SMEM = pl.BlockSpec(memory_space=pltpu.SMEM)


def params(mib):
    return pltpu.CompilerParams(vmem_limit_bytes=mib << 20)


def cost(flops, size):
    return pl.CostEstimate(flops=flops, bytes_accessed=size, transcendentals=0)


def pack_kernel(me_ref, amp_ref, bin_ref, *refs):
    outs, turned = refs[:-1], refs[-1]
    scaled = (amp_ref[...].astype(F32) * AMP_SCALE).astype(jnp.int32)
    turned[...] = jnp.transpose((scaled << 16) | bin_ref[...])
    width = outs[0].shape[0]
    for k, out in enumerate(outs):
        first = pl.multiple_of(lax.rem(me_ref[0] + k, len(outs)) * width, 8)
        out[...] = turned[pl.ds(first, width), :]


def pack(me, amplitude, delay_bin, members):
    panels, observers = amplitude.shape
    width = observers // members
    block = pl.BlockSpec((LANES, observers), lambda i: (i, 0))
    out = jax.ShapeDtypeStruct((width, panels), jnp.int32)
    return pl.pallas_call(
        pack_kernel,
        grid=(panels // LANES,),
        in_specs=[SMEM, block, block],
        out_specs=[pl.BlockSpec((width, LANES), lambda i: (0, i))] * members,
        out_shape=[out] * members,
        scratch_shapes=[pltpu.VMEM((observers, LANES), jnp.int32)],
        compiler_params=params(56),
        cost_estimate=cost(panels * observers, 10 * panels * observers),
    )(me, amplitude, delay_bin)


def rows_kernel(field_ref, mask_ref, visc_ref, coded_ref, first_ref, last_ref):
    length = field_ref.shape[0]
    coded = jnp.where(mask_ref[...] != 0, visc_ref[...], 0.0)
    coded_ref[...] = coded
    first_ref[:STEPS] = field_ref[:STEPS]
    first_ref[STEPS:] = coded[:STEPS]
    last_ref[:STEPS] = field_ref[length - STEPS :]
    last_ref[STEPS:] = coded[length - STEPS :]


def columns_kernel(field_ref, coded_ref, before_ref, after_ref, first_ref, last_ref, tall):
    rows, cols = field_ref.shape
    tall[...] = jnp.zeros_like(tall)
    for part, ref in enumerate((field_ref, coded_ref)):
        halo = slice(part * STEPS, (part + 1) * STEPS)
        for start, low, out in ((0, 0, first_ref), (cols - LANES, LANES - STEPS, last_ref)):
            lanes = slice(start, start + LANES)
            tall[:rows] = ref[:, lanes]
            tall[rows : rows + STEPS] = after_ref[halo, lanes]
            tall[rows + STEPS : rows + EDGE] = before_ref[halo, lanes]
            out[halo] = jnp.transpose(tall[...])[low : low + STEPS]


def step_kernel(
    cell_smem,
    cell_ref,
    field_ref,
    coded_ref,
    before_ref,
    after_ref,
    south_ref,
    north_ref,
    end_ref,
    sample_ref,
    fields,
    visc,
    wide,
    picked,
):
    rows, cols = field_ref.shape
    panels = cell_ref.shape[1]
    height, width = visc.shape
    wide[...] = jnp.zeros_like(wide)
    blank = jnp.zeros((PAD, width), F32)
    for part, (ref, buf) in enumerate(((field_ref, fields.at[0]), (coded_ref, visc))):
        halo = slice(part * STEPS, (part + 1) * STEPS)
        wide[:STEPS] = north_ref[halo]
        wide[LANES - STEPS :] = south_ref[halo]
        side = jnp.transpose(wide[...])
        buf[:PAD] = blank
        buf[PAD + rows :] = blank
        buf[PAD : PAD + rows, :cols] = ref[...]
        buf[PAD + rows : PAD + rows + STEPS, :cols] = after_ref[halo]
        buf[PAD - STEPS : PAD, :cols] = before_ref[halo]
        buf[PAD : PAD + rows, cols:] = side[:rows]
        buf[PAD + rows : PAD + rows + STEPS, cols:] = side[rows : rows + STEPS]
        buf[PAD - STEPS : PAD, cols:] = side[rows + STEPS : rows + EDGE]

    strip = 16
    for step in range(STEPS):
        old, new = fields.at[step], fields.at[step + 1]
        new[:8] = jnp.zeros((8, width), F32)
        new[height - 8 :] = jnp.zeros((8, width), F32)

        def one_strip(i, carry):
            top = pl.multiple_of(i * strip, 8)
            window = old[pl.ds(top, strip + 16), :]
            base = visc[pl.ds(top + 8, strip), :]
            center = window[8 : 8 + strip]
            west = window[7 : 7 + strip]
            east = window[9 : 9 + strip]
            south = pltpu.roll(center, 1, 1)
            north = pltpu.roll(center, width - 1, 1)
            grad_x = 0.5 * (east - west)
            grad_y = 0.5 * (north - south)
            grad_norm = jnp.sqrt(grad_x * grad_x + grad_y * grad_y)
            viscosity = base + 0.05 * grad_norm / (1.0 + grad_norm)
            update = center + viscosity * (east + west + north + south - 4.0 * center)
            update = update - 0.15 * (center - west) - 0.1 * (center - south)
            new[pl.ds(top + 8, strip), :] = jnp.where(base > 0.0, update, 0.0)
            return carry

        lax.fori_loop(0, (height - 16) // strip, one_strip, 0)
    end_ref[...] = fields[STEPS, PAD : PAD + rows, :cols]

    def one_panel(k, carry):
        cell = cell_smem[0, k]
        row = cell // cols + PAD
        for step in range(STEPS):
            picked[step, pl.ds(k, 1), :] = fields[step + 1, pl.ds(row, 1), :cols]
        return carry

    lax.fori_loop(0, panels, one_panel, 0, unroll=4)
    column = lax.rem(cell_ref[...], cols)
    chosen = lax.broadcasted_iota(jnp.int32, (cols, panels), 0) == column
    for step in range(STEPS):
        turned = jnp.transpose(picked[step])
        value = jnp.sum(jnp.where(chosen, turned, 0.0), axis=0, keepdims=True)
        sample_ref[step : step + 1, :] = value


def edges(field, mask, visc):
    rows, cols = field.shape
    edge_rows = jax.ShapeDtypeStruct((EDGE, cols), F32)
    return pl.pallas_call(
        rows_kernel,
        in_specs=[VMEM] * 3,
        out_specs=[VMEM] * 3,
        out_shape=[jax.ShapeDtypeStruct((rows, cols), F32), edge_rows, edge_rows],
        compiler_params=params(16),
        cost_estimate=cost(rows * cols, 16 * rows * cols),
    )(field, mask, visc)


def shifted(axis, first, last):
    peers = lax.axis_size(axis)
    up = [(i, i + 1) for i in range(peers - 1)]
    down = [(i + 1, i) for i in range(peers - 1)]
    return lax.ppermute(last, axis, up), lax.ppermute(first, axis, down)


def field_window(field, coded, before, after, panel_cell):
    rows, cols = field.shape
    tall = -(-(rows + EDGE) // LANES) * LANES
    edge_cols = jax.ShapeDtypeStruct((EDGE, tall), F32)

    first, last = pl.pallas_call(
        columns_kernel,
        in_specs=[VMEM] * 4,
        out_specs=[VMEM] * 2,
        out_shape=[edge_cols, edge_cols],
        scratch_shapes=[pltpu.VMEM((tall, LANES), F32)],
        compiler_params=params(16),
        cost_estimate=cost(rows * cols, 4 * rows * cols),
    )(field, coded, before, after)
    south, north = shifted("panel", first, last)
    panels = panel_cell.shape[0]
    cells = panel_cell.reshape(1, panels)
    height, width = rows + 2 * PAD, cols + LANES
    return pl.pallas_call(
        step_kernel,
        in_specs=[SMEM] + [VMEM] * 7,
        out_specs=[VMEM] * 2,
        out_shape=[
            jax.ShapeDtypeStruct((rows, cols), F32),
            jax.ShapeDtypeStruct((STEPS, panels), F32),
        ],
        scratch_shapes=[
            pltpu.VMEM((STEPS + 1, height, width), F32),
            pltpu.VMEM((height, width), F32),
            pltpu.VMEM((LANES, tall), F32),
            pltpu.VMEM((STEPS, panels, cols), F32),
        ],
        compiler_params=params(24),
        cost_estimate=cost(100 * rows * cols, 800 * rows * cols),
    )(cells, cells, field, coded, before, after, south, north)


def bin_kernel(half_ref, *refs):
    members = (len(refs) - 7) // 2
    words, samples = refs[:members], refs[members : 2 * members]
    keep_ref, send_ref, low_s, high_s, weight_s, acc_s, sig_s = refs[2 * members :]
    block, local = words[0].shape
    parts = local // LANES
    high = NB // LOW
    span = LOW + 16
    depth = 2 * LANES
    shift = LOW.bit_length() - 1
    for s in range(members):
        for j in range(parts):
            word = words[s][:, j * LANES : (j + 1) * LANES]
            at = slice((s * parts + j) * LANES, (s * parts + j + 1) * LANES)
            low_s[:, at] = (word & (LOW - 1)).astype(F32)
            high_s[:, at] = ((word >> shift) & (high - 1)).astype(F32)
            amp = (word >> 16).astype(F32) * (1.0 / AMP_SCALE)
            for t in range(STEPS):
                weight_s[t, :, at] = amp * samples[s][j, t : t + 1, :]

    one = jnp.ones((), BF16)
    zero = jnp.zeros((), BF16)
    high_ids = lax.broadcasted_iota(jnp.int32, (high, depth), 0).astype(F32).astype(BF16)
    low_ids = [
        (lax.broadcasted_iota(jnp.int32, (span, depth), 0) - t).astype(F32).astype(BF16)
        for t in range(STEPS)
    ]
    lane = lax.broadcasted_iota(jnp.int32, (NB // LANES, LANES), 1)
    acc_s[...] = jnp.zeros_like(acc_s)

    def spread(row):
        return jnp.broadcast_to(row, (16, depth)).astype(BF16)

    def one_observer(o, u):
        acc = None
        for c in range(members * local // depth):
            at = slice(c * depth, (c + 1) * depth)
            low_row = spread(low_s[pl.ds(o, 1), at])
            high_row = spread(high_s[pl.ds(o, 1), at])
            weights = [spread(weight_s[t, pl.ds(o, 1), at]) for t in range(STEPS)]
            left = jnp.concatenate(
                [jnp.where(high_ids[k : k + 16] == high_row, one, zero) for k in range(0, high, 16)]
            )
            right = []
            for k in range(0, span, 16):
                placed = zero
                for t in range(1 if k >= LOW else 0, STEPS):
                    placed = jnp.where(low_ids[t][k : k + 16] == low_row, weights[t], placed)
                right.append(placed)
            term = lax.dot_general(
                left, jnp.concatenate(right), (((1,), (1,)), ((), ())), preferred_element_type=F32
            )
            acc = term if acc is None else acc + term
        acc_s[u, :, :span] = acc
        per_row = LANES // LOW
        total = None
        for j in range(per_row):
            x = acc_s[u, pl.ds(j, NB // LANES, stride=per_row), :]
            if j:
                x = pltpu.roll(x, LOW * j, 1)
            if j == per_row - 1:
                x = jnp.where(lane < 16, pltpu.roll(x, 1, 0), x)
            total = x if total is None else total + x
        sig_s[:, pl.ds(o, 1), :] = total[:, None, :]

    unroll = acc_s.shape[0]

    def some_observers(i, carry):
        for u in range(unroll):
            one_observer(i * unroll + u, u)
        return carry

    lax.fori_loop(0, block // unroll, some_observers, 0)
    tiles = NB // LANES // 2
    per_owner = tiles // keep_ref.shape[0]
    for r in range(tiles):
        lanes = slice(r % per_owner * LANES, (r % per_owner + 1) * LANES)
        keep_ref[r // per_owner, :, lanes] = sig_s[half_ref[0] * tiles + r]
        sent = sig_s[(1 - half_ref[0]) * tiles + r]
        send_ref[r // per_owner, :, lanes] = sent.astype(BF16)


def binned(half, words, samples, first, count):
    members = len(words)
    local = words[0].shape[1]
    block = 16
    panels = members * local
    bins = NB // 2 // members
    out = pl.BlockSpec((members, block, bins), lambda i: (0, i, 0))
    return pl.pallas_call(
        bin_kernel,
        grid=(count // block,),
        in_specs=[SMEM]
        + [pl.BlockSpec((block, local), lambda i: (first // block + i, 0))] * members
        + [pl.BlockSpec(samples[0].shape, lambda i: (0, 0, 0))] * members,
        out_specs=[out, out],
        out_shape=[
            jax.ShapeDtypeStruct((members, count, bins), F32),
            jax.ShapeDtypeStruct((members, count, bins), BF16),
        ],
        scratch_shapes=[
            pltpu.VMEM((block, panels), F32),
            pltpu.VMEM((block, panels), F32),
            pltpu.VMEM((STEPS, block, panels), F32),
            pltpu.VMEM((UNROLL, NB // LOW, LANES), F32),
            pltpu.VMEM((NB // LANES, block, LANES), F32),
        ],
        compiler_params=params(40),
        cost_estimate=cost(65536 * count * panels, 8 * count * panels),
    )(half, *words, *samples)


def join_kernel(me_ref, keep_ref, got_ref, *outs):
    for k, out in enumerate(outs):
        owner = lax.rem(me_ref[0] + k, len(outs))
        out[...] = (keep_ref[owner] + got_ref[owner].astype(F32)).astype(BF16)


def join(me, keep, got):
    members, count, bins = keep.shape
    return pl.pallas_call(
        join_kernel,
        in_specs=[SMEM, VMEM, VMEM],
        out_specs=[VMEM] * members,
        out_shape=[jax.ShapeDtypeStruct((count, bins), BF16)] * members,
        compiler_params=params(16),
        cost_estimate=cost(keep.size, 8 * keep.size),
    )(me, keep, got)


def place_kernel(firsts, width, me_ref, *refs):
    out_ref, members = refs[-1], (len(refs) - 1) // len(firsts)
    for c, first in enumerate(firsts):
        for k in range(members):
            ref = refs[c * members + k]
            owner = lax.rem(me_ref[0] - k + members, members)
            start = pl.multiple_of(owner * width + first, 16)
            out_ref[pl.ds(start, ref.shape[0]), :] = ref[...].astype(F32)


def on_device(field_start, fluid_mask, base_visc, panel_cell, amplitude, delay_bin):
    peers = lax.axis_size("box")
    members = peers // 2
    index = lax.axis_index("box").astype(jnp.int32).reshape(1)
    me, half = lax.rem(index, members), index // members

    def spread(parts):
        def perm(k):
            return [(i, i // members * members + (i + k) % members) for i in range(peers)]

        return [lax.ppermute(x, "box", perm(k)) if k else x for k, x in enumerate(parts)]

    coded, *ends = edges(field_start, fluid_mask, base_visc)
    amplitude, delay_bin, *ends = lax.optimization_barrier((amplitude, delay_bin, *ends))
    before, after = shifted("box", *ends)
    packed = pack(me, amplitude, delay_bin, members)
    before, after, *packed = lax.optimization_barrier((before, after, *packed))
    words = spread(packed)
    field, sample = field_window(field_start, coded, before, after, panel_cell)
    samples = spread([lax.all_gather(sample, "panel")] * members)
    observers = words[0].shape[0]
    across = [(i, (i + members) % peers) for i in range(peers)]
    pieces, firsts, first = [], [], 0
    for count in sizes(observers):
        keep, send = binned(half, words, samples, first, count)
        got = lax.ppermute(send, "box", across)
        if pieces:
            got, *pieces = lax.optimization_barrier((got, *pieces))
        pieces += spread(join(me, keep, got))
        firsts.append(first)
        first += count
    signals = pl.pallas_call(
        functools.partial(place_kernel, firsts, observers),
        in_specs=[SMEM] + [VMEM] * len(pieces),
        out_specs=VMEM,
        out_shape=jax.ShapeDtypeStruct((observers * members, pieces[0].shape[1]), F32),
        compiler_params=params(16),
    )(me, *pieces)
    return (field, signals)


def sizes(observers):
    last = -(-observers * LAST // 16 // 16) * 16
    return [observers - last, last]


def solution(mesh):
    placed = (
        P("box", "panel"),
        P("box", "panel"),
        P("box", "panel"),
        P(("box", "panel")),
        P("box", "panel"),
        P("box", "panel"),
    )
    return jax.shard_map(
        on_device,
        mesh=mesh,
        in_specs=placed,
        out_specs=(P("box", "panel"), P("panel", "box")),
        check_vma=False,
    )
```

```python
import functools

import jax
import jax.numpy as jnp
from jax import lax
from jax.experimental import pallas as pl
from jax.experimental.pallas import tpu as pltpu
from jax.sharding import PartitionSpec as P

F32 = jnp.float32
BF16 = jnp.bfloat16
STEPS = 4
NB = 2048
LOW = 32
LANES = 128
EDGE = 2 * STEPS
PAD = 16
AMP_SCALE = 4096.0
LAST = 6
VMEM = pl.BlockSpec(memory_space=pltpu.VMEM)
SMEM = pl.BlockSpec(memory_space=pltpu.SMEM)


def params(mib):
    return pltpu.CompilerParams(vmem_limit_bytes=mib << 20)


def cost(flops, size):
    return pl.CostEstimate(flops=flops, bytes_accessed=size, transcendentals=0)


def pack_kernel(me_ref, amp_ref, bin_ref, *refs):
    outs, turned = refs[:-1], refs[-1]
    scaled = (amp_ref[...].astype(F32) * AMP_SCALE).astype(jnp.int32)
    turned[...] = jnp.transpose((scaled << 16) | bin_ref[...])
    width = outs[0].shape[0]
    for k, out in enumerate(outs):
        first = pl.multiple_of(lax.rem(me_ref[0] + k, len(outs)) * width, 8)
        out[...] = turned[pl.ds(first, width), :]


def pack(me, amplitude, delay_bin, members):
    panels, observers = amplitude.shape
    width = observers // members
    block = pl.BlockSpec((LANES, observers), lambda i: (i, 0))
    out = jax.ShapeDtypeStruct((width, panels), jnp.int32)
    return pl.pallas_call(
        pack_kernel,
        grid=(panels // LANES,),
        in_specs=[SMEM, block, block],
        out_specs=[pl.BlockSpec((width, LANES), lambda i: (0, i))] * members,
        out_shape=[out] * members,
        scratch_shapes=[pltpu.VMEM((observers, LANES), jnp.int32)],
        compiler_params=params(56),
        cost_estimate=cost(panels * observers, 10 * panels * observers),
    )(me, amplitude, delay_bin)


def coded(mask, visc):
    return jnp.where(mask != 0, visc, 0.0)


def rows_kernel(f_top, m_top, v_top, f_end, m_end, v_end, first_ref, last_ref):
    first_ref[:STEPS] = f_top[:STEPS]
    first_ref[STEPS:] = coded(m_top[:STEPS], v_top[:STEPS])
    last_ref[:STEPS] = f_end[8 - STEPS :]
    last_ref[STEPS:] = coded(m_end[8 - STEPS :], v_end[8 - STEPS :])


def columns_kernel(
    field_ref, mask_ref, visc_ref, before_ref, after_ref, first_ref, last_ref, tall
):
    rows, cols = field_ref.shape
    tall[...] = jnp.zeros_like(tall)
    for part in range(2):
        halo = slice(part * STEPS, (part + 1) * STEPS)
        for start, low, out in ((0, 0, first_ref), (cols - LANES, LANES - STEPS, last_ref)):
            lanes = slice(start, start + LANES)
            if part:
                tall[:rows] = coded(mask_ref[:, lanes], visc_ref[:, lanes])
            else:
                tall[:rows] = field_ref[:, lanes]
            tall[rows : rows + STEPS] = after_ref[halo, lanes]
            tall[rows + STEPS : rows + EDGE] = before_ref[halo, lanes]
            out[halo] = jnp.transpose(tall[...])[low : low + STEPS]


def step_kernel(
    cell_ref,
    field_ref,
    mask_ref,
    visc_ref,
    before_ref,
    after_ref,
    south_ref,
    north_ref,
    end_ref,
    sample_ref,
    fields,
    visc,
    wide,
):
    rows, cols = field_ref.shape
    panels = sample_ref.shape[1]
    height, width = visc.shape
    wide[...] = jnp.zeros_like(wide)
    blank = jnp.zeros((PAD, width), F32)
    for part, buf in enumerate((fields.at[0], visc)):
        halo = slice(part * STEPS, (part + 1) * STEPS)
        wide[:STEPS] = north_ref[halo]
        wide[LANES - STEPS :] = south_ref[halo]
        side = jnp.transpose(wide[...])
        buf[:PAD] = blank
        buf[PAD + rows :] = blank
        if part:
            buf[PAD : PAD + rows, :cols] = coded(mask_ref[...], visc_ref[...])
        else:
            buf[PAD : PAD + rows, :cols] = field_ref[...]
        buf[PAD + rows : PAD + rows + STEPS, :cols] = after_ref[halo]
        buf[PAD - STEPS : PAD, :cols] = before_ref[halo]
        buf[PAD : PAD + rows, cols:] = side[:rows]
        buf[PAD + rows : PAD + rows + STEPS, cols:] = side[rows : rows + STEPS]
        buf[PAD - STEPS : PAD, cols:] = side[rows + STEPS : rows + EDGE]

    strip = 16
    for step in range(STEPS):
        old, new = fields.at[step], fields.at[step + 1]
        new[:8] = jnp.zeros((8, width), F32)
        new[height - 8 :] = jnp.zeros((8, width), F32)

        def one_strip(i, carry):
            top = pl.multiple_of(i * strip, 8)
            window = old[pl.ds(top, strip + 16), :]
            base = visc[pl.ds(top + 8, strip), :]
            center = window[8 : 8 + strip]
            west = pltpu.roll(window, 1, 0)[8 : 8 + strip]
            east = pltpu.roll(window, strip + 15, 0)[8 : 8 + strip]
            south = pltpu.roll(center, 1, 1)
            north = pltpu.roll(center, width - 1, 1)
            diff_x = east - west
            diff_y = north - south
            square = diff_x * diff_x + diff_y * diff_y
            norm = square * lax.rsqrt(jnp.maximum(square, 1e-37))
            viscosity = base + 0.05 * norm / (2.0 + norm)
            around = (east + west) + (north + south)
            update = 0.75 * center + 0.15 * west + 0.1 * south
            update = update + viscosity * (around - 4.0 * center)
            new[pl.ds(top + 8, strip), :] = jnp.where(base > 0.0, update, 0.0)
            return carry

        lax.fori_loop(0, (height - 16) // strip, one_strip, 0)
    end_ref[...] = fields[STEPS, PAD : PAD + rows, :cols]

    lane = lax.broadcasted_iota(jnp.int32, (8, LANES), 1)
    line = lax.broadcasted_iota(jnp.int32, (8, LANES), 0)
    for base in range(0, panels, LANES):

        def one_panel(k, found):
            cell = cell_ref[0, base + k]
            row = cell // cols
            col = cell - row * cols
            top = pl.multiple_of(row // 8 * 8 + PAD, 8)
            left = pl.multiple_of(col // LANES * LANES, LANES)
            here = (lane == k) & (line == row % 8)
            turn = (k - col) & (LANES - 1)
            return tuple(
                jnp.where(
                    here,
                    pltpu.roll(fields[t + 1, pl.ds(top, 8), pl.ds(left, LANES)], turn, 1),
                    found[t],
                )
                for t in range(STEPS)
            )

        none = (jnp.zeros((8, LANES), F32),) * STEPS
        found = lax.fori_loop(0, LANES, one_panel, none, unroll=8)
        for t in range(STEPS):
            sample_ref[t : t + 1, base : base + LANES] = jnp.sum(found[t], axis=0, keepdims=True)


def edges(field, mask, visc):
    rows, cols = field.shape
    edge_rows = jax.ShapeDtypeStruct((EDGE, cols), F32)
    return pl.pallas_call(
        rows_kernel,
        grid=(1,),
        in_specs=[pl.BlockSpec((8, cols), lambda i: (0, 0))] * 3
        + [pl.BlockSpec((8, cols), lambda i: (rows // 8 - 1, 0))] * 3,
        out_specs=[pl.BlockSpec((EDGE, cols), lambda i: (0, 0))] * 2,
        out_shape=[edge_rows, edge_rows],
        compiler_params=params(56),
        cost_estimate=cost(16 * cols, 256 * cols),
    )(field, mask, visc, field, mask, visc)


def shifted(axis, first, last):
    peers = lax.axis_size(axis)
    up = [(i, i + 1) for i in range(peers - 1)]
    down = [(i + 1, i) for i in range(peers - 1)]
    return lax.ppermute(last, axis, up), lax.ppermute(first, axis, down)


def field_window(field, mask, visc, before, after, panel_cell):
    rows, cols = field.shape
    tall = -(-(rows + EDGE) // LANES) * LANES
    edge_cols = jax.ShapeDtypeStruct((EDGE, tall), F32)

    first, last = pl.pallas_call(
        columns_kernel,
        in_specs=[VMEM] * 5,
        out_specs=[VMEM] * 2,
        out_shape=[edge_cols, edge_cols],
        scratch_shapes=[pltpu.VMEM((tall, LANES), F32)],
        compiler_params=params(16),
        cost_estimate=cost(rows * cols, 4 * rows * cols),
    )(field, mask, visc, before, after)
    south, north = shifted("panel", first, last)
    panels = panel_cell.shape[0]
    cells = panel_cell.reshape(1, panels)
    height, width = rows + 2 * PAD, cols + LANES
    return pl.pallas_call(
        step_kernel,
        in_specs=[SMEM] + [VMEM] * 7,
        out_specs=[VMEM] * 2,
        out_shape=[
            jax.ShapeDtypeStruct((rows, cols), F32),
            jax.ShapeDtypeStruct((STEPS, panels), F32),
        ],
        scratch_shapes=[
            pltpu.VMEM((STEPS + 1, height, width), F32),
            pltpu.VMEM((height, width), F32),
            pltpu.VMEM((LANES, tall), F32),
        ],
        compiler_params=params(24),
        cost_estimate=cost(100 * rows * cols, 800 * rows * cols),
    )(cells, field, mask, visc, before, after, south, north)


def bin_kernel(half_ref, *refs):
    members = (len(refs) - 7) // 2
    words, samples = refs[:members], refs[members : 2 * members]
    keep_ref, send_ref, low_s, high_s, weight_s, acc_s, sig_s = refs[2 * members :]
    block, local = words[0].shape
    parts = local // LANES
    high = NB // LOW
    per_row = LANES // LOW
    half_rows = NB // LANES // 8
    low_tiles = LOW // 8 + 1
    depth = 2 * LANES
    shift = LOW.bit_length() - 1
    for s in range(members):
        for j in range(parts):
            word = words[s][:, j * LANES : (j + 1) * LANES]
            at = slice((s * parts + j) * LANES, (s * parts + j + 1) * LANES)
            low_s[:, at] = (word & (LOW - 1)).astype(F32)
            high_s[:, at] = ((word >> shift) & (high - 1)).astype(F32)
            amp = (word >> 16).astype(F32) * (1.0 / AMP_SCALE)
            for t in range(STEPS):
                weight_s[t, :, at] = amp * samples[s][j, t : t + 1, :]

    one = jnp.ones((), BF16)
    zero = jnp.zeros((), BF16)
    sub = lax.broadcasted_iota(jnp.int32, (16, depth), 0) & 7

    def number(x):
        return x.astype(F32).astype(BF16)

    high_ids = [
        number(per_row * (8 * (k % half_rows) + sub) + k // half_rows) for k in range(high // 8)
    ]
    low_ids = [[number(8 * k + sub - t) for t in range(STEPS)] for k in range(low_tiles)]
    lane = lax.broadcasted_iota(jnp.int32, (8, LANES), 1)
    lanes = lax.broadcasted_iota(jnp.int32, (NB // LANES, LANES), 1)
    acc_s[...] = jnp.zeros_like(acc_s)

    def two_observers(o, u):
        def spread(ref, *lead):
            rows = [
                jnp.broadcast_to(ref[(*lead, slice(o + e, o + e + 1), at)], (8, depth))
                for e in range(2)
            ]
            return jnp.concatenate(rows).astype(BF16)

        acc = None
        for c in range(members * local // depth):
            at = slice(c * depth, (c + 1) * depth)
            low_row, high_row = spread(low_s), spread(high_s)
            weights = [spread(weight_s, t) for t in range(STEPS)]
            left = jnp.concatenate([jnp.where(ids == high_row, one, zero) for ids in high_ids])
            right = []
            for k in range(low_tiles):
                placed = zero
                for t in range(1 if k * 8 >= LOW else 0, STEPS):
                    placed = jnp.where(low_ids[k][t] == low_row, weights[t], placed)
                right.append(placed)
            term = lax.dot_general(
                left, jnp.concatenate(right), (((1,), (1,)), ((), ())), preferred_element_type=F32
            )
            acc = term if acc is None else acc + term
        acc_s[u, :, : 16 * low_tiles] = acc
        for e in range(2):
            total = None
            for j in range(per_row):
                low = (lane - LOW * j) & (LANES - 1)
                source = jnp.where(low < 8 * low_tiles, 16 * (low // 8) + 8 * e + (low & 7), LANES - 1)
                tops = [16 * (j * half_rows + g) + 8 * e for g in range(half_rows)]
                x = jnp.concatenate(
                    [jnp.take_along_axis(acc_s[u, top : top + 8], source, axis=1) for top in tops]
                )
                if j == per_row - 1:
                    x = jnp.where(lanes < LOW, pltpu.roll(x, 1, 0), x)
                total = x if total is None else total + x
            sig_s[:, o + e : o + e + 1, :] = total[:, None, :]

    for u in range(block // 2):
        two_observers(2 * u, u)
    tiles = NB // LANES // 2
    per_owner = tiles // keep_ref.shape[0]
    for r in range(tiles):
        lanes = slice(r % per_owner * LANES, (r % per_owner + 1) * LANES)
        keep_ref[r // per_owner, :, lanes] = sig_s[half_ref[0] * tiles + r]
        sent = sig_s[(1 - half_ref[0]) * tiles + r]
        send_ref[r // per_owner, :, lanes] = sent.astype(BF16)


def binned(half, words, samples, first, count):
    members = len(words)
    local = words[0].shape[1]
    block = 16
    panels = members * local
    bins = NB // 2 // members
    out = pl.BlockSpec((members, block, bins), lambda i: (0, i, 0))
    return pl.pallas_call(
        bin_kernel,
        grid=(count // block,),
        in_specs=[SMEM]
        + [pl.BlockSpec((block, local), lambda i: (first // block + i, 0))] * members
        + [pl.BlockSpec(samples[0].shape, lambda i: (0, 0, 0))] * members,
        out_specs=[out, out],
        out_shape=[
            jax.ShapeDtypeStruct((members, count, bins), F32),
            jax.ShapeDtypeStruct((members, count, bins), BF16),
        ],
        scratch_shapes=[
            pltpu.VMEM((block, panels), F32),
            pltpu.VMEM((block, panels), F32),
            pltpu.VMEM((STEPS, block, panels), F32),
            pltpu.VMEM((block // 2, 2 * NB // LOW, LANES), F32),
            pltpu.VMEM((NB // LANES, block, LANES), F32),
        ],
        compiler_params=params(40),
        cost_estimate=cost(65536 * count * panels, 8 * count * panels),
    )(half, *words, *samples)


def join_kernel(me_ref, keep_ref, got_ref, *outs):
    for k, out in enumerate(outs):
        owner = lax.rem(me_ref[0] + k, len(outs))
        out[...] = (keep_ref[owner] + got_ref[owner].astype(F32)).astype(BF16)


def join(me, keep, got):
    members, count, bins = keep.shape
    return pl.pallas_call(
        join_kernel,
        in_specs=[SMEM, VMEM, VMEM],
        out_specs=[VMEM] * members,
        out_shape=[jax.ShapeDtypeStruct((count, bins), BF16)] * members,
        compiler_params=params(16),
        cost_estimate=cost(keep.size, 8 * keep.size),
    )(me, keep, got)


def place_kernel(firsts, width, me_ref, *refs):
    out_ref, members = refs[-1], (len(refs) - 1) // len(firsts)
    for c, first in enumerate(firsts):
        for k in range(members):
            ref = refs[c * members + k]
            owner = lax.rem(me_ref[0] - k + members, members)
            start = pl.multiple_of(owner * width + first, 16)
            out_ref[pl.ds(start, ref.shape[0]), :] = ref[...].astype(F32)


def on_device(field_start, fluid_mask, base_visc, panel_cell, amplitude, delay_bin):
    peers = lax.axis_size("box")
    members = peers // 2
    index = lax.axis_index("box").astype(jnp.int32).reshape(1)
    me, half = lax.rem(index, members), index // members

    def spread(parts):
        def perm(k):
            return [(i, i // members * members + (i + k) % members) for i in range(peers)]

        return [lax.ppermute(x, "box", perm(k)) if k else x for k, x in enumerate(parts)]

    ends = edges(field_start, fluid_mask, base_visc)
    amplitude, delay_bin, *ends = lax.optimization_barrier((amplitude, delay_bin, *ends))
    before, after = shifted("box", *ends)
    packed = pack(me, amplitude, delay_bin, members)
    before, after, *packed = lax.optimization_barrier((before, after, *packed))
    words = spread(packed)
    field, sample = field_window(
        field_start, fluid_mask, base_visc, before, after, panel_cell
    )
    samples = spread([lax.all_gather(sample, "panel")] * members)
    observers = words[0].shape[0]
    across = [(i, (i + members) % peers) for i in range(peers)]
    pieces, firsts, first = [], [], 0
    for count in sizes(observers):
        keep, send = binned(half, words, samples, first, count)
        got = lax.ppermute(send, "box", across)
        if pieces:
            got, *pieces = lax.optimization_barrier((got, *pieces))
        pieces += spread(join(me, keep, got))
        firsts.append(first)
        first += count
    signals = pl.pallas_call(
        functools.partial(place_kernel, firsts, observers),
        in_specs=[SMEM] + [VMEM] * len(pieces),
        out_specs=VMEM,
        out_shape=jax.ShapeDtypeStruct((observers * members, pieces[0].shape[1]), F32),
        compiler_params=params(16),
    )(me, *pieces)
    return (field, signals)


def sizes(observers):
    last = -(-observers * LAST // 16 // 16) * 16
    return [observers - last, last]


def solution(mesh):
    placed = (
        P("box", "panel"),
        P("box", "panel"),
        P("box", "panel"),
        P(("box", "panel")),
        P("box", "panel"),
        P("box", "panel"),
    )
    return jax.shard_map(
        on_device,
        mesh=mesh,
        in_specs=placed,
        out_specs=(P("box", "panel"), P("panel", "box")),
        check_vma=False,
    )
```

```python
import functools

import jax
import jax.numpy as jnp
from jax import lax
from jax.experimental import pallas as pl
from jax.experimental.pallas import tpu as pltpu
from jax.sharding import PartitionSpec as P

F32 = jnp.float32
BF16 = jnp.bfloat16
STEPS = 4
NB = 2048
LOW = 32
LANES = 128
EDGE = 2 * STEPS
PAD = 16
STRIP = 32
AMP_SCALE = 4096.0
LAST = 6
VMEM = pl.BlockSpec(memory_space=pltpu.VMEM)
SMEM = pl.BlockSpec(memory_space=pltpu.SMEM)


def params(mib):
    return pltpu.CompilerParams(vmem_limit_bytes=mib << 20)


def cost(flops, size):
    return pl.CostEstimate(flops=flops, bytes_accessed=size, transcendentals=0)


def pack_kernel(cols, me_ref, cell_ref, amp_ref, bin_ref, place_ref, *refs):
    outs, turned = refs[:-1], refs[-1]
    cell = cell_ref[...]
    row = lax.div(cell, cols)
    col = cell - row * cols
    panel = lax.broadcasted_iota(jnp.int32, cell.shape, 1)
    place_ref[0:1] = col // LANES
    place_ref[1:2] = row // 8 * 8 + PAD
    place_ref[2:3] = row & 7
    place_ref[3:4] = (panel - col) & (LANES - 1)
    scaled = (amp_ref[...].astype(F32) * AMP_SCALE).astype(jnp.int32)
    turned[...] = jnp.transpose((scaled << 16) | bin_ref[...])
    width = outs[0].shape[0]
    for k, out in enumerate(outs):
        first = pl.multiple_of(lax.rem(me_ref[0] + k, len(outs)) * width, 8)
        out[...] = turned[pl.ds(first, width), :]


def pack(me, panel_cell, cols, amplitude, delay_bin, members):
    panels, observers = amplitude.shape
    cells = panel_cell.reshape(1, -1)
    width = observers // members
    block = pl.BlockSpec((LANES, observers), lambda i: (i, 0))
    out = jax.ShapeDtypeStruct((width, panels), jnp.int32)
    whole = pl.BlockSpec(cells.shape, lambda i: (0, 0))
    return pl.pallas_call(
        functools.partial(pack_kernel, cols),
        grid=(panels // LANES,),
        in_specs=[SMEM, whole, block, block],
        out_specs=[pl.BlockSpec((4, cells.shape[1]), lambda i: (0, 0))]
        + [pl.BlockSpec((width, LANES), lambda i: (0, i))] * members,
        out_shape=[jax.ShapeDtypeStruct((4, cells.shape[1]), jnp.int32)] + [out] * members,
        scratch_shapes=[pltpu.VMEM((observers, LANES), jnp.int32)],
        compiler_params=params(56),
        cost_estimate=cost(panels * observers, 10 * panels * observers),
    )(me, cells, amplitude, delay_bin)


def coded(mask, visc):
    return jnp.where(mask != 0, visc, 0.0)


def rows_kernel(f_top, m_top, v_top, f_end, m_end, v_end, first_ref, last_ref):
    first_ref[:STEPS] = f_top[:STEPS]
    first_ref[STEPS:] = coded(m_top[:STEPS], v_top[:STEPS])
    last_ref[:STEPS] = f_end[8 - STEPS :]
    last_ref[STEPS:] = coded(m_end[8 - STEPS :], v_end[8 - STEPS :])


def columns_kernel(
    field_ref, mask_ref, visc_ref, before_ref, after_ref, first_ref, last_ref, tall
):
    rows, cols = field_ref.shape
    tall[...] = jnp.zeros_like(tall)
    for part in range(2):
        halo = slice(part * STEPS, (part + 1) * STEPS)
        for start, low, out in ((0, 0, first_ref), (cols - LANES, LANES - STEPS, last_ref)):
            lanes = slice(start, start + LANES)
            if part:
                tall[:rows] = coded(mask_ref[:, lanes], visc_ref[:, lanes])
            else:
                tall[:rows] = field_ref[:, lanes]
            tall[rows : rows + STEPS] = after_ref[halo, lanes]
            tall[rows + STEPS : rows + EDGE] = before_ref[halo, lanes]
            out[halo] = jnp.transpose(tall[...])[low : low + STEPS]


def step_kernel(
    cell_ref,
    field_ref,
    mask_ref,
    visc_ref,
    before_ref,
    after_ref,
    south_ref,
    north_ref,
    end_ref,
    sample_ref,
    fields,
    visc,
    wide,
):
    rows, cols = field_ref.shape
    panels = sample_ref.shape[1]
    tiles, height, _ = visc.shape
    wide[...] = jnp.zeros_like(wide)
    for part, buf in enumerate((fields.at[0], visc)):
        halo = slice(part * STEPS, (part + 1) * STEPS)
        wide[:STEPS] = north_ref[halo]
        wide[LANES - STEPS :] = south_ref[halo]
        side = jnp.transpose(wide[...])
        for k in range(tiles):
            at = slice(k * LANES, (k + 1) * LANES)
            buf[k, :PAD] = jnp.zeros((PAD, LANES), F32)
            buf[k, PAD + rows :] = jnp.zeros((height - PAD - rows, LANES), F32)
            if k == tiles - 1:
                inside, before, after = (
                    side[:rows],
                    side[rows + STEPS : rows + EDGE],
                    side[rows : rows + STEPS],
                )
            else:
                inside = coded(mask_ref[:, at], visc_ref[:, at]) if part else field_ref[:, at]
                before, after = before_ref[halo, at], after_ref[halo, at]
            buf[k, PAD : PAD + rows] = inside
            buf[k, PAD - STEPS : PAD] = before
            buf[k, PAD + rows : PAD + rows + STEPS] = after

    first_lane = lax.broadcasted_iota(jnp.int32, (STRIP, LANES), 1) == 0
    last_lane = lax.broadcasted_iota(jnp.int32, (STRIP, LANES), 1) == LANES - 1
    for step in range(STEPS):
        old, new = fields.at[step], fields.at[step + 1]
        for k in range(tiles):
            new[k, :8] = jnp.zeros((8, LANES), F32)
            new[k, height - 8 :] = jnp.zeros((8, LANES), F32)

        def one_strip(i, carry):
            top = pl.multiple_of(i * STRIP, 8)
            centers = [old[k, pl.ds(top + 8, STRIP), :] for k in range(tiles)]
            right = [pltpu.roll(x, 1, 1) for x in centers]
            left = [pltpu.roll(x, LANES - 1, 1) for x in centers]
            for k in range(tiles):
                window = old[k, pl.ds(top, STRIP + 16), :]
                base = visc[k, pl.ds(top + 8, STRIP), :]
                center = centers[k]
                west = pltpu.roll(window, 1, 0)[8 : 8 + STRIP]
                east = pltpu.roll(window, STRIP + 15, 0)[8 : 8 + STRIP]
                south = jnp.where(first_lane, right[k - 1], right[k])
                north = jnp.where(last_lane, left[(k + 1) % tiles], left[k])
                diff_x = east - west
                diff_y = north - south
                square = diff_x * diff_x + diff_y * diff_y
                norm = square * lax.rsqrt(jnp.maximum(square, 1e-37))
                viscosity = base + 0.05 * norm / (2.0 + norm)
                around = (east + west) + (north + south)
                update = 0.75 * center + 0.15 * west + 0.1 * south
                update = update + viscosity * (around - 4.0 * center)
                new[k, pl.ds(top + 8, STRIP), :] = jnp.where(base > 0.0, update, 0.0)
            return carry

        strips = (height - 16) // STRIP
        lax.fori_loop(0, strips, one_strip, 0, unroll=strips)
    for k in range(tiles - 1):
        end_ref[:, k * LANES : (k + 1) * LANES] = fields[STEPS, k, PAD : PAD + rows, :]

    lane = lax.broadcasted_iota(jnp.int32, (8, LANES), 1)
    line = lax.broadcasted_iota(jnp.int32, (8, LANES), 0)
    for base in range(0, panels, LANES):

        def one_panel(k, found):
            tile, top, row, turn = [cell_ref[c, base + k] for c in range(4)]
            top = pl.multiple_of(top, 8)
            here = (lane == k) & (line == row)
            return tuple(
                jnp.where(
                    here, pltpu.roll(fields[t + 1, tile, pl.ds(top, 8), :], turn, 1), found[t]
                )
                for t in range(STEPS)
            )

        none = (jnp.zeros((8, LANES), F32),) * STEPS
        found = lax.fori_loop(0, LANES, one_panel, none, unroll=32)
        for t in range(STEPS):
            sample_ref[t : t + 1, base : base + LANES] = jnp.sum(found[t], axis=0, keepdims=True)


def edges(field, mask, visc):
    rows, cols = field.shape
    edge_rows = jax.ShapeDtypeStruct((EDGE, cols), F32)
    return pl.pallas_call(
        rows_kernel,
        grid=(1,),
        in_specs=[pl.BlockSpec((8, cols), lambda i: (0, 0))] * 3
        + [pl.BlockSpec((8, cols), lambda i: (rows // 8 - 1, 0))] * 3,
        out_specs=[pl.BlockSpec((EDGE, cols), lambda i: (0, 0))] * 2,
        out_shape=[edge_rows, edge_rows],
        compiler_params=params(56),
        cost_estimate=cost(16 * cols, 256 * cols),
    )(field, mask, visc, field, mask, visc)


def shifted(axis, first, last):
    peers = lax.axis_size(axis)
    up = [(i, i + 1) for i in range(peers - 1)]
    down = [(i + 1, i) for i in range(peers - 1)]
    return lax.ppermute(last, axis, up), lax.ppermute(first, axis, down)


def field_window(field, mask, visc, before, after, places):
    rows, cols = field.shape
    tall = -(-(rows + EDGE) // LANES) * LANES
    edge_cols = jax.ShapeDtypeStruct((EDGE, tall), F32)

    first, last = pl.pallas_call(
        columns_kernel,
        in_specs=[VMEM] * 5,
        out_specs=[VMEM] * 2,
        out_shape=[edge_cols, edge_cols],
        scratch_shapes=[pltpu.VMEM((tall, LANES), F32)],
        compiler_params=params(16),
        cost_estimate=cost(rows * cols, 4 * rows * cols),
    )(field, mask, visc, before, after)
    south, north = shifted("panel", first, last)
    panels = places.shape[1]
    tiles = cols // LANES + 1
    height = 16 + -(-(rows + 2 * PAD - 16) // STRIP) * STRIP
    return pl.pallas_call(
        step_kernel,
        in_specs=[SMEM] + [VMEM] * 7,
        out_specs=[VMEM] * 2,
        out_shape=[
            jax.ShapeDtypeStruct((rows, cols), F32),
            jax.ShapeDtypeStruct((STEPS, panels), F32),
        ],
        scratch_shapes=[
            pltpu.VMEM((STEPS + 1, tiles, height, LANES), F32),
            pltpu.VMEM((tiles, height, LANES), F32),
            pltpu.VMEM((LANES, tall), F32),
        ],
        compiler_params=params(24),
        cost_estimate=cost(100 * rows * cols, 800 * rows * cols),
    )(places, field, mask, visc, before, after, south, north)


def bin_kernel(half_ref, *refs):
    members = (len(refs) - 7) // 2
    words, samples = refs[:members], refs[members : 2 * members]
    keep_ref, send_ref, low_s, high_s, weight_s, acc_s, sig_s = refs[2 * members :]
    block, local = words[0].shape
    parts = local // LANES
    high = NB // LOW
    per_row = LANES // LOW
    half_rows = NB // LANES // 8
    low_tiles = LOW // 8 + 1
    depth = 2 * LANES
    shift = LOW.bit_length() - 1
    for s in range(members):
        for j in range(parts):
            word = words[s][:, j * LANES : (j + 1) * LANES]
            at = slice((s * parts + j) * LANES, (s * parts + j + 1) * LANES)
            low_s[:, at] = (word & (LOW - 1)).astype(F32)
            high_s[:, at] = ((word >> shift) & (high - 1)).astype(F32)
            amp = (word >> 16).astype(F32) * (1.0 / AMP_SCALE)
            for t in range(STEPS):
                weight_s[t, :, at] = amp * samples[s][j, t : t + 1, :]

    one = jnp.ones((), BF16)
    zero = jnp.zeros((), BF16)
    sub = lax.broadcasted_iota(jnp.int32, (16, depth), 0) & 7

    def number(x):
        return x.astype(F32).astype(BF16)

    high_ids = [
        number(per_row * (8 * (k % half_rows) + sub) + k // half_rows) for k in range(high // 8)
    ]
    low_ids = [[number(8 * k + sub - t) for t in range(STEPS)] for k in range(low_tiles)]
    lane = lax.broadcasted_iota(jnp.int32, (8, LANES), 1)
    lanes = lax.broadcasted_iota(jnp.int32, (NB // LANES, LANES), 1)
    acc_s[...] = jnp.zeros_like(acc_s)

    def two_observers(o, u):
        def spread(ref, *lead):
            rows = [
                jnp.broadcast_to(ref[(*lead, slice(o + e, o + e + 1), at)], (8, depth))
                for e in range(2)
            ]
            return jnp.concatenate(rows).astype(BF16)

        acc = None
        for c in range(members * local // depth):
            at = slice(c * depth, (c + 1) * depth)
            low_row, high_row = spread(low_s), spread(high_s)
            weights = [spread(weight_s, t) for t in range(STEPS)]
            left = jnp.concatenate([jnp.where(ids == high_row, one, zero) for ids in high_ids])
            right = []
            for k in range(low_tiles):
                placed = zero
                for t in range(1 if k * 8 >= LOW else 0, STEPS):
                    placed = jnp.where(low_ids[k][t] == low_row, weights[t], placed)
                right.append(placed)
            term = lax.dot_general(
                left, jnp.concatenate(right), (((1,), (1,)), ((), ())), preferred_element_type=F32
            )
            acc = term if acc is None else acc + term
        acc_s[u, :, : 16 * low_tiles] = acc
        for e in range(2):
            total = None
            for j in range(per_row):
                low = (lane - LOW * j) & (LANES - 1)
                source = jnp.where(low < 8 * low_tiles, 16 * (low // 8) + 8 * e + (low & 7), LANES - 1)
                tops = [16 * (j * half_rows + g) + 8 * e for g in range(half_rows)]
                x = jnp.concatenate(
                    [jnp.take_along_axis(acc_s[u, top : top + 8], source, axis=1) for top in tops]
                )
                if j == per_row - 1:
                    x = jnp.where(lanes < LOW, pltpu.roll(x, 1, 0), x)
                total = x if total is None else total + x
            sig_s[:, o + e : o + e + 1, :] = total[:, None, :]

    for u in range(block // 2):
        two_observers(2 * u, u)
    tiles = NB // LANES // 2
    per_owner = tiles // keep_ref.shape[0]
    for r in range(tiles):
        lanes = slice(r % per_owner * LANES, (r % per_owner + 1) * LANES)
        keep_ref[r // per_owner, :, lanes] = sig_s[half_ref[0] * tiles + r]
        sent = sig_s[(1 - half_ref[0]) * tiles + r]
        send_ref[r // per_owner, :, lanes] = sent.astype(BF16)


def binned(half, words, samples, first, count):
    members = len(words)
    local = words[0].shape[1]
    block = 16
    panels = members * local
    bins = NB // 2 // members
    out = pl.BlockSpec((members, block, bins), lambda i: (0, i, 0))
    return pl.pallas_call(
        bin_kernel,
        grid=(count // block,),
        in_specs=[SMEM]
        + [pl.BlockSpec((block, local), lambda i: (first // block + i, 0))] * members
        + [pl.BlockSpec(samples[0].shape, lambda i: (0, 0, 0))] * members,
        out_specs=[out, out],
        out_shape=[
            jax.ShapeDtypeStruct((members, count, bins), F32),
            jax.ShapeDtypeStruct((members, count, bins), BF16),
        ],
        scratch_shapes=[
            pltpu.VMEM((block, panels), F32),
            pltpu.VMEM((block, panels), F32),
            pltpu.VMEM((STEPS, block, panels), F32),
            pltpu.VMEM((block // 2, 2 * NB // LOW, LANES), F32),
            pltpu.VMEM((NB // LANES, block, LANES), F32),
        ],
        compiler_params=params(40),
        cost_estimate=cost(65536 * count * panels, 8 * count * panels),
    )(half, *words, *samples)


def join_kernel(me_ref, keep_ref, got_ref, *outs):
    for k, out in enumerate(outs):
        owner = lax.rem(me_ref[0] + k, len(outs))
        out[...] = (keep_ref[owner] + got_ref[owner].astype(F32)).astype(BF16)


def join(me, keep, got):
    members, count, bins = keep.shape
    return pl.pallas_call(
        join_kernel,
        in_specs=[SMEM, VMEM, VMEM],
        out_specs=[VMEM] * members,
        out_shape=[jax.ShapeDtypeStruct((count, bins), BF16)] * members,
        compiler_params=params(16),
        cost_estimate=cost(keep.size, 8 * keep.size),
    )(me, keep, got)


def place_kernel(first, width, me_ref, *refs):
    members, count, _ = refs[-2].shape
    pieces, (out_ref, wide, sems) = refs[:members], refs[-3:]
    copies = []
    for k, ref in enumerate(pieces):
        owner = lax.rem(me_ref[0] - k + members, members)
        start = pl.multiple_of(owner * width + first, 16)
        wide[k] = ref[...].astype(F32)
        copies.append(
            pltpu.make_async_copy(wide.at[k], out_ref.at[pl.ds(start, count), :], sems.at[k])
        )
        copies[-1].start()
    for copy in copies:
        copy.wait()


def place(me, pieces, signals, first, width):
    members = len(pieces)
    count, bins = pieces[0].shape
    before = [] if signals is None else [signals]
    return pl.pallas_call(
        functools.partial(place_kernel, first, width),
        in_specs=[SMEM] + [VMEM] * members + [pl.BlockSpec(memory_space=pl.ANY)] * len(before),
        out_specs=pl.BlockSpec(memory_space=pl.ANY),
        out_shape=jax.ShapeDtypeStruct((width * members, bins), F32),
        input_output_aliases={members + 1: 0} if before else {},
        scratch_shapes=[
            pltpu.VMEM((members, count, bins), F32),
            pltpu.SemaphoreType.DMA((members,)),
        ],
        compiler_params=params(16),
        cost_estimate=cost(members * count * bins, 6 * members * count * bins),
    )(me, *pieces, *before)


def on_device(field_start, fluid_mask, base_visc, panel_cell, amplitude, delay_bin):
    peers = lax.axis_size("box")
    members = peers // 2
    index = lax.axis_index("box").astype(jnp.int32).reshape(1)
    me, half = lax.rem(index, members), index // members

    def spread(parts):
        def perm(k):
            return [(i, i // members * members + (i + k) % members) for i in range(peers)]

        return [lax.ppermute(x, "box", perm(k)) if k else x for k, x in enumerate(parts)]

    ends = edges(field_start, fluid_mask, base_visc)
    amplitude, delay_bin, *ends = lax.optimization_barrier((amplitude, delay_bin, *ends))
    before, after = shifted("box", *ends)
    places, *packed = pack(
        me, panel_cell, field_start.shape[1], amplitude, delay_bin, members
    )
    before, after, *packed = lax.optimization_barrier((before, after, *packed))
    words = spread(packed)
    field, sample = field_window(
        field_start, fluid_mask, base_visc, before, after, places
    )
    samples = spread([lax.all_gather(sample, "panel")] * members)
    observers = words[0].shape[0]
    across = [(i, (i + members) % peers) for i in range(peers)]
    first, joined, signals = 0, None, None
    waiting = []
    for count in sizes(observers):
        keep, send = binned(half, words, samples, first, count)
        got = lax.ppermute(send, "box", across)
        if joined:
            pieces = spread(joined)
            got, pieces[members // 2] = lax.optimization_barrier((got, pieces[members // 2]))
            waiting.append(pieces)
        joined = join(me, keep, got)
        first += count
    waiting.append(spread(joined))
    first = 0
    for pieces in waiting:
        signals = place(me, pieces, signals, first, observers)
        first += pieces[0].shape[0]
    return (field, signals)


def sizes(observers):
    last = -(-observers * LAST // 16 // 16) * 16
    return [observers - last, last]


def solution(mesh):
    placed = (
        P("box", "panel"),
        P("box", "panel"),
        P("box", "panel"),
        P(("box", "panel")),
        P("box", "panel"),
        P("box", "panel"),
    )
    return jax.shard_map(
        on_device,
        mesh=mesh,
        in_specs=placed,
        out_specs=(P("box", "panel"), P("panel", "box")),
        check_vma=False,
    )
```

```python
import functools

import jax
import jax.numpy as jnp
from jax import lax
from jax.experimental import pallas as pl
from jax.experimental.pallas import tpu as pltpu
from jax.sharding import PartitionSpec as P

F32 = jnp.float32
BF16 = jnp.bfloat16
STEPS = 4
NB = 2048
LOW = 32
LANES = 128
EDGE = 2 * STEPS
PAD = 16
STRIP = 32
AMP_SCALE = 4096.0
LAST = 6
VMEM = pl.BlockSpec(memory_space=pltpu.VMEM)
SMEM = pl.BlockSpec(memory_space=pltpu.SMEM)


def params(mib):
    return pltpu.CompilerParams(vmem_limit_bytes=mib << 20)


def cost(flops, size):
    return pl.CostEstimate(flops=flops, bytes_accessed=size, transcendentals=0)


def pack_kernel(me_ref, amp_ref, bin_ref, *refs):
    outs, turned = refs[:-1], refs[-1]
    scaled = (amp_ref[...].astype(F32) * AMP_SCALE).astype(jnp.int32)
    turned[...] = jnp.transpose((scaled << 16) | bin_ref[...])
    width = outs[0].shape[0]
    for k, out in enumerate(outs):
        first = pl.multiple_of(lax.rem(me_ref[0] + k, len(outs)) * width, 8)
        out[...] = turned[pl.ds(first, width), :]


def pack(me, amplitude, delay_bin, members):
    panels, observers = amplitude.shape
    width = observers // members
    block = pl.BlockSpec((LANES, observers), lambda i: (i, 0))
    out = jax.ShapeDtypeStruct((width, panels), jnp.int32)
    return pl.pallas_call(
        pack_kernel,
        grid=(panels // LANES,),
        in_specs=[SMEM, block, block],
        out_specs=[pl.BlockSpec((width, LANES), lambda i: (0, i))] * members,
        out_shape=[out] * members,
        scratch_shapes=[pltpu.VMEM((observers, LANES), jnp.int32)],
        compiler_params=params(56),
        cost_estimate=cost(panels * observers, 10 * panels * observers),
    )(me, amplitude, delay_bin)


def coded(mask, visc):
    return jnp.where(mask != 0, visc, 0.0)


def rows_kernel(f_top, m_top, v_top, f_end, m_end, v_end, first_ref, last_ref):
    first_ref[:STEPS] = f_top[:STEPS]
    first_ref[STEPS:] = coded(m_top[:STEPS], v_top[:STEPS])
    last_ref[:STEPS] = f_end[8 - STEPS :]
    last_ref[STEPS:] = coded(m_end[8 - STEPS :], v_end[8 - STEPS :])


def columns_kernel(
    cell_ref, field_ref, mask_ref, visc_ref, before_ref, after_ref, first_ref, last_ref, place_ref, tall
):
    rows, cols = field_ref.shape
    cell = cell_ref[...]
    row = lax.div(cell, cols)
    col = cell - row * cols
    panel = lax.broadcasted_iota(jnp.int32, cell.shape, 1)
    place_ref[0:1] = col // LANES
    place_ref[1:2] = row // 8 * 8 + PAD
    place_ref[2:3] = row & 7
    place_ref[3:4] = (panel - col) & (LANES - 1)
    tall[...] = jnp.zeros_like(tall)
    for part in range(2):
        halo = slice(part * STEPS, (part + 1) * STEPS)
        for start, low, out in ((0, 0, first_ref), (cols - LANES, LANES - STEPS, last_ref)):
            lanes = slice(start, start + LANES)
            if part:
                tall[:rows] = coded(mask_ref[:, lanes], visc_ref[:, lanes])
            else:
                tall[:rows] = field_ref[:, lanes]
            tall[rows : rows + STEPS] = after_ref[halo, lanes]
            tall[rows + STEPS : rows + EDGE] = before_ref[halo, lanes]
            out[halo] = jnp.transpose(tall[...])[low : low + STEPS]


def step_kernel(
    cell_ref,
    field_ref,
    mask_ref,
    visc_ref,
    before_ref,
    after_ref,
    south_ref,
    north_ref,
    end_ref,
    sample_ref,
    fields,
    visc,
    wide,
):
    rows, cols = field_ref.shape
    panels = sample_ref.shape[1]
    tiles, height, _ = visc.shape
    wide[...] = jnp.zeros_like(wide)
    for part, buf in enumerate((fields.at[0], visc)):
        halo = slice(part * STEPS, (part + 1) * STEPS)
        wide[:STEPS] = north_ref[halo]
        wide[LANES - STEPS :] = south_ref[halo]
        side = jnp.transpose(wide[...])
        for k in range(tiles):
            at = slice(k * LANES, (k + 1) * LANES)
            buf[k, :PAD] = jnp.zeros((PAD, LANES), F32)
            buf[k, PAD + rows :] = jnp.zeros((height - PAD - rows, LANES), F32)
            if k == tiles - 1:
                inside, before, after = (
                    side[:rows],
                    side[rows + STEPS : rows + EDGE],
                    side[rows : rows + STEPS],
                )
            else:
                inside = coded(mask_ref[:, at], visc_ref[:, at]) if part else field_ref[:, at]
                before, after = before_ref[halo, at], after_ref[halo, at]
            buf[k, PAD : PAD + rows] = inside
            buf[k, PAD - STEPS : PAD] = before
            buf[k, PAD + rows : PAD + rows + STEPS] = after

    first_lane = lax.broadcasted_iota(jnp.int32, (STRIP, LANES), 1) == 0
    last_lane = lax.broadcasted_iota(jnp.int32, (STRIP, LANES), 1) == LANES - 1
    for step in range(STEPS):
        old, new = fields.at[step], fields.at[step + 1]
        for k in range(tiles):
            new[k, :8] = jnp.zeros((8, LANES), F32)
            new[k, height - 8 :] = jnp.zeros((8, LANES), F32)

        def one_strip(i, carry):
            top = pl.multiple_of(i * STRIP, 8)
            centers = [old[k, pl.ds(top + 8, STRIP), :] for k in range(tiles)]
            right = [pltpu.roll(x, 1, 1) for x in centers]
            left = [pltpu.roll(x, LANES - 1, 1) for x in centers]
            for k in range(tiles):
                window = old[k, pl.ds(top, STRIP + 16), :]
                base = visc[k, pl.ds(top + 8, STRIP), :]
                center = centers[k]
                west = pltpu.roll(window, 1, 0)[8 : 8 + STRIP]
                east = pltpu.roll(window, STRIP + 15, 0)[8 : 8 + STRIP]
                south = jnp.where(first_lane, right[k - 1], right[k])
                north = jnp.where(last_lane, left[(k + 1) % tiles], left[k])
                diff_x = east - west
                diff_y = north - south
                square = diff_x * diff_x + diff_y * diff_y
                norm = square * lax.rsqrt(jnp.maximum(square, 1e-37))
                viscosity = base + 0.05 * norm / (2.0 + norm)
                around = (east + west) + (north + south)
                update = 0.75 * center + 0.15 * west + 0.1 * south
                update = update + viscosity * (around - 4.0 * center)
                new[k, pl.ds(top + 8, STRIP), :] = jnp.where(base > 0.0, update, 0.0)
            return carry

        strips = (height - 16) // STRIP
        lax.fori_loop(0, strips, one_strip, 0, unroll=strips)
    for k in range(tiles - 1):
        end_ref[:, k * LANES : (k + 1) * LANES] = fields[STEPS, k, PAD : PAD + rows, :]

    lane = lax.broadcasted_iota(jnp.int32, (8, LANES), 1)
    line = lax.broadcasted_iota(jnp.int32, (8, LANES), 0)
    for base in range(0, panels, LANES):

        def one_panel(k, found):
            tile, top, row, turn = [cell_ref[c, base + k] for c in range(4)]
            top = pl.multiple_of(top, 8)
            here = (lane == k) & (line == row)
            return tuple(
                jnp.where(
                    here, pltpu.roll(fields[t + 1, tile, pl.ds(top, 8), :], turn, 1), found[t]
                )
                for t in range(STEPS)
            )

        none = (jnp.zeros((8, LANES), F32),) * STEPS
        found = lax.fori_loop(0, LANES, one_panel, none, unroll=32)
        for t in range(STEPS):
            sample_ref[t : t + 1, base : base + LANES] = jnp.sum(found[t], axis=0, keepdims=True)


def edges(field, mask, visc):
    rows, cols = field.shape
    edge_rows = jax.ShapeDtypeStruct((EDGE, cols), F32)
    return pl.pallas_call(
        rows_kernel,
        grid=(1,),
        in_specs=[pl.BlockSpec((8, cols), lambda i: (0, 0))] * 3
        + [pl.BlockSpec((8, cols), lambda i: (rows // 8 - 1, 0))] * 3,
        out_specs=[pl.BlockSpec((EDGE, cols), lambda i: (0, 0))] * 2,
        out_shape=[edge_rows, edge_rows],
        compiler_params=params(56),
        cost_estimate=cost(16 * cols, 256 * cols),
    )(field, mask, visc, field, mask, visc)


def shifted(axis, first, last):
    peers = lax.axis_size(axis)
    up = [(i, i + 1) for i in range(peers - 1)]
    down = [(i + 1, i) for i in range(peers - 1)]
    return lax.ppermute(last, axis, up), lax.ppermute(first, axis, down)


def field_window(field, mask, visc, before, after, panel_cell):
    rows, cols = field.shape
    tall = -(-(rows + EDGE) // LANES) * LANES
    edge_cols = jax.ShapeDtypeStruct((EDGE, tall), F32)

    panels = panel_cell.shape[0]
    first, last, places = pl.pallas_call(
        columns_kernel,
        in_specs=[VMEM] * 6,
        out_specs=[VMEM] * 3,
        out_shape=[edge_cols, edge_cols, jax.ShapeDtypeStruct((4, panels), jnp.int32)],
        scratch_shapes=[pltpu.VMEM((tall, LANES), F32)],
        compiler_params=params(16),
        cost_estimate=cost(rows * cols, 4 * rows * cols),
    )(panel_cell.reshape(1, panels), field, mask, visc, before, after)
    south, north = shifted("panel", first, last)
    tiles = cols // LANES + 1
    height = 16 + -(-(rows + 2 * PAD - 16) // STRIP) * STRIP
    return pl.pallas_call(
        step_kernel,
        in_specs=[SMEM] + [VMEM] * 7,
        out_specs=[VMEM] * 2,
        out_shape=[
            jax.ShapeDtypeStruct((rows, cols), F32),
            jax.ShapeDtypeStruct((STEPS, panels), F32),
        ],
        scratch_shapes=[
            pltpu.VMEM((STEPS + 1, tiles, height, LANES), F32),
            pltpu.VMEM((tiles, height, LANES), F32),
            pltpu.VMEM((LANES, tall), F32),
        ],
        compiler_params=params(24),
        cost_estimate=cost(100 * rows * cols, 800 * rows * cols),
    )(places, field, mask, visc, before, after, south, north)


def bin_kernel(half_ref, *refs):
    members = (len(refs) - 7) // 2
    words, samples = refs[:members], refs[members : 2 * members]
    keep_ref, send_ref, low_s, high_s, weight_s, acc_s, sig_s = refs[2 * members :]
    block, local = words[0].shape
    parts = local // LANES
    high = NB // LOW
    per_row = LANES // LOW
    half_rows = NB // LANES // 8
    low_tiles = LOW // 8 + 1
    depth = 2 * LANES
    shift = LOW.bit_length() - 1
    for s in range(members):
        for j in range(parts):
            word = words[s][:, j * LANES : (j + 1) * LANES]
            at = slice((s * parts + j) * LANES, (s * parts + j + 1) * LANES)
            low_s[:, at] = (word & (LOW - 1)).astype(F32)
            high_s[:, at] = ((word >> shift) & (high - 1)).astype(F32)
            amp = (word >> 16).astype(F32) * (1.0 / AMP_SCALE)
            for t in range(STEPS):
                weight_s[t, :, at] = amp * samples[s][j, t : t + 1, :]

    one = jnp.ones((), BF16)
    zero = jnp.zeros((), BF16)
    sub = lax.broadcasted_iota(jnp.int32, (16, depth), 0) & 7

    def number(x):
        return x.astype(F32).astype(BF16)

    high_ids = [
        number(per_row * (8 * (k % half_rows) + sub) + k // half_rows) for k in range(high // 8)
    ]
    low_ids = [[number(8 * k + sub - t) for t in range(STEPS)] for k in range(low_tiles)]
    lane = lax.broadcasted_iota(jnp.int32, (8, LANES), 1)
    lanes = lax.broadcasted_iota(jnp.int32, (NB // LANES, LANES), 1)
    acc_s[...] = jnp.zeros_like(acc_s)

    def two_observers(o, u):
        def spread(ref, *lead):
            rows = [
                jnp.broadcast_to(ref[(*lead, slice(o + e, o + e + 1), at)], (8, depth))
                for e in range(2)
            ]
            return jnp.concatenate(rows).astype(BF16)

        acc = None
        for c in range(members * local // depth):
            at = slice(c * depth, (c + 1) * depth)
            low_row, high_row = spread(low_s), spread(high_s)
            weights = [spread(weight_s, t) for t in range(STEPS)]
            left = jnp.concatenate([jnp.where(ids == high_row, one, zero) for ids in high_ids])
            right = []
            for k in range(low_tiles):
                placed = zero
                for t in range(1 if k * 8 >= LOW else 0, STEPS):
                    placed = jnp.where(low_ids[k][t] == low_row, weights[t], placed)
                right.append(placed)
            term = lax.dot_general(
                left, jnp.concatenate(right), (((1,), (1,)), ((), ())), preferred_element_type=F32
            )
            acc = term if acc is None else acc + term
        acc_s[u, :, : 16 * low_tiles] = acc
        for e in range(2):
            total = None
            for j in range(per_row):
                low = (lane - LOW * j) & (LANES - 1)
                source = jnp.where(low < 8 * low_tiles, 16 * (low // 8) + 8 * e + (low & 7), LANES - 1)
                tops = [16 * (j * half_rows + g) + 8 * e for g in range(half_rows)]
                x = jnp.concatenate(
                    [jnp.take_along_axis(acc_s[u, top : top + 8], source, axis=1) for top in tops]
                )
                if j == per_row - 1:
                    x = jnp.where(lanes < LOW, pltpu.roll(x, 1, 0), x)
                total = x if total is None else total + x
            sig_s[:, o + e : o + e + 1, :] = total[:, None, :]

    for u in range(block // 2):
        two_observers(2 * u, u)
    tiles = NB // LANES // 2
    per_owner = tiles // keep_ref.shape[0]
    for r in range(tiles):
        lanes = slice(r % per_owner * LANES, (r % per_owner + 1) * LANES)
        keep_ref[r // per_owner, :, lanes] = sig_s[half_ref[0] * tiles + r]
        sent = sig_s[(1 - half_ref[0]) * tiles + r]
        send_ref[r // per_owner, :, lanes] = sent.astype(BF16)


def binned(half, words, samples, first, count):
    members = len(words)
    local = words[0].shape[1]
    block = 16
    panels = members * local
    bins = NB // 2 // members
    out = pl.BlockSpec((members, block, bins), lambda i: (0, i, 0))
    return pl.pallas_call(
        bin_kernel,
        grid=(count // block,),
        in_specs=[SMEM]
        + [pl.BlockSpec((block, local), lambda i: (first // block + i, 0))] * members
        + [pl.BlockSpec(samples[0].shape, lambda i: (0, 0, 0))] * members,
        out_specs=[out, out],
        out_shape=[
            jax.ShapeDtypeStruct((members, count, bins), F32),
            jax.ShapeDtypeStruct((members, count, bins), BF16),
        ],
        scratch_shapes=[
            pltpu.VMEM((block, panels), F32),
            pltpu.VMEM((block, panels), F32),
            pltpu.VMEM((STEPS, block, panels), F32),
            pltpu.VMEM((block // 2, 2 * NB // LOW, LANES), F32),
            pltpu.VMEM((NB // LANES, block, LANES), F32),
        ],
        compiler_params=params(40),
        cost_estimate=cost(65536 * count * panels, 8 * count * panels),
    )(half, *words, *samples)


def join_kernel(me_ref, keep_ref, got_ref, *outs):
    for k, out in enumerate(outs):
        owner = lax.rem(me_ref[0] + k, len(outs))
        out[...] = (keep_ref[owner] + got_ref[owner].astype(F32)).astype(BF16)


def join(me, keep, got):
    members, count, bins = keep.shape
    return pl.pallas_call(
        join_kernel,
        in_specs=[SMEM, VMEM, VMEM],
        out_specs=[VMEM] * members,
        out_shape=[jax.ShapeDtypeStruct((count, bins), BF16)] * members,
        compiler_params=params(16),
        cost_estimate=cost(keep.size, 8 * keep.size),
    )(me, keep, got)


def place_kernel(first, width, me_ref, *refs):
    members, count, _ = refs[-2].shape
    pieces, (out_ref, wide, sems) = refs[:members], refs[-3:]
    copies = []
    for k, ref in enumerate(pieces):
        owner = lax.rem(me_ref[0] - k + members, members)
        start = pl.multiple_of(owner * width + first, 16)
        wide[k] = ref[...].astype(F32)
        copies.append(
            pltpu.make_async_copy(wide.at[k], out_ref.at[pl.ds(start, count), :], sems.at[k])
        )
        copies[-1].start()
    for copy in copies:
        copy.wait()


def place(me, pieces, signals, first, width):
    members = len(pieces)
    count, bins = pieces[0].shape
    before = [] if signals is None else [signals]
    return pl.pallas_call(
        functools.partial(place_kernel, first, width),
        in_specs=[SMEM] + [VMEM] * members + [pl.BlockSpec(memory_space=pl.ANY)] * len(before),
        out_specs=pl.BlockSpec(memory_space=pl.ANY),
        out_shape=jax.ShapeDtypeStruct((width * members, bins), F32),
        input_output_aliases={members + 1: 0} if before else {},
        scratch_shapes=[
            pltpu.VMEM((members, count, bins), F32),
            pltpu.SemaphoreType.DMA((members,)),
        ],
        compiler_params=params(16),
        cost_estimate=cost(members * count * bins, 6 * members * count * bins),
    )(me, *pieces, *before)


def on_device(field_start, fluid_mask, base_visc, panel_cell, amplitude, delay_bin):
    peers = lax.axis_size("box")
    members = peers // 2
    index = lax.axis_index("box").astype(jnp.int32).reshape(1)
    me, half = lax.rem(index, members), index // members

    def spread(parts):
        def perm(k):
            return [(i, i // members * members + (i + k) % members) for i in range(peers)]

        return [lax.ppermute(x, "box", perm(k)) if k else x for k, x in enumerate(parts)]

    ends = edges(field_start, fluid_mask, base_visc)
    amplitude, delay_bin, *ends = lax.optimization_barrier((amplitude, delay_bin, *ends))
    before, after = shifted("box", *ends)
    packed = pack(me, amplitude, delay_bin, members)
    before, after, *packed = lax.optimization_barrier((before, after, *packed))
    words = spread(packed)
    field, sample = field_window(
        field_start, fluid_mask, base_visc, before, after, panel_cell
    )
    sample = lax.all_gather(sample, "panel")
    middle = members // 2
    sample, words[middle] = lax.optimization_barrier((sample, words[middle]))
    samples = spread([sample] * members)
    observers = words[0].shape[0]
    across = [(i, (i + members) % peers) for i in range(peers)]
    first, joined, signals = 0, None, None
    waiting = []
    for count in sizes(observers):
        keep, send = binned(half, words, samples, first, count)
        got = lax.ppermute(send, "box", across)
        if joined:
            pieces = spread(joined)
            got, pieces[middle] = lax.optimization_barrier((got, pieces[middle]))
            waiting.append(pieces)
        joined = join(me, keep, got)
        first += count
    waiting.append(spread(joined))
    first = 0
    for pieces in waiting:
        signals = place(me, pieces, signals, first, observers)
        first += pieces[0].shape[0]
    return (field, signals)


def sizes(observers):
    last = -(-observers * LAST // 16 // 16) * 16
    return [observers - last, last]


def solution(mesh):
    placed = (
        P("box", "panel"),
        P("box", "panel"),
        P("box", "panel"),
        P(("box", "panel")),
        P("box", "panel"),
        P("box", "panel"),
    )
    return jax.shard_map(
        on_device,
        mesh=mesh,
        in_specs=placed,
        out_specs=(P("box", "panel"), P("panel", "box")),
        check_vma=False,
    )
```

```python
import functools

import jax
import jax.numpy as jnp
from jax import lax
from jax.experimental import pallas as pl
from jax.experimental.pallas import tpu as pltpu
from jax.sharding import PartitionSpec as P

F32 = jnp.float32
BF16 = jnp.bfloat16
STEPS = 4
NB = 2048
LOW = 32
LANES = 128
EDGE = 2 * STEPS
PAD = 16
STRIP = 32
AMP_SCALE = 4096.0
PARTS = (7, 12, 16)
VMEM = pl.BlockSpec(memory_space=pltpu.VMEM)
SMEM = pl.BlockSpec(memory_space=pltpu.SMEM)


def params(mib):
    return pltpu.CompilerParams(vmem_limit_bytes=mib << 20)


def cost(flops, size):
    return pl.CostEstimate(flops=flops, bytes_accessed=size, transcendentals=0)


def pack_kernel(me_ref, amp_ref, bin_ref, *refs):
    outs, turned = refs[:-1], refs[-1]
    scaled = (amp_ref[...].astype(F32) * AMP_SCALE).astype(jnp.int32)
    turned[...] = jnp.transpose((scaled << 16) | bin_ref[...])
    width = outs[0].shape[0]
    for k, out in enumerate(outs):
        first = pl.multiple_of(lax.rem(me_ref[0] + k, len(outs)) * width, 8)
        out[...] = turned[pl.ds(first, width), :]


def pack(me, amplitude, delay_bin, members):
    panels, observers = amplitude.shape
    width = observers // members
    block = pl.BlockSpec((LANES, observers), lambda i: (i, 0))
    out = jax.ShapeDtypeStruct((width, panels), jnp.int32)
    return pl.pallas_call(
        pack_kernel,
        grid=(panels // LANES,),
        in_specs=[SMEM, block, block],
        out_specs=[pl.BlockSpec((width, LANES), lambda i: (0, i))] * members,
        out_shape=[out] * members,
        scratch_shapes=[pltpu.VMEM((observers, LANES), jnp.int32)],
        compiler_params=params(56),
        cost_estimate=cost(panels * observers, 10 * panels * observers),
    )(me, amplitude, delay_bin)


def coded(mask, visc):
    return jnp.where(mask != 0, visc, 0.0)


def rows_kernel(f_top, m_top, v_top, f_end, m_end, v_end, first_ref, last_ref):
    first_ref[:STEPS] = f_top[:STEPS]
    first_ref[STEPS:] = coded(m_top[:STEPS], v_top[:STEPS])
    last_ref[:STEPS] = f_end[8 - STEPS :]
    last_ref[STEPS:] = coded(m_end[8 - STEPS :], v_end[8 - STEPS :])


def columns_kernel(
    cell_ref, field_ref, mask_ref, visc_ref, before_ref, after_ref, first_ref, last_ref, place_ref, tall
):
    rows, cols = field_ref.shape
    cell = cell_ref[...]
    row = lax.div(cell, cols)
    col = cell - row * cols
    panel = lax.broadcasted_iota(jnp.int32, cell.shape, 1)
    place_ref[0:1] = col // LANES
    place_ref[1:2] = row // 8 * 8 + PAD
    place_ref[2:3] = row & 7
    place_ref[3:4] = (panel - col) & (LANES - 1)
    tall[...] = jnp.zeros_like(tall)
    for part in range(2):
        halo = slice(part * STEPS, (part + 1) * STEPS)
        for start, low, out in ((0, 0, first_ref), (cols - LANES, LANES - STEPS, last_ref)):
            lanes = slice(start, start + LANES)
            if part:
                tall[:rows] = coded(mask_ref[:, lanes], visc_ref[:, lanes])
            else:
                tall[:rows] = field_ref[:, lanes]
            tall[rows : rows + STEPS] = after_ref[halo, lanes]
            tall[rows + STEPS : rows + EDGE] = before_ref[halo, lanes]
            out[halo] = jnp.transpose(tall[...])[low : low + STEPS]


def step_kernel(
    cell_ref,
    field_ref,
    mask_ref,
    visc_ref,
    before_ref,
    after_ref,
    south_ref,
    north_ref,
    end_ref,
    sample_ref,
    fields,
    visc,
    wide,
    last,
    sem,
):
    rows, cols = field_ref.shape
    panels = sample_ref.shape[1]
    tiles, height, _ = visc.shape
    wide[...] = jnp.zeros_like(wide)
    for part, buf in enumerate((fields.at[0], visc)):
        halo = slice(part * STEPS, (part + 1) * STEPS)
        wide[:STEPS] = north_ref[halo]
        wide[LANES - STEPS :] = south_ref[halo]
        side = jnp.transpose(wide[...])
        for k in range(tiles):
            at = slice(k * LANES, (k + 1) * LANES)
            buf[k, :PAD] = jnp.zeros((PAD, LANES), F32)
            buf[k, PAD + rows :] = jnp.zeros((height - PAD - rows, LANES), F32)
            if k == tiles - 1:
                inside, before, after = (
                    side[:rows],
                    side[rows + STEPS : rows + EDGE],
                    side[rows : rows + STEPS],
                )
            else:
                inside = coded(mask_ref[:, at], visc_ref[:, at]) if part else field_ref[:, at]
                before, after = before_ref[halo, at], after_ref[halo, at]
            buf[k, PAD : PAD + rows] = inside
            buf[k, PAD - STEPS : PAD] = before
            buf[k, PAD + rows : PAD + rows + STEPS] = after

    first_lane = lax.broadcasted_iota(jnp.int32, (STRIP, LANES), 1) == 0
    last_lane = lax.broadcasted_iota(jnp.int32, (STRIP, LANES), 1) == LANES - 1
    for step in range(STEPS):
        old, new = fields.at[step], fields.at[step + 1]
        for k in range(tiles):
            new[k, :8] = jnp.zeros((8, LANES), F32)
            new[k, height - 8 :] = jnp.zeros((8, LANES), F32)

        def one_strip(i, carry):
            top = pl.multiple_of(i * STRIP, 8)
            centers = [old[k, pl.ds(top + 8, STRIP), :] for k in range(tiles)]
            right = [pltpu.roll(x, 1, 1) for x in centers]
            left = [pltpu.roll(x, LANES - 1, 1) for x in centers]
            for k in range(tiles):
                window = old[k, pl.ds(top, STRIP + 16), :]
                base = visc[k, pl.ds(top + 8, STRIP), :]
                center = centers[k]
                west = pltpu.roll(window, 1, 0)[8 : 8 + STRIP]
                east = pltpu.roll(window, STRIP + 15, 0)[8 : 8 + STRIP]
                south = jnp.where(first_lane, right[k - 1], right[k])
                north = jnp.where(last_lane, left[(k + 1) % tiles], left[k])
                diff_x = east - west
                diff_y = north - south
                square = diff_x * diff_x + diff_y * diff_y
                norm = square * lax.rsqrt(jnp.maximum(square, 1e-37))
                viscosity = base + 0.05 * norm / (2.0 + norm)
                around = (east + west) + (north + south)
                update = 0.75 * center + 0.15 * west + 0.1 * south
                update = update + viscosity * (around - 4.0 * center)
                new[k, pl.ds(top + 8, STRIP), :] = jnp.where(base > 0.0, update, 0.0)
            return carry

        strips = (height - 16) // STRIP
        lax.fori_loop(0, strips, one_strip, 0, unroll=strips)
    for k in range(tiles - 1):
        last[:, k * LANES : (k + 1) * LANES] = fields[STEPS, k, PAD : PAD + rows, :]
    leave = pltpu.make_async_copy(last, end_ref, sem)
    leave.start()

    lane = lax.broadcasted_iota(jnp.int32, (8, LANES), 1)
    line = lax.broadcasted_iota(jnp.int32, (8, LANES), 0)
    for base in range(0, panels, LANES):

        def one_panel(k, found):
            tile, top, row, turn = [cell_ref[c, base + k] for c in range(4)]
            top = pl.multiple_of(top, 8)
            here = (lane == k) & (line == row)
            return tuple(
                jnp.where(
                    here, pltpu.roll(fields[t + 1, tile, pl.ds(top, 8), :], turn, 1), found[t]
                )
                for t in range(STEPS)
            )

        none = (jnp.zeros((8, LANES), F32),) * STEPS
        found = lax.fori_loop(0, LANES, one_panel, none, unroll=32)
        for t in range(STEPS):
            sample_ref[t : t + 1, base : base + LANES] = jnp.sum(found[t], axis=0, keepdims=True)
    leave.wait()


def edges(field, mask, visc):
    rows, cols = field.shape
    edge_rows = jax.ShapeDtypeStruct((EDGE, cols), F32)
    return pl.pallas_call(
        rows_kernel,
        grid=(1,),
        in_specs=[pl.BlockSpec((8, cols), lambda i: (0, 0))] * 3
        + [pl.BlockSpec((8, cols), lambda i: (rows // 8 - 1, 0))] * 3,
        out_specs=[pl.BlockSpec((EDGE, cols), lambda i: (0, 0))] * 2,
        out_shape=[edge_rows, edge_rows],
        compiler_params=params(56),
        cost_estimate=cost(16 * cols, 256 * cols),
    )(field, mask, visc, field, mask, visc)


def shifted(axis, first, last):
    peers = lax.axis_size(axis)
    up = [(i, i + 1) for i in range(peers - 1)]
    down = [(i + 1, i) for i in range(peers - 1)]
    return lax.ppermute(last, axis, up), lax.ppermute(first, axis, down)


def field_window(field, mask, visc, before, after, panel_cell):
    rows, cols = field.shape
    tall = -(-(rows + EDGE) // LANES) * LANES
    edge_cols = jax.ShapeDtypeStruct((EDGE, tall), F32)

    panels = panel_cell.shape[0]
    first, last, places = pl.pallas_call(
        columns_kernel,
        in_specs=[VMEM] * 6,
        out_specs=[VMEM] * 3,
        out_shape=[edge_cols, edge_cols, jax.ShapeDtypeStruct((4, panels), jnp.int32)],
        scratch_shapes=[pltpu.VMEM((tall, LANES), F32)],
        compiler_params=params(16),
        cost_estimate=cost(rows * cols, 4 * rows * cols),
    )(panel_cell.reshape(1, panels), field, mask, visc, before, after)
    south, north = shifted("panel", first, last)
    tiles = cols // LANES + 1
    height = 16 + -(-(rows + 2 * PAD - 16) // STRIP) * STRIP
    return pl.pallas_call(
        step_kernel,
        in_specs=[SMEM] + [VMEM] * 7,
        out_specs=[pl.BlockSpec(memory_space=pl.ANY), VMEM],
        out_shape=[
            jax.ShapeDtypeStruct((rows, cols), F32),
            jax.ShapeDtypeStruct((STEPS, panels), F32),
        ],
        scratch_shapes=[
            pltpu.VMEM((STEPS + 1, tiles, height, LANES), F32),
            pltpu.VMEM((tiles, height, LANES), F32),
            pltpu.VMEM((LANES, tall), F32),
            pltpu.VMEM((rows, cols), F32),
            pltpu.SemaphoreType.DMA,
        ],
        compiler_params=params(24),
        cost_estimate=cost(100 * rows * cols, 800 * rows * cols),
    )(places, field, mask, visc, before, after, south, north)


def bin_kernel(half_ref, *refs):
    members = (len(refs) - 7) // 2
    words, samples = refs[:members], refs[members : 2 * members]
    keep_ref, send_ref, low_s, high_s, weight_s, acc_s, sig_s = refs[2 * members :]
    block, local = words[0].shape
    parts = local // LANES
    high = NB // LOW
    per_row = LANES // LOW
    half_rows = NB // LANES // 8
    low_tiles = LOW // 8 + 1
    depth = 2 * LANES
    shift = LOW.bit_length() - 1
    for s in range(members):
        for j in range(parts):
            word = words[s][:, j * LANES : (j + 1) * LANES]
            at = slice((s * parts + j) * LANES, (s * parts + j + 1) * LANES)
            low_s[:, at] = (word & (LOW - 1)).astype(F32)
            high_s[:, at] = ((word >> shift) & (high - 1)).astype(F32)
            amp = (word >> 16).astype(F32) * (1.0 / AMP_SCALE)
            for t in range(STEPS):
                weight_s[t, :, at] = amp * samples[s][j, t : t + 1, :]

    one = jnp.ones((), BF16)
    zero = jnp.zeros((), BF16)
    sub = lax.broadcasted_iota(jnp.int32, (16, depth), 0) & 7

    def number(x):
        return x.astype(F32).astype(BF16)

    high_ids = [
        number(per_row * (8 * (k % half_rows) + sub) + k // half_rows) for k in range(high // 8)
    ]
    low_ids = [[number(8 * k + sub - t) for t in range(STEPS)] for k in range(low_tiles)]
    lane = lax.broadcasted_iota(jnp.int32, (8, LANES), 1)
    lanes = lax.broadcasted_iota(jnp.int32, (NB // LANES, LANES), 1)
    acc_s[...] = jnp.zeros_like(acc_s)

    def two_observers(o, u):
        def spread(ref, *lead):
            rows = [
                jnp.broadcast_to(ref[(*lead, slice(o + e, o + e + 1), at)], (8, depth))
                for e in range(2)
            ]
            return jnp.concatenate(rows).astype(BF16)

        acc = None
        for c in range(members * local // depth):
            at = slice(c * depth, (c + 1) * depth)
            low_row, high_row = spread(low_s), spread(high_s)
            weights = [spread(weight_s, t) for t in range(STEPS)]
            left = jnp.concatenate([jnp.where(ids == high_row, one, zero) for ids in high_ids])
            right = []
            for k in range(low_tiles):
                placed = zero
                for t in range(1 if k * 8 >= LOW else 0, STEPS):
                    placed = jnp.where(low_ids[k][t] == low_row, weights[t], placed)
                right.append(placed)
            term = lax.dot_general(
                left, jnp.concatenate(right), (((1,), (1,)), ((), ())), preferred_element_type=F32
            )
            acc = term if acc is None else acc + term
        acc_s[u, :, : 16 * low_tiles] = acc
        for e in range(2):
            total = None
            for j in range(per_row):
                low = (lane - LOW * j) & (LANES - 1)
                source = jnp.where(low < 8 * low_tiles, 16 * (low // 8) + 8 * e + (low & 7), LANES - 1)
                tops = [16 * (j * half_rows + g) + 8 * e for g in range(half_rows)]
                x = jnp.concatenate(
                    [jnp.take_along_axis(acc_s[u, top : top + 8], source, axis=1) for top in tops]
                )
                if j == per_row - 1:
                    x = jnp.where(lanes < LOW, pltpu.roll(x, 1, 0), x)
                total = x if total is None else total + x
            sig_s[:, o + e : o + e + 1, :] = total[:, None, :]

    for u in range(block // 2):
        two_observers(2 * u, u)
    tiles = NB // LANES // 2
    per_owner = tiles // keep_ref.shape[0]
    for r in range(tiles):
        lanes = slice(r % per_owner * LANES, (r % per_owner + 1) * LANES)
        keep_ref[r // per_owner, :, lanes] = sig_s[half_ref[0] * tiles + r]
        sent = sig_s[(1 - half_ref[0]) * tiles + r]
        send_ref[r // per_owner, :, lanes] = sent.astype(BF16)


def binned(half, words, samples, first, count):
    members = len(words)
    local = words[0].shape[1]
    block = 16
    panels = members * local
    bins = NB // 2 // members
    out = pl.BlockSpec((members, block, bins), lambda i: (0, i, 0))
    return pl.pallas_call(
        bin_kernel,
        grid=(count // block,),
        in_specs=[SMEM]
        + [pl.BlockSpec((block, local), lambda i: (first // block + i, 0))] * members
        + [pl.BlockSpec(samples[0].shape, lambda i: (0, 0, 0))] * members,
        out_specs=[out, out],
        out_shape=[
            jax.ShapeDtypeStruct((members, count, bins), F32),
            jax.ShapeDtypeStruct((members, count, bins), BF16),
        ],
        scratch_shapes=[
            pltpu.VMEM((block, panels), F32),
            pltpu.VMEM((block, panels), F32),
            pltpu.VMEM((STEPS, block, panels), F32),
            pltpu.VMEM((block // 2, 2 * NB // LOW, LANES), F32),
            pltpu.VMEM((NB // LANES, block, LANES), F32),
        ],
        compiler_params=params(40),
        cost_estimate=cost(65536 * count * panels, 8 * count * panels),
    )(half, *words, *samples)


def join_kernel(parts, me_ref, *refs):
    keeps, gots, outs = refs[:parts], refs[parts : 2 * parts], refs[2 * parts :]
    for k, out in enumerate(outs):
        owner = lax.rem(me_ref[0] + k, len(outs))
        at = 0
        for keep, got in zip(keeps, gots):
            count = keep.shape[1]
            out[at : at + count] = (keep[owner] + got[owner].astype(F32)).astype(BF16)
            at += count


def join(me, keeps, gots):
    members, _, bins = keeps[0].shape
    count = sum(keep.shape[1] for keep in keeps)
    return pl.pallas_call(
        functools.partial(join_kernel, len(keeps)),
        in_specs=[SMEM] + [VMEM] * (2 * len(keeps)),
        out_specs=[VMEM] * members,
        out_shape=[jax.ShapeDtypeStruct((count, bins), BF16)] * members,
        compiler_params=params(16),
        cost_estimate=cost(members * count * bins, 8 * members * count * bins),
    )(me, *keeps, *gots)


def place_kernel(first, width, me_ref, *refs):
    members, count, _ = refs[-2].shape
    pieces, (out_ref, wide, sems) = refs[:members], refs[-3:]
    copies = []
    for k, ref in enumerate(pieces):
        owner = lax.rem(me_ref[0] - k + members, members)
        start = pl.multiple_of(owner * width + first, 16)
        wide[k] = ref[...].astype(F32)
        copies.append(
            pltpu.make_async_copy(wide.at[k], out_ref.at[pl.ds(start, count), :], sems.at[k])
        )
        copies[-1].start()
    for copy in copies:
        copy.wait()


def place(me, pieces, signals, first, width):
    members = len(pieces)
    count, bins = pieces[0].shape
    before = [] if signals is None else [signals]
    return pl.pallas_call(
        functools.partial(place_kernel, first, width),
        in_specs=[SMEM] + [VMEM] * members + [pl.BlockSpec(memory_space=pl.ANY)] * len(before),
        out_specs=pl.BlockSpec(memory_space=pl.ANY),
        out_shape=jax.ShapeDtypeStruct((width * members, bins), F32),
        input_output_aliases={members + 1: 0} if before else {},
        scratch_shapes=[
            pltpu.VMEM((members, count, bins), F32),
            pltpu.SemaphoreType.DMA((members,)),
        ],
        compiler_params=params(16),
        cost_estimate=cost(members * count * bins, 6 * members * count * bins),
    )(me, *pieces, *before)


def on_device(field_start, fluid_mask, base_visc, panel_cell, amplitude, delay_bin):
    peers = lax.axis_size("box")
    members = peers // 2
    index = lax.axis_index("box").astype(jnp.int32).reshape(1)
    me, half = lax.rem(index, members), index // members

    def spread(parts):
        def perm(k):
            return [(i, i // members * members + (i + k) % members) for i in range(peers)]

        return [lax.ppermute(x, "box", perm(k)) if k else x for k, x in enumerate(parts)]

    ends = edges(field_start, fluid_mask, base_visc)
    amplitude, delay_bin, *ends = lax.optimization_barrier((amplitude, delay_bin, *ends))
    before, after = shifted("box", *ends)
    packed = pack(me, amplitude, delay_bin, members)
    before, after, *packed = lax.optimization_barrier((before, after, *packed))
    words = spread(packed)
    field, sample = field_window(
        field_start, fluid_mask, base_visc, before, after, panel_cell
    )
    sample = lax.all_gather(sample, "panel")
    middle = members // 2
    sample, words[middle] = lax.optimization_barrier((sample, words[middle]))
    samples = spread([sample] * members)
    observers = words[0].shape[0]
    across = [(i, (i + members) % peers) for i in range(peers)]
    first, groups = 0, []
    for chunks in sizes(observers):
        groups.append([])
        for count in chunks:
            keep, send = binned(half, words, samples, first, count)
            keep, half = lax.optimization_barrier((keep, half))
            groups[-1].append((keep, lax.ppermute(send, "box", across)))
            first += count
    pieces, waiting = None, []
    for group in groups:
        keeps, gots = [x[0] for x in group], [x[1] for x in group]
        if pieces is not None:
            gots[-1], pieces[middle] = lax.optimization_barrier((gots[-1], pieces[middle]))
        pieces = spread(join(me, keeps, gots))
        waiting.append(pieces)
    first, signals = 0, None
    for pieces in waiting:
        signals = place(me, pieces, signals, first, observers)
        first += pieces[0].shape[0]
    return (field, signals)


def sizes(observers):
    units = observers // 16
    ends = [-(-units * part // 16) * 16 for part in PARTS]
    counts = [end - start for start, end in zip([0] + ends, ends)]
    return [[c for c in group if c] for group in (counts[:2], counts[2:]) if any(group)]


def solution(mesh):
    placed = (
        P("box", "panel"),
        P("box", "panel"),
        P("box", "panel"),
        P(("box", "panel")),
        P("box", "panel"),
        P("box", "panel"),
    )
    return jax.shard_map(
        on_device,
        mesh=mesh,
        in_specs=placed,
        out_specs=(P("box", "panel"), P("panel", "box")),
        check_vma=False,
    )
```

```python
import functools

import jax
import jax.numpy as jnp
from jax import lax
from jax.experimental import pallas as pl
from jax.experimental.pallas import tpu as pltpu
from jax.sharding import PartitionSpec as P

F32 = jnp.float32
BF16 = jnp.bfloat16
STEPS = 4
NB = 2048
LOW = 32
LANES = 128
EDGE = 2 * STEPS
PAD = 16
STRIP = 32
AMP_SCALE = 4096.0
PARTS = (7, 12, 16)
VMEM = pl.BlockSpec(memory_space=pltpu.VMEM)
SMEM = pl.BlockSpec(memory_space=pltpu.SMEM)


def params(mib):
    return pltpu.CompilerParams(vmem_limit_bytes=mib << 20)


def cost(flops, size):
    return pl.CostEstimate(flops=flops, bytes_accessed=size, transcendentals=0)


def target(me, k, members):
    return me ^ k if members & (members - 1) == 0 else (me + k) % members


def source(me, k, members):
    return me ^ k if members & (members - 1) == 0 else (me + members - k) % members


def pack_kernel(me_ref, amp_ref, bin_ref, *refs):
    outs, turned = refs[:-1], refs[-1]
    scaled = (amp_ref[...].astype(F32) * AMP_SCALE).astype(jnp.int32)
    turned[...] = jnp.transpose((scaled << 16) | bin_ref[...])
    width = outs[0].shape[0]
    for k, out in enumerate(outs):
        first = pl.multiple_of(target(me_ref[0], k, len(outs)) * width, 8)
        out[...] = turned[pl.ds(first, width), :]


def pack(me, amplitude, delay_bin, members):
    panels, observers = amplitude.shape
    width = observers // members
    block = pl.BlockSpec((LANES, observers), lambda i: (i, 0))
    out = jax.ShapeDtypeStruct((width, panels), jnp.int32)
    return pl.pallas_call(
        pack_kernel,
        grid=(panels // LANES,),
        in_specs=[SMEM, block, block],
        out_specs=[pl.BlockSpec((width, LANES), lambda i: (0, i))] * members,
        out_shape=[out] * members,
        scratch_shapes=[pltpu.VMEM((observers, LANES), jnp.int32)],
        compiler_params=params(56),
        cost_estimate=cost(panels * observers, 10 * panels * observers),
    )(me, amplitude, delay_bin)


def coded(mask, visc):
    return jnp.where(mask != 0, visc, 0.0)


def rows_kernel(f_top, m_top, v_top, f_end, m_end, v_end, first_ref, last_ref):
    first_ref[:STEPS] = f_top[:STEPS]
    first_ref[STEPS:] = coded(m_top[:STEPS], v_top[:STEPS])
    last_ref[:STEPS] = f_end[8 - STEPS :]
    last_ref[STEPS:] = coded(m_end[8 - STEPS :], v_end[8 - STEPS :])


def columns_kernel(
    cell_ref, field_ref, mask_ref, visc_ref, before_ref, after_ref, first_ref, last_ref, place_ref, tall
):
    rows, cols = field_ref.shape
    cell = cell_ref[...]
    row = lax.div(cell, cols)
    col = cell - row * cols
    panel = lax.broadcasted_iota(jnp.int32, cell.shape, 1)
    place_ref[0:1] = col // LANES
    place_ref[1:2] = row // 8 * 8 + PAD
    place_ref[2:3] = row & 7
    place_ref[3:4] = (panel - col) & (LANES - 1)
    tall[...] = jnp.zeros_like(tall)
    for part in range(2):
        halo = slice(part * STEPS, (part + 1) * STEPS)
        for start, low, out in ((0, 0, first_ref), (cols - LANES, LANES - STEPS, last_ref)):
            lanes = slice(start, start + LANES)
            if part:
                tall[:rows] = coded(mask_ref[:, lanes], visc_ref[:, lanes])
            else:
                tall[:rows] = field_ref[:, lanes]
            tall[rows : rows + STEPS] = after_ref[halo, lanes]
            tall[rows + STEPS : rows + EDGE] = before_ref[halo, lanes]
            out[halo] = jnp.transpose(tall[...])[low : low + STEPS]


def step_kernel(
    cell_ref,
    field_ref,
    mask_ref,
    visc_ref,
    before_ref,
    after_ref,
    south_ref,
    north_ref,
    end_ref,
    sample_ref,
    fields,
    visc,
    wide,
    last,
    sem,
):
    rows, cols = field_ref.shape
    panels = sample_ref.shape[1]
    tiles, height, _ = visc.shape
    wide[...] = jnp.zeros_like(wide)
    for part, buf in enumerate((fields.at[0], visc)):
        halo = slice(part * STEPS, (part + 1) * STEPS)
        wide[:STEPS] = north_ref[halo]
        wide[LANES - STEPS :] = south_ref[halo]
        side = jnp.transpose(wide[...])
        for k in range(tiles):
            at = slice(k * LANES, (k + 1) * LANES)
            buf[k, :PAD] = jnp.zeros((PAD, LANES), F32)
            buf[k, PAD + rows :] = jnp.zeros((height - PAD - rows, LANES), F32)
            if k == tiles - 1:
                inside, before, after = (
                    side[:rows],
                    side[rows + STEPS : rows + EDGE],
                    side[rows : rows + STEPS],
                )
            else:
                inside = coded(mask_ref[:, at], visc_ref[:, at]) if part else field_ref[:, at]
                before, after = before_ref[halo, at], after_ref[halo, at]
            buf[k, PAD : PAD + rows] = inside
            buf[k, PAD - STEPS : PAD] = before
            buf[k, PAD + rows : PAD + rows + STEPS] = after

    first_lane = lax.broadcasted_iota(jnp.int32, (STRIP, LANES), 1) == 0
    last_lane = lax.broadcasted_iota(jnp.int32, (STRIP, LANES), 1) == LANES - 1
    for step in range(STEPS):
        old, new = fields.at[step], fields.at[step + 1]
        for k in range(tiles):
            new[k, :8] = jnp.zeros((8, LANES), F32)
            new[k, height - 8 :] = jnp.zeros((8, LANES), F32)

        def one_strip(i, carry):
            top = pl.multiple_of(i * STRIP, 8)
            centers = [old[k, pl.ds(top + 8, STRIP), :] for k in range(tiles)]
            right = [pltpu.roll(x, 1, 1) for x in centers]
            left = [pltpu.roll(x, LANES - 1, 1) for x in centers]
            for k in range(tiles):
                window = old[k, pl.ds(top, STRIP + 16), :]
                base = visc[k, pl.ds(top + 8, STRIP), :]
                center = centers[k]
                west = pltpu.roll(window, 1, 0)[8 : 8 + STRIP]
                east = pltpu.roll(window, STRIP + 15, 0)[8 : 8 + STRIP]
                south = jnp.where(first_lane, right[k - 1], right[k])
                north = jnp.where(last_lane, left[(k + 1) % tiles], left[k])
                diff_x = east - west
                diff_y = north - south
                square = diff_x * diff_x + diff_y * diff_y
                norm = square * lax.rsqrt(jnp.maximum(square, 1e-37))
                viscosity = base + 0.05 * norm / (2.0 + norm)
                around = (east + west) + (north + south)
                update = 0.75 * center + 0.15 * west + 0.1 * south
                update = update + viscosity * (around - 4.0 * center)
                new[k, pl.ds(top + 8, STRIP), :] = jnp.where(base > 0.0, update, 0.0)
            return carry

        strips = (height - 16) // STRIP
        lax.fori_loop(0, strips, one_strip, 0, unroll=strips)
    for k in range(tiles - 1):
        last[:, k * LANES : (k + 1) * LANES] = fields[STEPS, k, PAD : PAD + rows, :]
    leave = pltpu.make_async_copy(last, end_ref, sem)
    leave.start()

    lane = lax.broadcasted_iota(jnp.int32, (8, LANES), 1)
    line = lax.broadcasted_iota(jnp.int32, (8, LANES), 0)
    for base in range(0, panels, LANES):

        def one_panel(k, found):
            tile, top, row, turn = [cell_ref[c, base + k] for c in range(4)]
            top = pl.multiple_of(top, 8)
            here = (lane == k) & (line == row)
            return tuple(
                jnp.where(
                    here, pltpu.roll(fields[t + 1, tile, pl.ds(top, 8), :], turn, 1), found[t]
                )
                for t in range(STEPS)
            )

        none = (jnp.zeros((8, LANES), F32),) * STEPS
        found = lax.fori_loop(0, LANES, one_panel, none, unroll=32)
        for t in range(STEPS):
            sample_ref[t : t + 1, base : base + LANES] = jnp.sum(found[t], axis=0, keepdims=True)
    leave.wait()


def edges(field, mask, visc):
    rows, cols = field.shape
    edge_rows = jax.ShapeDtypeStruct((EDGE, cols), F32)
    return pl.pallas_call(
        rows_kernel,
        grid=(1,),
        in_specs=[pl.BlockSpec((8, cols), lambda i: (0, 0))] * 3
        + [pl.BlockSpec((8, cols), lambda i: (rows // 8 - 1, 0))] * 3,
        out_specs=[pl.BlockSpec((EDGE, cols), lambda i: (0, 0))] * 2,
        out_shape=[edge_rows, edge_rows],
        compiler_params=params(56),
        cost_estimate=cost(16 * cols, 256 * cols),
    )(field, mask, visc, field, mask, visc)


def shifted(axis, first, last):
    peers = lax.axis_size(axis)
    up = [(i, i + 1) for i in range(peers - 1)]
    down = [(i + 1, i) for i in range(peers - 1)]
    return lax.ppermute(last, axis, up), lax.ppermute(first, axis, down)


def field_window(field, mask, visc, before, after, panel_cell):
    rows, cols = field.shape
    tall = -(-(rows + EDGE) // LANES) * LANES
    edge_cols = jax.ShapeDtypeStruct((EDGE, tall), F32)

    panels = panel_cell.shape[0]
    first, last, places = pl.pallas_call(
        columns_kernel,
        in_specs=[VMEM] * 6,
        out_specs=[VMEM] * 3,
        out_shape=[edge_cols, edge_cols, jax.ShapeDtypeStruct((4, panels), jnp.int32)],
        scratch_shapes=[pltpu.VMEM((tall, LANES), F32)],
        compiler_params=params(16),
        cost_estimate=cost(rows * cols, 4 * rows * cols),
    )(panel_cell.reshape(1, panels), field, mask, visc, before, after)
    south, north = shifted("panel", first, last)
    tiles = cols // LANES + 1
    height = 16 + -(-(rows + 2 * PAD - 16) // STRIP) * STRIP
    return pl.pallas_call(
        step_kernel,
        in_specs=[SMEM] + [VMEM] * 7,
        out_specs=[pl.BlockSpec(memory_space=pl.ANY), VMEM],
        out_shape=[
            jax.ShapeDtypeStruct((rows, cols), F32),
            jax.ShapeDtypeStruct((STEPS, panels), F32),
        ],
        scratch_shapes=[
            pltpu.VMEM((STEPS + 1, tiles, height, LANES), F32),
            pltpu.VMEM((tiles, height, LANES), F32),
            pltpu.VMEM((LANES, tall), F32),
            pltpu.VMEM((rows, cols), F32),
            pltpu.SemaphoreType.DMA,
        ],
        compiler_params=params(24),
        cost_estimate=cost(100 * rows * cols, 800 * rows * cols),
    )(places, field, mask, visc, before, after, south, north)


def bin_kernel(half_ref, *refs):
    members = (len(refs) - 7) // 2
    words, samples = refs[:members], refs[members : 2 * members]
    keep_ref, send_ref, low_s, high_s, weight_s, acc_s, sig_s = refs[2 * members :]
    block, local = words[0].shape
    parts = local // LANES
    high = NB // LOW
    per_row = LANES // LOW
    half_rows = NB // LANES // 8
    low_tiles = LOW // 8 + 1
    depth = 2 * LANES
    shift = LOW.bit_length() - 1
    for s in range(members):
        for j in range(parts):
            word = words[s][:, j * LANES : (j + 1) * LANES]
            at = slice((s * parts + j) * LANES, (s * parts + j + 1) * LANES)
            low_s[:, at] = (word & (LOW - 1)).astype(F32)
            high_s[:, at] = ((word >> shift) & (high - 1)).astype(F32)
            amp = (word >> 16).astype(F32) * (1.0 / AMP_SCALE)
            for t in range(STEPS):
                weight_s[t, :, at] = amp * samples[s][j, t : t + 1, :]

    one = jnp.ones((), BF16)
    zero = jnp.zeros((), BF16)
    sub = lax.broadcasted_iota(jnp.int32, (16, depth), 0) & 7

    def number(x):
        return x.astype(F32).astype(BF16)

    high_ids = [
        number(per_row * (8 * (k % half_rows) + sub) + k // half_rows) for k in range(high // 8)
    ]
    low_ids = [[number(8 * k + sub - t) for t in range(STEPS)] for k in range(low_tiles)]
    lane = lax.broadcasted_iota(jnp.int32, (8, LANES), 1)
    lanes = lax.broadcasted_iota(jnp.int32, (NB // LANES, LANES), 1)
    acc_s[...] = jnp.zeros_like(acc_s)

    def two_observers(o, u):
        def spread(ref, *lead):
            rows = [
                jnp.broadcast_to(ref[(*lead, slice(o + e, o + e + 1), at)], (8, depth))
                for e in range(2)
            ]
            return jnp.concatenate(rows).astype(BF16)

        acc = None
        for c in range(members * local // depth):
            at = slice(c * depth, (c + 1) * depth)
            low_row, high_row = spread(low_s), spread(high_s)
            weights = [spread(weight_s, t) for t in range(STEPS)]
            left = jnp.concatenate([jnp.where(ids == high_row, one, zero) for ids in high_ids])
            right = []
            for k in range(low_tiles):
                placed = zero
                for t in range(1 if k * 8 >= LOW else 0, STEPS):
                    placed = jnp.where(low_ids[k][t] == low_row, weights[t], placed)
                right.append(placed)
            term = lax.dot_general(
                left, jnp.concatenate(right), (((1,), (1,)), ((), ())), preferred_element_type=F32
            )
            acc = term if acc is None else acc + term
        acc_s[u, :, : 16 * low_tiles] = acc
        for e in range(2):
            total = None
            for j in range(per_row):
                low = (lane - LOW * j) & (LANES - 1)
                source = jnp.where(low < 8 * low_tiles, 16 * (low // 8) + 8 * e + (low & 7), LANES - 1)
                tops = [16 * (j * half_rows + g) + 8 * e for g in range(half_rows)]
                x = jnp.concatenate(
                    [jnp.take_along_axis(acc_s[u, top : top + 8], source, axis=1) for top in tops]
                )
                if j == per_row - 1:
                    x = jnp.where(lanes < LOW, pltpu.roll(x, 1, 0), x)
                total = x if total is None else total + x
            sig_s[:, o + e : o + e + 1, :] = total[:, None, :]

    for u in range(block // 2):
        two_observers(2 * u, u)
    tiles = NB // LANES // 2
    per_owner = tiles // keep_ref.shape[0]
    for r in range(tiles):
        lanes = slice(r % per_owner * LANES, (r % per_owner + 1) * LANES)
        keep_ref[r // per_owner, :, lanes] = sig_s[half_ref[0] * tiles + r]
        sent = sig_s[(1 - half_ref[0]) * tiles + r]
        send_ref[r // per_owner, :, lanes] = sent.astype(BF16)


def binned(half, words, samples, first, count):
    members = len(words)
    local = words[0].shape[1]
    block = 16
    panels = members * local
    bins = NB // 2 // members
    out = pl.BlockSpec((members, block, bins), lambda i: (0, i, 0))
    return pl.pallas_call(
        bin_kernel,
        grid=(count // block,),
        in_specs=[SMEM]
        + [pl.BlockSpec((block, local), lambda i: (first // block + i, 0))] * members
        + [pl.BlockSpec(samples[0].shape, lambda i: (0, 0, 0))] * members,
        out_specs=[out, out],
        out_shape=[
            jax.ShapeDtypeStruct((members, count, bins), F32),
            jax.ShapeDtypeStruct((members, count, bins), BF16),
        ],
        scratch_shapes=[
            pltpu.VMEM((block, panels), F32),
            pltpu.VMEM((block, panels), F32),
            pltpu.VMEM((STEPS, block, panels), F32),
            pltpu.VMEM((block // 2, 2 * NB // LOW, LANES), F32),
            pltpu.VMEM((NB // LANES, block, LANES), F32),
        ],
        compiler_params=params(40),
        cost_estimate=cost(65536 * count * panels, 8 * count * panels),
    )(half, *words, *samples)


def join_kernel(parts, me_ref, *refs):
    keeps, gots, outs = refs[:parts], refs[parts : 2 * parts], refs[2 * parts :]
    for k, out in enumerate(outs):
        owner = target(me_ref[0], k, len(outs))
        at = 0
        for keep, got in zip(keeps, gots):
            count = keep.shape[1]
            out[at : at + count] = (keep[owner] + got[owner].astype(F32)).astype(BF16)
            at += count


def join(me, keeps, gots):
    members, _, bins = keeps[0].shape
    count = sum(keep.shape[1] for keep in keeps)
    return pl.pallas_call(
        functools.partial(join_kernel, len(keeps)),
        in_specs=[SMEM] + [VMEM] * (2 * len(keeps)),
        out_specs=[VMEM] * members,
        out_shape=[jax.ShapeDtypeStruct((count, bins), BF16)] * members,
        compiler_params=params(16),
        cost_estimate=cost(members * count * bins, 8 * members * count * bins),
    )(me, *keeps, *gots)


def place_kernel(first, width, me_ref, *refs):
    members, count, _ = refs[-2].shape
    pieces, (out_ref, wide, sems) = refs[:members], refs[-3:]
    copies = []
    for k, ref in enumerate(pieces):
        owner = source(me_ref[0], k, members)
        start = pl.multiple_of(owner * width + first, 16)
        wide[k] = ref[...].astype(F32)
        copies.append(
            pltpu.make_async_copy(wide.at[k], out_ref.at[pl.ds(start, count), :], sems.at[k])
        )
        copies[-1].start()
    for copy in copies:
        copy.wait()


def place(me, pieces, signals, first, width):
    members = len(pieces)
    count, bins = pieces[0].shape
    before = [] if signals is None else [signals]
    return pl.pallas_call(
        functools.partial(place_kernel, first, width),
        in_specs=[SMEM] + [VMEM] * members + [pl.BlockSpec(memory_space=pl.ANY)] * len(before),
        out_specs=pl.BlockSpec(memory_space=pl.ANY),
        out_shape=jax.ShapeDtypeStruct((width * members, bins), F32),
        input_output_aliases={members + 1: 0} if before else {},
        scratch_shapes=[
            pltpu.VMEM((members, count, bins), F32),
            pltpu.SemaphoreType.DMA((members,)),
        ],
        compiler_params=params(16),
        cost_estimate=cost(members * count * bins, 6 * members * count * bins),
    )(me, *pieces, *before)


def on_device(field_start, fluid_mask, base_visc, panel_cell, amplitude, delay_bin):
    peers = lax.axis_size("box")
    members = peers // 2
    index = lax.axis_index("box").astype(jnp.int32).reshape(1)
    me, half = lax.rem(index, members), index // members

    def spread(parts):
        def perm(k):
            return [
                (i, i // members * members + target(i % members, k, members)) for i in range(peers)
            ]

        return [lax.ppermute(x, "box", perm(k)) if k else x for k, x in enumerate(parts)]

    ends = edges(field_start, fluid_mask, base_visc)
    amplitude, delay_bin, *ends = lax.optimization_barrier((amplitude, delay_bin, *ends))
    before, after = shifted("box", *ends)
    packed = pack(me, amplitude, delay_bin, members)
    before, after, *packed = lax.optimization_barrier((before, after, *packed))
    words = spread(packed)
    field, sample = field_window(
        field_start, fluid_mask, base_visc, before, after, panel_cell
    )
    sample = lax.all_gather(sample, "panel")
    middle = members // 2
    sample, words[middle] = lax.optimization_barrier((sample, words[middle]))
    samples = spread([sample] * members)
    observers = words[0].shape[0]
    across = [(i, (i + members) % peers) for i in range(peers)]
    first, groups = 0, []
    for chunks in sizes(observers):
        groups.append([])
        for count in chunks:
            keep, send = binned(half, words, samples, first, count)
            keep, half = lax.optimization_barrier((keep, half))
            groups[-1].append((keep, lax.ppermute(send, "box", across)))
            first += count
    pieces, waiting = None, []
    for group in groups:
        keeps, gots = [x[0] for x in group], [x[1] for x in group]
        if pieces is not None:
            gots[-1], pieces[middle] = lax.optimization_barrier((gots[-1], pieces[middle]))
        pieces = spread(join(me, keeps, gots))
        waiting.append(pieces)
    first, signals = 0, None
    for pieces in waiting:
        signals = place(me, pieces, signals, first, observers)
        first += pieces[0].shape[0]
    return (field, signals)


def sizes(observers):
    units = observers // 16
    ends = [-(-units * part // 16) * 16 for part in PARTS]
    counts = [end - start for start, end in zip([0] + ends, ends)]
    return [[c for c in group if c] for group in (counts[:2], counts[2:]) if any(group)]


def solution(mesh):
    placed = (
        P("box", "panel"),
        P("box", "panel"),
        P("box", "panel"),
        P(("box", "panel")),
        P("box", "panel"),
        P("box", "panel"),
    )
    return jax.shard_map(
        on_device,
        mesh=mesh,
        in_specs=placed,
        out_specs=(P("box", "panel"), P("panel", "box")),
        check_vma=False,
    )
```

```python
import functools

import jax
import jax.numpy as jnp
from jax import lax
from jax.experimental import pallas as pl
from jax.experimental.pallas import tpu as pltpu
from jax.sharding import PartitionSpec as P

F32 = jnp.float32
BF16 = jnp.bfloat16
STEPS = 4
NB = 2048
LOW = 32
LANES = 128
EDGE = 2 * STEPS
PAD = 16
STRIP = 32
AMP_SCALE = 4096.0
PARTS = (7, 12, 16)
VMEM = pl.BlockSpec(memory_space=pltpu.VMEM)
SMEM = pl.BlockSpec(memory_space=pltpu.SMEM)


def params(mib):
    return pltpu.CompilerParams(vmem_limit_bytes=mib << 20)


def cost(flops, size):
    return pl.CostEstimate(flops=flops, bytes_accessed=size, transcendentals=0)


def target(me, k, members):
    return me ^ k if members & (members - 1) == 0 else (me + k) % members


def source(me, k, members):
    return me ^ k if members & (members - 1) == 0 else (me + members - k) % members


def pack_kernel(me_ref, amp_ref, bin_ref, *refs):
    outs, turned = refs[:-1], refs[-1]
    scaled = (amp_ref[...].astype(F32) * AMP_SCALE).astype(jnp.int32)
    turned[...] = jnp.transpose((scaled << 16) | bin_ref[...])
    width = outs[0].shape[0]
    for k, out in enumerate(outs):
        first = pl.multiple_of(target(me_ref[0], k, len(outs)) * width, 8)
        out[...] = turned[pl.ds(first, width), :]


def pack(me, amplitude, delay_bin, members):
    panels, observers = amplitude.shape
    width = observers // members
    block = pl.BlockSpec((LANES, observers), lambda i: (i, 0))
    out = jax.ShapeDtypeStruct((width, panels), jnp.int32)
    return pl.pallas_call(
        pack_kernel,
        grid=(panels // LANES,),
        in_specs=[SMEM, block, block],
        out_specs=[pl.BlockSpec((width, LANES), lambda i: (0, i))] * members,
        out_shape=[out] * members,
        scratch_shapes=[pltpu.VMEM((observers, LANES), jnp.int32)],
        compiler_params=params(56),
        cost_estimate=cost(panels * observers, 10 * panels * observers),
    )(me, amplitude, delay_bin)


def coded(mask, visc):
    return jnp.where(mask != 0, visc, 0.0)


def rows_kernel(f_top, m_top, v_top, f_end, m_end, v_end, first_ref, last_ref):
    first_ref[:STEPS] = f_top[:STEPS]
    first_ref[STEPS:] = coded(m_top[:STEPS], v_top[:STEPS])
    last_ref[:STEPS] = f_end[8 - STEPS :]
    last_ref[STEPS:] = coded(m_end[8 - STEPS :], v_end[8 - STEPS :])


def columns_kernel(
    cell_ref, field_ref, mask_ref, visc_ref, before_ref, after_ref, first_ref, last_ref, place_ref, tall
):
    rows, cols = field_ref.shape
    cell = cell_ref[...]
    row = lax.div(cell, cols)
    col = cell - row * cols
    panel = lax.broadcasted_iota(jnp.int32, cell.shape, 1)
    place_ref[0:1] = col // LANES
    place_ref[1:2] = row // 8 * 8 + PAD
    place_ref[2:3] = row & 7
    place_ref[3:4] = (panel - col) & (LANES - 1)
    tall[...] = jnp.zeros_like(tall)
    for part in range(2):
        halo = slice(part * STEPS, (part + 1) * STEPS)
        for start, low, out in ((0, 0, first_ref), (cols - LANES, LANES - STEPS, last_ref)):
            lanes = slice(start, start + LANES)
            if part:
                tall[:rows] = coded(mask_ref[:, lanes], visc_ref[:, lanes])
            else:
                tall[:rows] = field_ref[:, lanes]
            tall[rows : rows + STEPS] = after_ref[halo, lanes]
            tall[rows + STEPS : rows + EDGE] = before_ref[halo, lanes]
            out[halo] = jnp.transpose(tall[...])[low : low + STEPS]


def step_kernel(
    cell_ref,
    field_ref,
    mask_ref,
    visc_ref,
    before_ref,
    after_ref,
    south_ref,
    north_ref,
    end_ref,
    sample_ref,
    fields,
    visc,
    wide,
    last,
    sem,
):
    rows, cols = field_ref.shape
    panels = sample_ref.shape[1]
    tiles, height, _ = visc.shape
    wide[...] = jnp.zeros_like(wide)
    for part, buf in enumerate((fields.at[0], visc)):
        halo = slice(part * STEPS, (part + 1) * STEPS)
        wide[:STEPS] = north_ref[halo]
        wide[LANES - STEPS :] = south_ref[halo]
        side = jnp.transpose(wide[...])
        for k in range(tiles):
            at = slice(k * LANES, (k + 1) * LANES)
            buf[k, :PAD] = jnp.zeros((PAD, LANES), F32)
            buf[k, PAD + rows :] = jnp.zeros((height - PAD - rows, LANES), F32)
            if k == tiles - 1:
                inside, before, after = (
                    side[:rows],
                    side[rows + STEPS : rows + EDGE],
                    side[rows : rows + STEPS],
                )
            else:
                inside = coded(mask_ref[:, at], visc_ref[:, at]) if part else field_ref[:, at]
                before, after = before_ref[halo, at], after_ref[halo, at]
            buf[k, PAD : PAD + rows] = inside
            buf[k, PAD - STEPS : PAD] = before
            buf[k, PAD + rows : PAD + rows + STEPS] = after

    first_lane = lax.broadcasted_iota(jnp.int32, (STRIP, LANES), 1) == 0
    last_lane = lax.broadcasted_iota(jnp.int32, (STRIP, LANES), 1) == LANES - 1
    for step in range(STEPS):
        old, new = fields.at[step], fields.at[step + 1]
        for k in range(tiles):
            new[k, :8] = jnp.zeros((8, LANES), F32)
            new[k, height - 8 :] = jnp.zeros((8, LANES), F32)

        def one_strip(i, carry):
            top = pl.multiple_of(i * STRIP, 8)
            centers = [old[k, pl.ds(top + 8, STRIP), :] for k in range(tiles)]
            right = [pltpu.roll(x, 1, 1) for x in centers]
            left = [pltpu.roll(x, LANES - 1, 1) for x in centers]
            for k in range(tiles):
                window = old[k, pl.ds(top, STRIP + 16), :]
                base = visc[k, pl.ds(top + 8, STRIP), :]
                center = centers[k]
                west = pltpu.roll(window, 1, 0)[8 : 8 + STRIP]
                east = pltpu.roll(window, STRIP + 15, 0)[8 : 8 + STRIP]
                south = jnp.where(first_lane, right[k - 1], right[k])
                north = jnp.where(last_lane, left[(k + 1) % tiles], left[k])
                diff_x = east - west
                diff_y = north - south
                square = diff_x * diff_x + diff_y * diff_y
                norm = square * lax.rsqrt(jnp.maximum(square, 1e-37))
                viscosity = base + 0.05 * norm / (2.0 + norm)
                around = (east + west) + (north + south)
                update = 0.75 * center + 0.15 * west + 0.1 * south
                update = update + viscosity * (around - 4.0 * center)
                new[k, pl.ds(top + 8, STRIP), :] = jnp.where(base > 0.0, update, 0.0)
            return carry

        strips = (height - 16) // STRIP
        lax.fori_loop(0, strips, one_strip, 0, unroll=strips)
    for k in range(tiles - 1):
        last[:, k * LANES : (k + 1) * LANES] = fields[STEPS, k, PAD : PAD + rows, :]
    leave = pltpu.make_async_copy(last, end_ref, sem)
    leave.start()

    lane = lax.broadcasted_iota(jnp.int32, (8, LANES), 1)
    line = lax.broadcasted_iota(jnp.int32, (8, LANES), 0)
    for base in range(0, panels, LANES):

        def one_panel(k, found):
            tile, top, row, turn = [cell_ref[c, base + k] for c in range(4)]
            top = pl.multiple_of(top, 8)
            here = (lane == k) & (line == row)
            return tuple(
                jnp.where(
                    here, pltpu.roll(fields[t + 1, tile, pl.ds(top, 8), :], turn, 1), found[t]
                )
                for t in range(STEPS)
            )

        none = (jnp.zeros((8, LANES), F32),) * STEPS
        found = lax.fori_loop(0, LANES, one_panel, none, unroll=32)
        for t in range(STEPS):
            sample_ref[t : t + 1, base : base + LANES] = jnp.sum(found[t], axis=0, keepdims=True)
    leave.wait()


def edges(field, mask, visc):
    rows, cols = field.shape
    edge_rows = jax.ShapeDtypeStruct((EDGE, cols), F32)
    return pl.pallas_call(
        rows_kernel,
        grid=(1,),
        in_specs=[pl.BlockSpec((8, cols), lambda i: (0, 0))] * 3
        + [pl.BlockSpec((8, cols), lambda i: (rows // 8 - 1, 0))] * 3,
        out_specs=[pl.BlockSpec((EDGE, cols), lambda i: (0, 0))] * 2,
        out_shape=[edge_rows, edge_rows],
        compiler_params=params(56),
        cost_estimate=cost(16 * cols, 256 * cols),
    )(field, mask, visc, field, mask, visc)


def shifted(axis, first, last):
    peers = lax.axis_size(axis)
    up = [(i, i + 1) for i in range(peers - 1)]
    down = [(i + 1, i) for i in range(peers - 1)]
    return lax.ppermute(last, axis, up), lax.ppermute(first, axis, down)


def field_window(field, mask, visc, before, after, panel_cell):
    rows, cols = field.shape
    tall = -(-(rows + EDGE) // LANES) * LANES
    edge_cols = jax.ShapeDtypeStruct((EDGE, tall), F32)

    panels = panel_cell.shape[0]
    first, last, places = pl.pallas_call(
        columns_kernel,
        in_specs=[VMEM] * 6,
        out_specs=[VMEM] * 3,
        out_shape=[edge_cols, edge_cols, jax.ShapeDtypeStruct((4, panels), jnp.int32)],
        scratch_shapes=[pltpu.VMEM((tall, LANES), F32)],
        compiler_params=params(16),
        cost_estimate=cost(rows * cols, 4 * rows * cols),
    )(panel_cell.reshape(1, panels), field, mask, visc, before, after)
    south, north = shifted("panel", first, last)
    tiles = cols // LANES + 1
    height = 16 + -(-(rows + 2 * PAD - 16) // STRIP) * STRIP
    return pl.pallas_call(
        step_kernel,
        in_specs=[SMEM] + [VMEM] * 7,
        out_specs=[pl.BlockSpec(memory_space=pl.ANY), VMEM],
        out_shape=[
            jax.ShapeDtypeStruct((rows, cols), F32),
            jax.ShapeDtypeStruct((STEPS, panels), F32),
        ],
        scratch_shapes=[
            pltpu.VMEM((STEPS + 1, tiles, height, LANES), F32),
            pltpu.VMEM((tiles, height, LANES), F32),
            pltpu.VMEM((LANES, tall), F32),
            pltpu.VMEM((rows, cols), F32),
            pltpu.SemaphoreType.DMA,
        ],
        compiler_params=params(24),
        cost_estimate=cost(100 * rows * cols, 800 * rows * cols),
    )(places, field, mask, visc, before, after, south, north)


def bin_kernel(half_ref, *refs):
    members = (len(refs) - 7) // 2
    words, samples = refs[:members], refs[members : 2 * members]
    keep_ref, send_ref, low_s, high_s, weight_s, acc_s, sig_s = refs[2 * members :]
    block, local = words[0].shape
    parts = local // LANES
    high = NB // LOW
    per_row = LANES // LOW
    half_rows = NB // LANES // 8
    low_tiles = LOW // 8 + 1
    depth = 2 * LANES
    shift = LOW.bit_length() - 1
    for s in range(members):
        for j in range(parts):
            word = words[s][:, j * LANES : (j + 1) * LANES]
            at = slice((s * parts + j) * LANES, (s * parts + j + 1) * LANES)
            low_s[:, at] = (word & (LOW - 1)).astype(F32)
            high_s[:, at] = ((word >> shift) & (high - 1)).astype(F32)
            amp = (word >> 16).astype(F32) * (1.0 / AMP_SCALE)
            for t in range(STEPS):
                weight_s[t, :, at] = amp * samples[s][j, t : t + 1, :]

    one = jnp.ones((), BF16)
    zero = jnp.zeros((), BF16)
    sub = lax.broadcasted_iota(jnp.int32, (16, depth), 0) & 7

    def number(x):
        return x.astype(F32).astype(BF16)

    high_ids = [
        number(per_row * (8 * (k % half_rows) + sub) + k // half_rows) for k in range(high // 8)
    ]
    low_ids = [[number(8 * k + sub - t) for t in range(STEPS)] for k in range(low_tiles)]
    lane = lax.broadcasted_iota(jnp.int32, (8, LANES), 1)
    lanes = lax.broadcasted_iota(jnp.int32, (NB // LANES, LANES), 1)
    acc_s[...] = jnp.zeros_like(acc_s)

    def two_observers(o, u):
        def spread(ref, *lead):
            rows = [
                jnp.broadcast_to(ref[(*lead, slice(o + e, o + e + 1), at)], (8, depth))
                for e in range(2)
            ]
            return jnp.concatenate(rows).astype(BF16)

        acc = None
        for c in range(members * local // depth):
            at = slice(c * depth, (c + 1) * depth)
            low_row, high_row = spread(low_s), spread(high_s)
            weights = [spread(weight_s, t) for t in range(STEPS)]
            left = jnp.concatenate([jnp.where(ids == high_row, one, zero) for ids in high_ids])
            right = []
            for k in range(low_tiles):
                placed = zero
                for t in range(1 if k * 8 >= LOW else 0, STEPS):
                    placed = jnp.where(low_ids[k][t] == low_row, weights[t], placed)
                right.append(placed)
            term = lax.dot_general(
                left, jnp.concatenate(right), (((1,), (1,)), ((), ())), preferred_element_type=F32
            )
            acc = term if acc is None else acc + term
        acc_s[u, :, : 16 * low_tiles] = acc
        for e in range(2):
            total = None
            for j in range(per_row):
                low = (lane - LOW * j) & (LANES - 1)
                source = jnp.where(low < 8 * low_tiles, 16 * (low // 8) + 8 * e + (low & 7), LANES - 1)
                tops = [16 * (j * half_rows + g) + 8 * e for g in range(half_rows)]
                x = jnp.concatenate(
                    [jnp.take_along_axis(acc_s[u, top : top + 8], source, axis=1) for top in tops]
                )
                if j == per_row - 1:
                    x = jnp.where(lanes < LOW, pltpu.roll(x, 1, 0), x)
                total = x if total is None else total + x
            sig_s[:, o + e : o + e + 1, :] = total[:, None, :]

    for u in range(block // 2):
        two_observers(2 * u, u)
    tiles = NB // LANES // 2
    per_owner = tiles // keep_ref.shape[0]
    for r in range(tiles):
        lanes = slice(r % per_owner * LANES, (r % per_owner + 1) * LANES)
        keep_ref[r // per_owner, :, lanes] = sig_s[half_ref[0] * tiles + r]
        sent = sig_s[(1 - half_ref[0]) * tiles + r]
        send_ref[r // per_owner, :, lanes] = sent.astype(BF16)


def binned(half, words, samples, first, count):
    members = len(words)
    local = words[0].shape[1]
    block = 16
    panels = members * local
    bins = NB // 2 // members
    out = pl.BlockSpec((members, block, bins), lambda i: (0, i, 0))
    return pl.pallas_call(
        bin_kernel,
        grid=(count // block,),
        in_specs=[SMEM]
        + [pl.BlockSpec((block, local), lambda i: (first // block + i, 0))] * members
        + [pl.BlockSpec(samples[0].shape, lambda i: (0, 0, 0))] * members,
        out_specs=[out, out],
        out_shape=[
            jax.ShapeDtypeStruct((members, count, bins), F32),
            jax.ShapeDtypeStruct((members, count, bins), BF16),
        ],
        scratch_shapes=[
            pltpu.VMEM((block, panels), F32),
            pltpu.VMEM((block, panels), F32),
            pltpu.VMEM((STEPS, block, panels), F32),
            pltpu.VMEM((block // 2, 2 * NB // LOW, LANES), F32),
            pltpu.VMEM((NB // LANES, block, LANES), F32),
        ],
        compiler_params=params(40),
        cost_estimate=cost(65536 * count * panels, 8 * count * panels),
    )(half, *words, *samples)


def join_kernel(parts, me_ref, *refs):
    keeps, gots, outs = refs[:parts], refs[parts : 2 * parts], refs[2 * parts :]
    for k, out in enumerate(outs):
        owner = target(me_ref[0], k, len(outs))
        at = 0
        for keep, got in zip(keeps, gots):
            count = keep.shape[1]
            out[at : at + count] = (keep[owner] + got[owner].astype(F32)).astype(BF16)
            at += count


def join(me, keeps, gots):
    members, _, bins = keeps[0].shape
    count = sum(keep.shape[1] for keep in keeps)
    return pl.pallas_call(
        functools.partial(join_kernel, len(keeps)),
        in_specs=[SMEM] + [VMEM] * (2 * len(keeps)),
        out_specs=[VMEM] * members,
        out_shape=[jax.ShapeDtypeStruct((count, bins), BF16)] * members,
        compiler_params=params(16),
        cost_estimate=cost(members * count * bins, 8 * members * count * bins),
    )(me, *keeps, *gots)


def place_kernel(first, width, me_ref, *refs):
    members, count, _ = refs[-2].shape
    pieces, (out_ref, wide, sems) = refs[:members], refs[-3:]
    copies = []
    for k, ref in enumerate(pieces):
        owner = source(me_ref[0], k, members)
        start = pl.multiple_of(owner * width + first, 16)
        wide[k] = ref[...].astype(F32)
        copies.append(
            pltpu.make_async_copy(wide.at[k], out_ref.at[pl.ds(start, count), :], sems.at[k])
        )
        copies[-1].start()
    for copy in copies:
        copy.wait()


def place(me, pieces, signals, first, width):
    members = len(pieces)
    count, bins = pieces[0].shape
    before = [] if signals is None else [signals]
    return pl.pallas_call(
        functools.partial(place_kernel, first, width),
        in_specs=[SMEM] + [VMEM] * members + [pl.BlockSpec(memory_space=pl.ANY)] * len(before),
        out_specs=pl.BlockSpec(memory_space=pl.ANY),
        out_shape=jax.ShapeDtypeStruct((width * members, bins), F32),
        input_output_aliases={members + 1: 0} if before else {},
        scratch_shapes=[
            pltpu.VMEM((members, count, bins), F32),
            pltpu.SemaphoreType.DMA((members,)),
        ],
        compiler_params=params(16),
        cost_estimate=cost(members * count * bins, 6 * members * count * bins),
    )(me, *pieces, *before)


def on_device(field_start, fluid_mask, base_visc, panel_cell, amplitude, delay_bin):
    peers = lax.axis_size("box")
    members = peers // 2
    index = lax.axis_index("box").astype(jnp.int32).reshape(1)
    me, half = lax.rem(index, members), index // members

    def spread(parts):
        def perm(k):
            return [
                (i, i // members * members + target(i % members, k, members)) for i in range(peers)
            ]

        return [lax.ppermute(x, "box", perm(k)) if k else x for k, x in enumerate(parts)]

    ends = edges(field_start, fluid_mask, base_visc)
    amplitude, delay_bin, *ends = lax.optimization_barrier((amplitude, delay_bin, *ends))
    before, after = shifted("box", *ends)
    packed = pack(me, amplitude, delay_bin, members)
    before, after, *packed = lax.optimization_barrier((before, after, *packed))
    words = spread(packed)
    field, sample = field_window(
        field_start, fluid_mask, base_visc, before, after, panel_cell
    )
    sample = lax.all_gather(sample, "panel")
    middle = members // 2
    sample, words[middle] = lax.optimization_barrier((sample, words[middle]))
    samples = spread([sample] * members)
    observers = words[0].shape[0]
    across = [(i, (i + members) % peers) for i in range(peers)]
    first, groups = 0, []
    for chunks in sizes(observers):
        groups.append([])
        for count in chunks:
            keep, send = binned(half, words, samples, first, count)
            keep, half = lax.optimization_barrier((keep, half))
            groups[-1].append((keep, lax.ppermute(send, "box", across)))
            first += count
    pieces, waiting = None, []
    for group in groups:
        keeps, gots = [x[0] for x in group], [x[1] for x in group]
        if pieces is not None:
            gots[-1], pieces[1] = lax.optimization_barrier((gots[-1], pieces[1]))
        pieces = spread(join(me, keeps, gots))
        waiting.append(pieces)
    first, signals = 0, None
    for pieces in waiting:
        signals = place(me, pieces, signals, first, observers)
        first += pieces[0].shape[0]
    return (field, signals)


def sizes(observers):
    units = observers // 16
    ends = [-(-units * part // 16) * 16 for part in PARTS]
    counts = [end - start for start, end in zip([0] + ends, ends)]
    return [[c for c in group if c] for group in (counts[:2], counts[2:]) if any(group)]


def solution(mesh):
    placed = (
        P("box", "panel"),
        P("box", "panel"),
        P("box", "panel"),
        P(("box", "panel")),
        P("box", "panel"),
        P("box", "panel"),
    )
    return jax.shard_map(
        on_device,
        mesh=mesh,
        in_specs=placed,
        out_specs=(P("box", "panel"), P("panel", "box")),
        check_vma=False,
    )
```

```python
import functools

import jax
import jax.numpy as jnp
from jax import lax
from jax.experimental import pallas as pl
from jax.experimental.pallas import tpu as pltpu
from jax.sharding import PartitionSpec as P

F32 = jnp.float32
BF16 = jnp.bfloat16
STEPS = 4
NB = 2048
LOW = 32
LANES = 128
EDGE = 2 * STEPS
PAD = 16
STRIP = 32
AMP_SCALE = 4096.0
PARTS = (7, 12, 16)
VMEM = pl.BlockSpec(memory_space=pltpu.VMEM)
SMEM = pl.BlockSpec(memory_space=pltpu.SMEM)


def params(mib):
    return pltpu.CompilerParams(vmem_limit_bytes=mib << 20)


def cost(flops, size):
    return pl.CostEstimate(flops=flops, bytes_accessed=size, transcendentals=0)


def target(me, k, members):
    return me ^ k if members & (members - 1) == 0 else (me + k) % members


def pack_kernel(me_ref, amp_ref, bin_ref, *refs):
    outs, turned = refs[:-1], refs[-1]
    scaled = (amp_ref[...].astype(F32) * AMP_SCALE).astype(jnp.int32)
    turned[...] = jnp.transpose((scaled << 16) | bin_ref[...])
    width = outs[0].shape[0]
    for k, out in enumerate(outs):
        first = pl.multiple_of(target(me_ref[0], k, len(outs)) * width, 8)
        out[...] = turned[pl.ds(first, width), :]


def pack(me, amplitude, delay_bin, members):
    panels, observers = amplitude.shape
    width = observers // members
    block = pl.BlockSpec((LANES, observers), lambda i: (i, 0))
    out = jax.ShapeDtypeStruct((width, panels), jnp.int32)
    return pl.pallas_call(
        pack_kernel,
        grid=(panels // LANES,),
        in_specs=[SMEM, block, block],
        out_specs=[pl.BlockSpec((width, LANES), lambda i: (0, i))] * members,
        out_shape=[out] * members,
        scratch_shapes=[pltpu.VMEM((observers, LANES), jnp.int32)],
        compiler_params=params(56),
        cost_estimate=cost(panels * observers, 10 * panels * observers),
    )(me, amplitude, delay_bin)


def coded(mask, visc):
    return jnp.where(mask != 0, visc, 0.0)


def rows_kernel(f_top, m_top, v_top, f_end, m_end, v_end, first_ref, last_ref):
    first_ref[:STEPS] = f_top[:STEPS]
    first_ref[STEPS:] = coded(m_top[:STEPS], v_top[:STEPS])
    last_ref[:STEPS] = f_end[8 - STEPS :]
    last_ref[STEPS:] = coded(m_end[8 - STEPS :], v_end[8 - STEPS :])


def columns_kernel(
    cell_ref, field_ref, mask_ref, visc_ref, before_ref, after_ref, first_ref, last_ref, place_ref, tall
):
    rows, cols = field_ref.shape
    cell = cell_ref[...]
    row = lax.div(cell, cols)
    col = cell - row * cols
    panel = lax.broadcasted_iota(jnp.int32, cell.shape, 1)
    place_ref[0:1] = col // LANES
    place_ref[1:2] = row // 8 * 8 + PAD
    place_ref[2:3] = row & 7
    place_ref[3:4] = (panel - col) & (LANES - 1)
    tall[...] = jnp.zeros_like(tall)
    for part in range(2):
        halo = slice(part * STEPS, (part + 1) * STEPS)
        for start, low, out in ((0, 0, first_ref), (cols - LANES, LANES - STEPS, last_ref)):
            lanes = slice(start, start + LANES)
            if part:
                tall[:rows] = coded(mask_ref[:, lanes], visc_ref[:, lanes])
            else:
                tall[:rows] = field_ref[:, lanes]
            tall[rows : rows + STEPS] = after_ref[halo, lanes]
            tall[rows + STEPS : rows + EDGE] = before_ref[halo, lanes]
            out[halo] = jnp.transpose(tall[...])[low : low + STEPS]


def step_kernel(
    cell_ref,
    field_ref,
    mask_ref,
    visc_ref,
    before_ref,
    after_ref,
    south_ref,
    north_ref,
    end_ref,
    sample_ref,
    fields,
    visc,
    wide,
    last,
    sem,
):
    rows, cols = field_ref.shape
    panels = sample_ref.shape[1]
    tiles, height, _ = visc.shape
    wide[...] = jnp.zeros_like(wide)
    for part, buf in enumerate((fields.at[0], visc)):
        halo = slice(part * STEPS, (part + 1) * STEPS)
        wide[:STEPS] = north_ref[halo]
        wide[LANES - STEPS :] = south_ref[halo]
        side = jnp.transpose(wide[...])
        for k in range(tiles):
            at = slice(k * LANES, (k + 1) * LANES)
            buf[k, :PAD] = jnp.zeros((PAD, LANES), F32)
            buf[k, PAD + rows :] = jnp.zeros((height - PAD - rows, LANES), F32)
            if k == tiles - 1:
                inside, before, after = (
                    side[:rows],
                    side[rows + STEPS : rows + EDGE],
                    side[rows : rows + STEPS],
                )
            else:
                inside = coded(mask_ref[:, at], visc_ref[:, at]) if part else field_ref[:, at]
                before, after = before_ref[halo, at], after_ref[halo, at]
            buf[k, PAD : PAD + rows] = inside
            buf[k, PAD - STEPS : PAD] = before
            buf[k, PAD + rows : PAD + rows + STEPS] = after

    first_lane = lax.broadcasted_iota(jnp.int32, (STRIP, LANES), 1) == 0
    last_lane = lax.broadcasted_iota(jnp.int32, (STRIP, LANES), 1) == LANES - 1
    for step in range(STEPS):
        old, new = fields.at[step], fields.at[step + 1]
        for k in range(tiles):
            new[k, :8] = jnp.zeros((8, LANES), F32)
            new[k, height - 8 :] = jnp.zeros((8, LANES), F32)

        def one_strip(i, carry):
            top = pl.multiple_of(i * STRIP, 8)
            centers = [old[k, pl.ds(top + 8, STRIP), :] for k in range(tiles)]
            right = [pltpu.roll(x, 1, 1) for x in centers]
            left = [pltpu.roll(x, LANES - 1, 1) for x in centers]
            for k in range(tiles):
                window = old[k, pl.ds(top, STRIP + 16), :]
                base = visc[k, pl.ds(top + 8, STRIP), :]
                center = centers[k]
                west = pltpu.roll(window, 1, 0)[8 : 8 + STRIP]
                east = pltpu.roll(window, STRIP + 15, 0)[8 : 8 + STRIP]
                south = jnp.where(first_lane, right[k - 1], right[k])
                north = jnp.where(last_lane, left[(k + 1) % tiles], left[k])
                diff_x = east - west
                diff_y = north - south
                square = diff_x * diff_x + diff_y * diff_y
                norm = square * lax.rsqrt(jnp.maximum(square, 1e-37))
                viscosity = base + 0.05 * norm / (2.0 + norm)
                around = (east + west) + (north + south)
                update = 0.75 * center + 0.15 * west + 0.1 * south
                update = update + viscosity * (around - 4.0 * center)
                new[k, pl.ds(top + 8, STRIP), :] = jnp.where(base > 0.0, update, 0.0)
            return carry

        strips = (height - 16) // STRIP
        lax.fori_loop(0, strips, one_strip, 0, unroll=strips)
    for k in range(tiles - 1):
        last[:, k * LANES : (k + 1) * LANES] = fields[STEPS, k, PAD : PAD + rows, :]
    leave = pltpu.make_async_copy(last, end_ref, sem)
    leave.start()

    lane = lax.broadcasted_iota(jnp.int32, (8, LANES), 1)
    line = lax.broadcasted_iota(jnp.int32, (8, LANES), 0)
    for base in range(0, panels, LANES):

        def one_panel(k, found):
            tile, top, row, turn = [cell_ref[c, base + k] for c in range(4)]
            top = pl.multiple_of(top, 8)
            here = (lane == k) & (line == row)
            return tuple(
                jnp.where(
                    here, pltpu.roll(fields[t + 1, tile, pl.ds(top, 8), :], turn, 1), found[t]
                )
                for t in range(STEPS)
            )

        none = (jnp.zeros((8, LANES), F32),) * STEPS
        found = lax.fori_loop(0, LANES, one_panel, none, unroll=32)
        for t in range(STEPS):
            sample_ref[t : t + 1, base : base + LANES] = jnp.sum(found[t], axis=0, keepdims=True)
    leave.wait()


def edges(field, mask, visc):
    rows, cols = field.shape
    edge_rows = jax.ShapeDtypeStruct((EDGE, cols), F32)
    return pl.pallas_call(
        rows_kernel,
        grid=(1,),
        in_specs=[pl.BlockSpec((8, cols), lambda i: (0, 0))] * 3
        + [pl.BlockSpec((8, cols), lambda i: (rows // 8 - 1, 0))] * 3,
        out_specs=[pl.BlockSpec((EDGE, cols), lambda i: (0, 0))] * 2,
        out_shape=[edge_rows, edge_rows],
        compiler_params=params(56),
        cost_estimate=cost(16 * cols, 256 * cols),
    )(field, mask, visc, field, mask, visc)


def shifted(axis, first, last):
    peers = lax.axis_size(axis)
    up = [(i, i + 1) for i in range(peers - 1)]
    down = [(i + 1, i) for i in range(peers - 1)]
    return lax.ppermute(last, axis, up), lax.ppermute(first, axis, down)


def field_window(field, mask, visc, before, after, panel_cell):
    rows, cols = field.shape
    tall = -(-(rows + EDGE) // LANES) * LANES
    edge_cols = jax.ShapeDtypeStruct((EDGE, tall), F32)

    panels = panel_cell.shape[0]
    first, last, places = pl.pallas_call(
        columns_kernel,
        in_specs=[VMEM] * 6,
        out_specs=[VMEM] * 3,
        out_shape=[edge_cols, edge_cols, jax.ShapeDtypeStruct((4, panels), jnp.int32)],
        scratch_shapes=[pltpu.VMEM((tall, LANES), F32)],
        compiler_params=params(16),
        cost_estimate=cost(rows * cols, 4 * rows * cols),
    )(panel_cell.reshape(1, panels), field, mask, visc, before, after)
    south, north = shifted("panel", first, last)
    tiles = cols // LANES + 1
    height = 16 + -(-(rows + 2 * PAD - 16) // STRIP) * STRIP
    return pl.pallas_call(
        step_kernel,
        in_specs=[SMEM] + [VMEM] * 7,
        out_specs=[pl.BlockSpec(memory_space=pl.ANY), VMEM],
        out_shape=[
            jax.ShapeDtypeStruct((rows, cols), F32),
            jax.ShapeDtypeStruct((STEPS, panels), F32),
        ],
        scratch_shapes=[
            pltpu.VMEM((STEPS + 1, tiles, height, LANES), F32),
            pltpu.VMEM((tiles, height, LANES), F32),
            pltpu.VMEM((LANES, tall), F32),
            pltpu.VMEM((rows, cols), F32),
            pltpu.SemaphoreType.DMA,
        ],
        compiler_params=params(24),
        cost_estimate=cost(100 * rows * cols, 800 * rows * cols),
    )(places, field, mask, visc, before, after, south, north)


def bin_kernel(half_ref, *refs):
    members = (len(refs) - 7) // 2
    words, samples = refs[:members], refs[members : 2 * members]
    keep_ref, send_ref, low_s, high_s, weight_s, acc_s, sig_s = refs[2 * members :]
    block, local = words[0].shape
    parts = local // LANES
    high = NB // LOW
    per_row = LANES // LOW
    half_rows = NB // LANES // 8
    low_tiles = LOW // 8 + 1
    depth = 2 * LANES
    shift = LOW.bit_length() - 1
    for s in range(members):
        for j in range(parts):
            word = words[s][:, j * LANES : (j + 1) * LANES]
            at = slice((s * parts + j) * LANES, (s * parts + j + 1) * LANES)
            low_s[:, at] = (word & (LOW - 1)).astype(F32)
            high_s[:, at] = ((word >> shift) & (high - 1)).astype(F32)
            amp = (word >> 16).astype(F32) * (1.0 / AMP_SCALE)
            for t in range(STEPS):
                weight_s[t, :, at] = amp * samples[s][j, t : t + 1, :]

    one = jnp.ones((), BF16)
    zero = jnp.zeros((), BF16)
    sub = lax.broadcasted_iota(jnp.int32, (16, depth), 0) & 7

    def number(x):
        return x.astype(F32).astype(BF16)

    high_ids = [
        number(per_row * (8 * (k % half_rows) + sub) + k // half_rows) for k in range(high // 8)
    ]
    low_ids = [[number(8 * k + sub - t) for t in range(STEPS)] for k in range(low_tiles)]
    lane = lax.broadcasted_iota(jnp.int32, (8, LANES), 1)
    lanes = lax.broadcasted_iota(jnp.int32, (NB // LANES, LANES), 1)
    acc_s[...] = jnp.zeros_like(acc_s)

    def two_observers(o, u):
        def spread(ref, *lead):
            rows = [
                jnp.broadcast_to(ref[(*lead, slice(o + e, o + e + 1), at)], (8, depth))
                for e in range(2)
            ]
            return jnp.concatenate(rows).astype(BF16)

        acc = None
        for c in range(members * local // depth):
            at = slice(c * depth, (c + 1) * depth)
            low_row, high_row = spread(low_s), spread(high_s)
            weights = [spread(weight_s, t) for t in range(STEPS)]
            left = jnp.concatenate([jnp.where(ids == high_row, one, zero) for ids in high_ids])
            right = []
            for k in range(low_tiles):
                placed = zero
                for t in range(1 if k * 8 >= LOW else 0, STEPS):
                    placed = jnp.where(low_ids[k][t] == low_row, weights[t], placed)
                right.append(placed)
            term = lax.dot_general(
                left, jnp.concatenate(right), (((1,), (1,)), ((), ())), preferred_element_type=F32
            )
            acc = term if acc is None else acc + term
        acc_s[u, :, : 16 * low_tiles] = acc
        for e in range(2):
            total = None
            for j in range(per_row):
                low = (lane - LOW * j) & (LANES - 1)
                source = jnp.where(low < 8 * low_tiles, 16 * (low // 8) + 8 * e + (low & 7), LANES - 1)
                tops = [16 * (j * half_rows + g) + 8 * e for g in range(half_rows)]
                x = jnp.concatenate(
                    [jnp.take_along_axis(acc_s[u, top : top + 8], source, axis=1) for top in tops]
                )
                if j == per_row - 1:
                    x = jnp.where(lanes < LOW, pltpu.roll(x, 1, 0), x)
                total = x if total is None else total + x
            sig_s[:, o + e : o + e + 1, :] = total[:, None, :]

    for u in range(block // 2):
        two_observers(2 * u, u)
    tiles = NB // LANES // 2
    per_owner = tiles // keep_ref.shape[0]
    for r in range(tiles):
        lanes = slice(r % per_owner * LANES, (r % per_owner + 1) * LANES)
        keep_ref[r // per_owner, :, lanes] = sig_s[half_ref[0] * tiles + r]
        sent = sig_s[(1 - half_ref[0]) * tiles + r]
        send_ref[r // per_owner, :, lanes] = sent.astype(BF16)


def binned(half, words, samples, first, count):
    members = len(words)
    local = words[0].shape[1]
    block = 16
    panels = members * local
    bins = NB // 2 // members
    out = pl.BlockSpec((members, block, bins), lambda i: (0, i, 0))
    return pl.pallas_call(
        bin_kernel,
        grid=(count // block,),
        in_specs=[SMEM]
        + [pl.BlockSpec((block, local), lambda i: (first // block + i, 0))] * members
        + [pl.BlockSpec(samples[0].shape, lambda i: (0, 0, 0))] * members,
        out_specs=[out, out],
        out_shape=[
            jax.ShapeDtypeStruct((members, count, bins), F32),
            jax.ShapeDtypeStruct((members, count, bins), BF16),
        ],
        scratch_shapes=[
            pltpu.VMEM((block, panels), F32),
            pltpu.VMEM((block, panels), F32),
            pltpu.VMEM((STEPS, block, panels), F32),
            pltpu.VMEM((block // 2, 2 * NB // LOW, LANES), F32),
            pltpu.VMEM((NB // LANES, block, LANES), F32),
        ],
        compiler_params=params(40),
        cost_estimate=cost(65536 * count * panels, 8 * count * panels),
    )(half, *words, *samples)


def join_kernel(parts, me_ref, *refs):
    keeps, gots, outs = refs[:parts], refs[parts : 2 * parts], refs[2 * parts :]
    for k, out in enumerate(outs):
        owner = lax.rem(me_ref[0] + k, len(outs))
        at = 0
        for keep, got in zip(keeps, gots):
            count = keep.shape[1]
            out[at : at + count] = (keep[owner] + got[owner].astype(F32)).astype(BF16)
            at += count


def join(me, keeps, gots):
    members, _, bins = keeps[0].shape
    count = sum(keep.shape[1] for keep in keeps)
    return pl.pallas_call(
        functools.partial(join_kernel, len(keeps)),
        in_specs=[SMEM] + [VMEM] * (2 * len(keeps)),
        out_specs=[VMEM] * members,
        out_shape=[jax.ShapeDtypeStruct((count, bins), BF16)] * members,
        compiler_params=params(16),
        cost_estimate=cost(members * count * bins, 8 * members * count * bins),
    )(me, *keeps, *gots)


def place_kernel(first, width, me_ref, *refs):
    members, count, _ = refs[-2].shape
    pieces, (out_ref, wide, sems) = refs[:members], refs[-3:]
    copies = []
    for k, ref in enumerate(pieces):
        owner = lax.rem(me_ref[0] - k + members, members)
        start = pl.multiple_of(owner * width + first, 16)
        wide[k] = ref[...].astype(F32)
        copies.append(
            pltpu.make_async_copy(wide.at[k], out_ref.at[pl.ds(start, count), :], sems.at[k])
        )
        copies[-1].start()
    for copy in copies:
        copy.wait()


def place(me, pieces, signals, first, width):
    members = len(pieces)
    count, bins = pieces[0].shape
    before = [] if signals is None else [signals]
    return pl.pallas_call(
        functools.partial(place_kernel, first, width),
        in_specs=[SMEM] + [VMEM] * members + [pl.BlockSpec(memory_space=pl.ANY)] * len(before),
        out_specs=pl.BlockSpec(memory_space=pl.ANY),
        out_shape=jax.ShapeDtypeStruct((width * members, bins), F32),
        input_output_aliases={members + 1: 0} if before else {},
        scratch_shapes=[
            pltpu.VMEM((members, count, bins), F32),
            pltpu.SemaphoreType.DMA((members,)),
        ],
        compiler_params=params(16),
        cost_estimate=cost(members * count * bins, 6 * members * count * bins),
    )(me, *pieces, *before)


def on_device(field_start, fluid_mask, base_visc, panel_cell, amplitude, delay_bin):
    peers = lax.axis_size("box")
    members = peers // 2
    index = lax.axis_index("box").astype(jnp.int32).reshape(1)
    me, half = lax.rem(index, members), index // members

    def spread(parts, to):
        def perm(k):
            return [(i, i // members * members + to(i % members, k, members)) for i in range(peers)]

        return [lax.ppermute(x, "box", perm(k)) if k else x for k, x in enumerate(parts)]

    ends = edges(field_start, fluid_mask, base_visc)
    amplitude, delay_bin, *ends = lax.optimization_barrier((amplitude, delay_bin, *ends))
    before, after = shifted("box", *ends)
    packed = pack(me, amplitude, delay_bin, members)
    before, after, *packed = lax.optimization_barrier((before, after, *packed))
    words = spread(packed, target)
    field, sample = field_window(
        field_start, fluid_mask, base_visc, before, after, panel_cell
    )
    sample = lax.all_gather(sample, "panel")
    middle = members // 2
    sample, words[middle] = lax.optimization_barrier((sample, words[middle]))
    samples = spread([sample] * members, target)
    observers = words[0].shape[0]
    across = [(i, (i + members) % peers) for i in range(peers)]
    first, groups = 0, []
    for chunks in sizes(observers):
        groups.append([])
        for count in chunks:
            keep, send = binned(half, words, samples, first, count)
            keep, half = lax.optimization_barrier((keep, half))
            groups[-1].append((keep, lax.ppermute(send, "box", across)))
            first += count
    pieces, waiting = None, []
    for group in groups:
        keeps, gots = [x[0] for x in group], [x[1] for x in group]
        if pieces is not None:
            gots[-1], pieces[middle] = lax.optimization_barrier((gots[-1], pieces[middle]))
        pieces = spread(join(me, keeps, gots), lambda i, k, n: (i + k) % n)
        waiting.append(pieces)
    first, signals = 0, None
    for pieces in waiting:
        signals = place(me, pieces, signals, first, observers)
        first += pieces[0].shape[0]
    return (field, signals)


def sizes(observers):
    units = observers // 16
    ends = [-(-units * part // 16) * 16 for part in PARTS]
    counts = [end - start for start, end in zip([0] + ends, ends)]
    return [[c for c in group if c] for group in (counts[:2], counts[2:]) if any(group)]


def solution(mesh):
    placed = (
        P("box", "panel"),
        P("box", "panel"),
        P("box", "panel"),
        P(("box", "panel")),
        P("box", "panel"),
        P("box", "panel"),
    )
    return jax.shard_map(
        on_device,
        mesh=mesh,
        in_specs=placed,
        out_specs=(P("box", "panel"), P("panel", "box")),
        check_vma=False,
    )
```

```python
import functools

import jax
import jax.numpy as jnp
from jax import lax
from jax.experimental import pallas as pl
from jax.experimental.pallas import tpu as pltpu
from jax.sharding import PartitionSpec as P

F32 = jnp.float32
BF16 = jnp.bfloat16
STEPS = 4
NB = 2048
LOW = 32
LANES = 128
EDGE = 2 * STEPS
PAD = 16
STRIP = 32
AMP_SCALE = 4096.0
PARTS = (7, 12, 16)
VMEM = pl.BlockSpec(memory_space=pltpu.VMEM)
SMEM = pl.BlockSpec(memory_space=pltpu.SMEM)


def params(mib):
    return pltpu.CompilerParams(vmem_limit_bytes=mib << 20)


def cost(flops, size):
    return pl.CostEstimate(flops=flops, bytes_accessed=size, transcendentals=0)


def target(me, k, members):
    return me ^ k if members & (members - 1) == 0 else (me + k) % members


def pack_kernel(me_ref, amp_ref, bin_ref, *refs):
    outs, turned = refs[:-1], refs[-1]
    scaled = (amp_ref[...].astype(F32) * AMP_SCALE).astype(jnp.int32)
    turned[...] = jnp.transpose((scaled << 16) | bin_ref[...])
    width = outs[0].shape[0]
    for k, out in enumerate(outs):
        first = pl.multiple_of(target(me_ref[0], k, len(outs)) * width, 8)
        out[...] = turned[pl.ds(first, width), :]


def pack(me, amplitude, delay_bin, members):
    panels, observers = amplitude.shape
    width = observers // members
    block = pl.BlockSpec((LANES, observers), lambda i: (i, 0))
    out = jax.ShapeDtypeStruct((width, panels), jnp.int32)
    return pl.pallas_call(
        pack_kernel,
        grid=(panels // LANES,),
        in_specs=[SMEM, block, block],
        out_specs=[pl.BlockSpec((width, LANES), lambda i: (0, i))] * members,
        out_shape=[out] * members,
        scratch_shapes=[pltpu.VMEM((observers, LANES), jnp.int32)],
        compiler_params=params(56),
        cost_estimate=cost(panels * observers, 10 * panels * observers),
    )(me, amplitude, delay_bin)


def coded(mask, visc):
    return jnp.where(mask != 0, visc, 0.0)


def rows_kernel(f_top, m_top, v_top, f_end, m_end, v_end, first_ref, last_ref):
    first_ref[:STEPS] = f_top[:STEPS]
    first_ref[STEPS:] = coded(m_top[:STEPS], v_top[:STEPS])
    last_ref[:STEPS] = f_end[8 - STEPS :]
    last_ref[STEPS:] = coded(m_end[8 - STEPS :], v_end[8 - STEPS :])


def columns_kernel(
    cell_ref, field_ref, mask_ref, visc_ref, before_ref, after_ref, first_ref, last_ref, place_ref, tall
):
    rows, cols = field_ref.shape
    cell = cell_ref[...]
    row = lax.div(cell, cols)
    col = cell - row * cols
    panel = lax.broadcasted_iota(jnp.int32, cell.shape, 1)
    place_ref[0:1] = col // LANES
    place_ref[1:2] = row // 8 * 8 + PAD
    place_ref[2:3] = row & 7
    place_ref[3:4] = (panel - col) & (LANES - 1)
    tall[...] = jnp.zeros_like(tall)
    for part in range(2):
        halo = slice(part * STEPS, (part + 1) * STEPS)
        for start, low, out in ((0, 0, first_ref), (cols - LANES, LANES - STEPS, last_ref)):
            lanes = slice(start, start + LANES)
            if part:
                tall[:rows] = coded(mask_ref[:, lanes], visc_ref[:, lanes])
            else:
                tall[:rows] = field_ref[:, lanes]
            tall[rows : rows + STEPS] = after_ref[halo, lanes]
            tall[rows + STEPS : rows + EDGE] = before_ref[halo, lanes]
            out[halo] = jnp.transpose(tall[...])[low : low + STEPS]


def step_kernel(
    cell_ref,
    field_ref,
    mask_ref,
    visc_ref,
    before_ref,
    after_ref,
    south_ref,
    north_ref,
    end_ref,
    sample_ref,
    fields,
    visc,
    wide,
    last,
    sem,
):
    rows, cols = field_ref.shape
    panels = sample_ref.shape[1]
    tiles, height, _ = visc.shape
    wide[...] = jnp.zeros_like(wide)
    for part, buf in enumerate((fields.at[0], visc)):
        halo = slice(part * STEPS, (part + 1) * STEPS)
        wide[:STEPS] = north_ref[halo]
        wide[LANES - STEPS :] = south_ref[halo]
        side = jnp.transpose(wide[...])
        for k in range(tiles):
            at = slice(k * LANES, (k + 1) * LANES)
            buf[k, :PAD] = jnp.zeros((PAD, LANES), F32)
            buf[k, PAD + rows :] = jnp.zeros((height - PAD - rows, LANES), F32)
            if k == tiles - 1:
                inside, before, after = (
                    side[:rows],
                    side[rows + STEPS : rows + EDGE],
                    side[rows : rows + STEPS],
                )
            else:
                inside = coded(mask_ref[:, at], visc_ref[:, at]) if part else field_ref[:, at]
                before, after = before_ref[halo, at], after_ref[halo, at]
            buf[k, PAD : PAD + rows] = inside
            buf[k, PAD - STEPS : PAD] = before
            buf[k, PAD + rows : PAD + rows + STEPS] = after

    first_lane = lax.broadcasted_iota(jnp.int32, (STRIP, LANES), 1) == 0
    last_lane = lax.broadcasted_iota(jnp.int32, (STRIP, LANES), 1) == LANES - 1
    for step in range(STEPS):
        old, new = fields.at[step], fields.at[step + 1]
        for k in range(tiles):
            new[k, :8] = jnp.zeros((8, LANES), F32)
            new[k, height - 8 :] = jnp.zeros((8, LANES), F32)

        def one_strip(i, carry):
            top = pl.multiple_of(i * STRIP, 8)
            centers = [old[k, pl.ds(top + 8, STRIP), :] for k in range(tiles)]
            right = [pltpu.roll(x, 1, 1) for x in centers]
            left = [pltpu.roll(x, LANES - 1, 1) for x in centers]
            for k in range(tiles):
                window = old[k, pl.ds(top, STRIP + 16), :]
                base = visc[k, pl.ds(top + 8, STRIP), :]
                center = centers[k]
                west = pltpu.roll(window, 1, 0)[8 : 8 + STRIP]
                east = pltpu.roll(window, STRIP + 15, 0)[8 : 8 + STRIP]
                south = jnp.where(first_lane, right[k - 1], right[k])
                north = jnp.where(last_lane, left[(k + 1) % tiles], left[k])
                diff_x = east - west
                diff_y = north - south
                square = diff_x * diff_x + diff_y * diff_y
                norm = square * lax.rsqrt(jnp.maximum(square, 1e-37))
                viscosity = base + 0.05 * norm / (2.0 + norm)
                around = (east + west) + (north + south)
                update = 0.75 * center + 0.15 * west + 0.1 * south
                update = update + viscosity * (around - 4.0 * center)
                new[k, pl.ds(top + 8, STRIP), :] = jnp.where(base > 0.0, update, 0.0)
            return carry

        strips = (height - 16) // STRIP
        lax.fori_loop(0, strips, one_strip, 0, unroll=strips)
    for k in range(tiles - 1):
        last[:, k * LANES : (k + 1) * LANES] = fields[STEPS, k, PAD : PAD + rows, :]
    leave = pltpu.make_async_copy(last, end_ref, sem)
    leave.start()

    lane = lax.broadcasted_iota(jnp.int32, (8, LANES), 1)
    line = lax.broadcasted_iota(jnp.int32, (8, LANES), 0)
    for base in range(0, panels, LANES):

        def one_panel(k, found):
            tile, top, row, turn = [cell_ref[c, base + k] for c in range(4)]
            top = pl.multiple_of(top, 8)
            here = (lane == k) & (line == row)
            return tuple(
                jnp.where(
                    here, pltpu.roll(fields[t + 1, tile, pl.ds(top, 8), :], turn, 1), found[t]
                )
                for t in range(STEPS)
            )

        none = (jnp.zeros((8, LANES), F32),) * STEPS
        found = lax.fori_loop(0, LANES, one_panel, none, unroll=32)
        for t in range(STEPS):
            sample_ref[t : t + 1, base : base + LANES] = jnp.sum(found[t], axis=0, keepdims=True)
    leave.wait()


def edges(field, mask, visc):
    rows, cols = field.shape
    edge_rows = jax.ShapeDtypeStruct((EDGE, cols), F32)
    return pl.pallas_call(
        rows_kernel,
        grid=(1,),
        in_specs=[pl.BlockSpec((8, cols), lambda i: (0, 0))] * 3
        + [pl.BlockSpec((8, cols), lambda i: (rows // 8 - 1, 0))] * 3,
        out_specs=[pl.BlockSpec((EDGE, cols), lambda i: (0, 0))] * 2,
        out_shape=[edge_rows, edge_rows],
        compiler_params=params(56),
        cost_estimate=cost(16 * cols, 256 * cols),
    )(field, mask, visc, field, mask, visc)


def shifted(axis, first, last):
    peers = lax.axis_size(axis)
    up = [(i, i + 1) for i in range(peers - 1)]
    down = [(i + 1, i) for i in range(peers - 1)]
    return lax.ppermute(last, axis, up), lax.ppermute(first, axis, down)


def field_window(field, mask, visc, before, after, panel_cell):
    rows, cols = field.shape
    tall = -(-(rows + EDGE) // LANES) * LANES
    edge_cols = jax.ShapeDtypeStruct((EDGE, tall), F32)

    panels = panel_cell.shape[0]
    first, last, places = pl.pallas_call(
        columns_kernel,
        in_specs=[VMEM] * 6,
        out_specs=[VMEM] * 3,
        out_shape=[edge_cols, edge_cols, jax.ShapeDtypeStruct((4, panels), jnp.int32)],
        scratch_shapes=[pltpu.VMEM((tall, LANES), F32)],
        compiler_params=params(16),
        cost_estimate=cost(rows * cols, 4 * rows * cols),
    )(panel_cell.reshape(1, panels), field, mask, visc, before, after)
    south, north = shifted("panel", first, last)
    tiles = cols // LANES + 1
    height = 16 + -(-(rows + 2 * PAD - 16) // STRIP) * STRIP
    return pl.pallas_call(
        step_kernel,
        in_specs=[SMEM] + [VMEM] * 7,
        out_specs=[pl.BlockSpec(memory_space=pl.ANY), VMEM],
        out_shape=[
            jax.ShapeDtypeStruct((rows, cols), F32),
            jax.ShapeDtypeStruct((STEPS, panels), F32),
        ],
        scratch_shapes=[
            pltpu.VMEM((STEPS + 1, tiles, height, LANES), F32),
            pltpu.VMEM((tiles, height, LANES), F32),
            pltpu.VMEM((LANES, tall), F32),
            pltpu.VMEM((rows, cols), F32),
            pltpu.SemaphoreType.DMA,
        ],
        compiler_params=params(24),
        cost_estimate=cost(100 * rows * cols, 800 * rows * cols),
    )(places, field, mask, visc, before, after, south, north)


def bin_kernel(half_ref, *refs):
    members = (len(refs) - 7) // 2
    words, samples = refs[:members], refs[members : 2 * members]
    keep_ref, send_ref, low_s, high_s, weight_s, acc_s, sig_s = refs[2 * members :]
    block, local = words[0].shape
    parts = local // LANES
    high = NB // LOW
    per_row = LANES // LOW
    half_rows = NB // LANES // 8
    low_tiles = LOW // 8 + 1
    depth = 2 * LANES
    shift = LOW.bit_length() - 1
    for s in range(members):
        for j in range(parts):
            word = words[s][:, j * LANES : (j + 1) * LANES]
            at = slice((s * parts + j) * LANES, (s * parts + j + 1) * LANES)
            low_s[:, at] = (word & (LOW - 1)).astype(F32)
            high_s[:, at] = ((word >> shift) & (high - 1)).astype(F32)
            amp = (word >> 16).astype(F32) * (1.0 / AMP_SCALE)
            for t in range(STEPS):
                weight_s[t, :, at] = amp * samples[s][j, t : t + 1, :]

    one = jnp.ones((), BF16)
    zero = jnp.zeros((), BF16)
    sub = lax.broadcasted_iota(jnp.int32, (16, depth), 0) & 7

    def number(x):
        return x.astype(F32).astype(BF16)

    high_ids = [
        number(per_row * (8 * (k % half_rows) + sub) + k // half_rows) for k in range(high // 8)
    ]
    low_ids = [[number(8 * k + sub - t) for t in range(STEPS)] for k in range(low_tiles)]
    lane = lax.broadcasted_iota(jnp.int32, (8, LANES), 1)
    lanes = lax.broadcasted_iota(jnp.int32, (NB // LANES, LANES), 1)
    acc_s[...] = jnp.zeros_like(acc_s)

    def two_observers(o, u):
        def spread(ref, *lead):
            rows = [
                jnp.broadcast_to(ref[(*lead, slice(o + e, o + e + 1), at)], (8, depth))
                for e in range(2)
            ]
            return jnp.concatenate(rows).astype(BF16)

        acc = None
        for c in range(members * local // depth):
            at = slice(c * depth, (c + 1) * depth)
            low_row, high_row = spread(low_s), spread(high_s)
            weights = [spread(weight_s, t) for t in range(STEPS)]
            left = jnp.concatenate([jnp.where(ids == high_row, one, zero) for ids in high_ids])
            right = []
            for k in range(low_tiles):
                placed = zero
                for t in range(1 if k * 8 >= LOW else 0, STEPS):
                    placed = jnp.where(low_ids[k][t] == low_row, weights[t], placed)
                right.append(placed)
            term = lax.dot_general(
                left, jnp.concatenate(right), (((1,), (1,)), ((), ())), preferred_element_type=F32
            )
            acc = term if acc is None else acc + term
        acc_s[u, :, : 16 * low_tiles] = acc
        for e in range(2):
            total = None
            for j in range(per_row):
                low = (lane - LOW * j) & (LANES - 1)
                source = jnp.where(low < 8 * low_tiles, 16 * (low // 8) + 8 * e + (low & 7), LANES - 1)
                tops = [16 * (j * half_rows + g) + 8 * e for g in range(half_rows)]
                x = jnp.concatenate(
                    [jnp.take_along_axis(acc_s[u, top : top + 8], source, axis=1) for top in tops]
                )
                if j == per_row - 1:
                    x = jnp.where(lanes < LOW, pltpu.roll(x, 1, 0), x)
                total = x if total is None else total + x
            sig_s[:, o + e : o + e + 1, :] = total[:, None, :]

    for u in range(block // 2):
        two_observers(2 * u, u)
    tiles = NB // LANES // 2
    per_owner = tiles // keep_ref.shape[0]
    for r in range(tiles):
        lanes = slice(r % per_owner * LANES, (r % per_owner + 1) * LANES)
        keep_ref[r // per_owner, :, lanes] = sig_s[half_ref[0] * tiles + r]
        sent = sig_s[(1 - half_ref[0]) * tiles + r]
        send_ref[r // per_owner, :, lanes] = sent.astype(BF16)


def binned(half, words, samples, first, count):
    members = len(words)
    local = words[0].shape[1]
    block = 16
    panels = members * local
    bins = NB // 2 // members
    out = pl.BlockSpec((members, block, bins), lambda i: (0, i, 0))
    return pl.pallas_call(
        bin_kernel,
        grid=(count // block,),
        in_specs=[SMEM]
        + [pl.BlockSpec((block, local), lambda i: (first // block + i, 0))] * members
        + [pl.BlockSpec(samples[0].shape, lambda i: (0, 0, 0))] * members,
        out_specs=[out, out],
        out_shape=[
            jax.ShapeDtypeStruct((members, count, bins), F32),
            jax.ShapeDtypeStruct((members, count, bins), BF16),
        ],
        scratch_shapes=[
            pltpu.VMEM((block, panels), F32),
            pltpu.VMEM((block, panels), F32),
            pltpu.VMEM((STEPS, block, panels), F32),
            pltpu.VMEM((block // 2, 2 * NB // LOW, LANES), F32),
            pltpu.VMEM((NB // LANES, block, LANES), F32),
        ],
        compiler_params=params(40),
        cost_estimate=cost(65536 * count * panels, 8 * count * panels),
    )(half, *words, *samples)


def join_kernel(parts, me_ref, *refs):
    keeps, gots, outs = refs[:parts], refs[parts : 2 * parts], refs[2 * parts :]
    for k, out in enumerate(outs):
        owner = lax.rem(me_ref[0] + k, len(outs))
        at = 0
        for keep, got in zip(keeps, gots):
            count = keep.shape[1]
            out[at : at + count] = (keep[owner] + got[owner].astype(F32)).astype(BF16)
            at += count


def join(me, keeps, gots):
    members, _, bins = keeps[0].shape
    count = sum(keep.shape[1] for keep in keeps)
    return pl.pallas_call(
        functools.partial(join_kernel, len(keeps)),
        in_specs=[SMEM] + [VMEM] * (2 * len(keeps)),
        out_specs=[VMEM] * members,
        out_shape=[jax.ShapeDtypeStruct((count, bins), BF16)] * members,
        compiler_params=params(16),
        cost_estimate=cost(members * count * bins, 8 * members * count * bins),
    )(me, *keeps, *gots)


def place_kernel(first, width, me_ref, *refs):
    members, count, _ = refs[-2].shape
    pieces, (out_ref, wide, sems) = refs[:members], refs[-3:]
    copies = []
    for k, ref in enumerate(pieces):
        owner = lax.rem(me_ref[0] - k + members, members)
        start = pl.multiple_of(owner * width + first, 16)
        wide[k] = ref[...].astype(F32)
        copies.append(
            pltpu.make_async_copy(wide.at[k], out_ref.at[pl.ds(start, count), :], sems.at[k])
        )
        copies[-1].start()
    for copy in copies:
        copy.wait()


def place(me, pieces, signals, first, width):
    members = len(pieces)
    count, bins = pieces[0].shape
    before = [] if signals is None else [signals]
    return pl.pallas_call(
        functools.partial(place_kernel, first, width),
        in_specs=[SMEM] + [VMEM] * members + [pl.BlockSpec(memory_space=pl.ANY)] * len(before),
        out_specs=pl.BlockSpec(memory_space=pl.ANY),
        out_shape=jax.ShapeDtypeStruct((width * members, bins), F32),
        input_output_aliases={members + 1: 0} if before else {},
        scratch_shapes=[
            pltpu.VMEM((members, count, bins), F32),
            pltpu.SemaphoreType.DMA((members,)),
        ],
        compiler_params=params(16),
        cost_estimate=cost(members * count * bins, 6 * members * count * bins),
    )(me, *pieces, *before)


def on_device(field_start, fluid_mask, base_visc, panel_cell, amplitude, delay_bin):
    peers = lax.axis_size("box")
    members = peers // 2
    index = lax.axis_index("box").astype(jnp.int32).reshape(1)
    me, half = lax.rem(index, members), index // members

    def spread(parts, to):
        def perm(k):
            return [(i, i // members * members + to(i % members, k, members)) for i in range(peers)]

        return [lax.ppermute(x, "box", perm(k)) if k else x for k, x in enumerate(parts)]

    ends = edges(field_start, fluid_mask, base_visc)
    amplitude, delay_bin, *ends = lax.optimization_barrier((amplitude, delay_bin, *ends))
    before, after = shifted("box", *ends)
    packed = pack(me, amplitude, delay_bin, members)
    before, after, *packed = lax.optimization_barrier((before, after, *packed))
    words = spread(packed, target)
    field, sample = field_window(
        field_start, fluid_mask, base_visc, before, after, panel_cell
    )
    sample = lax.all_gather(sample, "panel")
    middle = members // 2
    sample, words[middle] = lax.optimization_barrier((sample, words[middle]))
    samples = spread([sample] * members, target)
    observers = words[0].shape[0]
    across = [(i, (i + members) % peers) for i in range(peers)]
    first, groups = 0, []
    for chunks in sizes(observers):
        groups.append([])
        for count in chunks:
            keep, send = binned(half, words, samples, first, count)
            keep, half = lax.optimization_barrier((keep, half))
            groups[-1].append((keep, lax.ppermute(send, "box", across)))
            first += count
    pieces, waiting = None, []
    for group in groups:
        keeps, gots = [x[0] for x in group], [x[1] for x in group]
        if pieces is not None:
            gots[-1], pieces[middle] = lax.optimization_barrier((gots[-1], pieces[middle]))
        pieces = spread(join(me, keeps, gots), lambda i, k, n: (i + k) % n)
        waiting.append(pieces)
    first, signals = 0, None
    for pieces in waiting:
        signals = place(me, pieces, signals, first, observers)
        first += pieces[0].shape[0]
    return (field, signals)


def sizes(observers):
    units = observers // 16
    ends = [-(-units * part // 16) * 16 for part in PARTS]
    counts = [end - start for start, end in zip([0] + ends, ends)]
    return [[c for c in counts if c]]


def solution(mesh):
    placed = (
        P("box", "panel"),
        P("box", "panel"),
        P("box", "panel"),
        P(("box", "panel")),
        P("box", "panel"),
        P("box", "panel"),
    )
    return jax.shard_map(
        on_device,
        mesh=mesh,
        in_specs=placed,
        out_specs=(P("box", "panel"), P("panel", "box")),
        check_vma=False,
    )
```

```python
import functools

import jax
import jax.numpy as jnp
from jax import lax
from jax.experimental import pallas as pl
from jax.experimental.pallas import tpu as pltpu
from jax.sharding import PartitionSpec as P

F32 = jnp.float32
BF16 = jnp.bfloat16
STEPS = 4
NB = 2048
LOW = 32
LANES = 128
EDGE = 2 * STEPS
PAD = 16
STRIP = 32
AMP_SCALE = 4096.0
PARTS = (8, 13, 16)
VMEM = pl.BlockSpec(memory_space=pltpu.VMEM)
SMEM = pl.BlockSpec(memory_space=pltpu.SMEM)


def params(mib):
    return pltpu.CompilerParams(vmem_limit_bytes=mib << 20)


def cost(flops, size):
    return pl.CostEstimate(flops=flops, bytes_accessed=size, transcendentals=0)


def target(me, k, members):
    return me ^ k if members & (members - 1) == 0 else (me + k) % members


def pack_kernel(me_ref, amp_ref, bin_ref, *refs):
    outs, turned = refs[:-1], refs[-1]
    scaled = (amp_ref[...].astype(F32) * AMP_SCALE).astype(jnp.int32)
    turned[...] = jnp.transpose((scaled << 16) | bin_ref[...])
    width = outs[0].shape[0]
    for k, out in enumerate(outs):
        first = pl.multiple_of(target(me_ref[0], k, len(outs)) * width, 8)
        out[...] = turned[pl.ds(first, width), :]


def pack(me, amplitude, delay_bin, members):
    panels, observers = amplitude.shape
    width = observers // members
    block = pl.BlockSpec((LANES, observers), lambda i: (i, 0))
    out = jax.ShapeDtypeStruct((width, panels), jnp.int32)
    return pl.pallas_call(
        pack_kernel,
        grid=(panels // LANES,),
        in_specs=[SMEM, block, block],
        out_specs=[pl.BlockSpec((width, LANES), lambda i: (0, i))] * members,
        out_shape=[out] * members,
        scratch_shapes=[pltpu.VMEM((observers, LANES), jnp.int32)],
        compiler_params=params(56),
        cost_estimate=cost(panels * observers, 10 * panels * observers),
    )(me, amplitude, delay_bin)


def coded(mask, visc):
    return jnp.where(mask != 0, visc, 0.0)


def rows_kernel(f_top, m_top, v_top, f_end, m_end, v_end, first_ref, last_ref):
    first_ref[:STEPS] = f_top[:STEPS]
    first_ref[STEPS:] = coded(m_top[:STEPS], v_top[:STEPS])
    last_ref[:STEPS] = f_end[8 - STEPS :]
    last_ref[STEPS:] = coded(m_end[8 - STEPS :], v_end[8 - STEPS :])


def columns_kernel(
    cell_ref, field_ref, mask_ref, visc_ref, before_ref, after_ref, first_ref, last_ref, place_ref, tall
):
    rows, cols = field_ref.shape
    cell = cell_ref[...]
    row = lax.div(cell, cols)
    col = cell - row * cols
    panel = lax.broadcasted_iota(jnp.int32, cell.shape, 1)
    place_ref[0:1] = col // LANES
    place_ref[1:2] = row // 8 * 8 + PAD
    place_ref[2:3] = row & 7
    place_ref[3:4] = (panel - col) & (LANES - 1)
    tall[...] = jnp.zeros_like(tall)
    for part in range(2):
        halo = slice(part * STEPS, (part + 1) * STEPS)
        for start, low, out in ((0, 0, first_ref), (cols - LANES, LANES - STEPS, last_ref)):
            lanes = slice(start, start + LANES)
            if part:
                tall[:rows] = coded(mask_ref[:, lanes], visc_ref[:, lanes])
            else:
                tall[:rows] = field_ref[:, lanes]
            tall[rows : rows + STEPS] = after_ref[halo, lanes]
            tall[rows + STEPS : rows + EDGE] = before_ref[halo, lanes]
            out[halo] = jnp.transpose(tall[...])[low : low + STEPS]


def step_kernel(
    cell_ref,
    field_ref,
    mask_ref,
    visc_ref,
    before_ref,
    after_ref,
    south_ref,
    north_ref,
    end_ref,
    sample_ref,
    fields,
    visc,
    wide,
    last,
    sem,
):
    rows, cols = field_ref.shape
    panels = sample_ref.shape[1]
    tiles, height, _ = visc.shape
    wide[...] = jnp.zeros_like(wide)
    for part, buf in enumerate((fields.at[0], visc)):
        halo = slice(part * STEPS, (part + 1) * STEPS)
        wide[:STEPS] = north_ref[halo]
        wide[LANES - STEPS :] = south_ref[halo]
        side = jnp.transpose(wide[...])
        for k in range(tiles):
            at = slice(k * LANES, (k + 1) * LANES)
            buf[k, :PAD] = jnp.zeros((PAD, LANES), F32)
            buf[k, PAD + rows :] = jnp.zeros((height - PAD - rows, LANES), F32)
            if k == tiles - 1:
                inside, before, after = (
                    side[:rows],
                    side[rows + STEPS : rows + EDGE],
                    side[rows : rows + STEPS],
                )
            else:
                inside = coded(mask_ref[:, at], visc_ref[:, at]) if part else field_ref[:, at]
                before, after = before_ref[halo, at], after_ref[halo, at]
            buf[k, PAD : PAD + rows] = inside
            buf[k, PAD - STEPS : PAD] = before
            buf[k, PAD + rows : PAD + rows + STEPS] = after

    first_lane = lax.broadcasted_iota(jnp.int32, (STRIP, LANES), 1) == 0
    last_lane = lax.broadcasted_iota(jnp.int32, (STRIP, LANES), 1) == LANES - 1
    for step in range(STEPS):
        old, new = fields.at[step], fields.at[step + 1]
        for k in range(tiles):
            new[k, :8] = jnp.zeros((8, LANES), F32)
            new[k, height - 8 :] = jnp.zeros((8, LANES), F32)

        def one_strip(i, carry):
            top = pl.multiple_of(i * STRIP, 8)
            centers = [old[k, pl.ds(top + 8, STRIP), :] for k in range(tiles)]
            right = [pltpu.roll(x, 1, 1) for x in centers]
            left = [pltpu.roll(x, LANES - 1, 1) for x in centers]
            for k in range(tiles):
                window = old[k, pl.ds(top, STRIP + 16), :]
                base = visc[k, pl.ds(top + 8, STRIP), :]
                center = centers[k]
                west = pltpu.roll(window, 1, 0)[8 : 8 + STRIP]
                east = pltpu.roll(window, STRIP + 15, 0)[8 : 8 + STRIP]
                south = jnp.where(first_lane, right[k - 1], right[k])
                north = jnp.where(last_lane, left[(k + 1) % tiles], left[k])
                diff_x = east - west
                diff_y = north - south
                square = diff_x * diff_x + diff_y * diff_y
                norm = square * lax.rsqrt(jnp.maximum(square, 1e-37))
                viscosity = base + 0.05 * norm / (2.0 + norm)
                around = (east + west) + (north + south)
                update = 0.75 * center + 0.15 * west + 0.1 * south
                update = update + viscosity * (around - 4.0 * center)
                new[k, pl.ds(top + 8, STRIP), :] = jnp.where(base > 0.0, update, 0.0)
            return carry

        strips = (height - 16) // STRIP
        lax.fori_loop(0, strips, one_strip, 0, unroll=strips)
    for k in range(tiles - 1):
        last[:, k * LANES : (k + 1) * LANES] = fields[STEPS, k, PAD : PAD + rows, :]
    leave = pltpu.make_async_copy(last, end_ref, sem)
    leave.start()

    lane = lax.broadcasted_iota(jnp.int32, (8, LANES), 1)
    line = lax.broadcasted_iota(jnp.int32, (8, LANES), 0)
    for base in range(0, panels, LANES):

        def one_panel(k, found):
            tile, top, row, turn = [cell_ref[c, base + k] for c in range(4)]
            top = pl.multiple_of(top, 8)
            here = (lane == k) & (line == row)
            return tuple(
                jnp.where(
                    here, pltpu.roll(fields[t + 1, tile, pl.ds(top, 8), :], turn, 1), found[t]
                )
                for t in range(STEPS)
            )

        none = (jnp.zeros((8, LANES), F32),) * STEPS
        found = lax.fori_loop(0, LANES, one_panel, none, unroll=32)
        for t in range(STEPS):
            sample_ref[t : t + 1, base : base + LANES] = jnp.sum(found[t], axis=0, keepdims=True)
    leave.wait()


def edges(field, mask, visc):
    rows, cols = field.shape
    edge_rows = jax.ShapeDtypeStruct((EDGE, cols), F32)
    return pl.pallas_call(
        rows_kernel,
        grid=(1,),
        in_specs=[pl.BlockSpec((8, cols), lambda i: (0, 0))] * 3
        + [pl.BlockSpec((8, cols), lambda i: (rows // 8 - 1, 0))] * 3,
        out_specs=[pl.BlockSpec((EDGE, cols), lambda i: (0, 0))] * 2,
        out_shape=[edge_rows, edge_rows],
        compiler_params=params(56),
        cost_estimate=cost(16 * cols, 256 * cols),
    )(field, mask, visc, field, mask, visc)


def shifted(axis, first, last):
    peers = lax.axis_size(axis)
    up = [(i, i + 1) for i in range(peers - 1)]
    down = [(i + 1, i) for i in range(peers - 1)]
    return lax.ppermute(last, axis, up), lax.ppermute(first, axis, down)


def field_window(field, mask, visc, before, after, panel_cell):
    rows, cols = field.shape
    tall = -(-(rows + EDGE) // LANES) * LANES
    edge_cols = jax.ShapeDtypeStruct((EDGE, tall), F32)

    panels = panel_cell.shape[0]
    first, last, places = pl.pallas_call(
        columns_kernel,
        in_specs=[VMEM] * 6,
        out_specs=[VMEM] * 3,
        out_shape=[edge_cols, edge_cols, jax.ShapeDtypeStruct((4, panels), jnp.int32)],
        scratch_shapes=[pltpu.VMEM((tall, LANES), F32)],
        compiler_params=params(16),
        cost_estimate=cost(rows * cols, 4 * rows * cols),
    )(panel_cell.reshape(1, panels), field, mask, visc, before, after)
    south, north = shifted("panel", first, last)
    tiles = cols // LANES + 1
    height = 16 + -(-(rows + 2 * PAD - 16) // STRIP) * STRIP
    return pl.pallas_call(
        step_kernel,
        in_specs=[SMEM] + [VMEM] * 7,
        out_specs=[pl.BlockSpec(memory_space=pl.ANY), VMEM],
        out_shape=[
            jax.ShapeDtypeStruct((rows, cols), F32),
            jax.ShapeDtypeStruct((STEPS, panels), F32),
        ],
        scratch_shapes=[
            pltpu.VMEM((STEPS + 1, tiles, height, LANES), F32),
            pltpu.VMEM((tiles, height, LANES), F32),
            pltpu.VMEM((LANES, tall), F32),
            pltpu.VMEM((rows, cols), F32),
            pltpu.SemaphoreType.DMA,
        ],
        compiler_params=params(24),
        cost_estimate=cost(100 * rows * cols, 800 * rows * cols),
    )(places, field, mask, visc, before, after, south, north)


def bin_kernel(half_ref, *refs):
    members = (len(refs) - 7) // 2
    words, samples = refs[:members], refs[members : 2 * members]
    keep_ref, send_ref, low_s, high_s, weight_s, acc_s, sig_s = refs[2 * members :]
    block, local = words[0].shape
    parts = local // LANES
    high = NB // LOW
    per_row = LANES // LOW
    half_rows = NB // LANES // 8
    low_tiles = LOW // 8 + 1
    depth = 2 * LANES
    shift = LOW.bit_length() - 1
    for s in range(members):
        for j in range(parts):
            word = words[s][:, j * LANES : (j + 1) * LANES]
            at = slice((s * parts + j) * LANES, (s * parts + j + 1) * LANES)
            low_s[:, at] = (word & (LOW - 1)).astype(F32)
            high_s[:, at] = ((word >> shift) & (high - 1)).astype(F32)
            amp = (word >> 16).astype(F32) * (1.0 / AMP_SCALE)
            for t in range(STEPS):
                weight_s[t, :, at] = amp * samples[s][j, t : t + 1, :]

    one = jnp.ones((), BF16)
    zero = jnp.zeros((), BF16)
    sub = lax.broadcasted_iota(jnp.int32, (16, depth), 0) & 7

    def number(x):
        return x.astype(F32).astype(BF16)

    high_ids = [
        number(per_row * (8 * (k % half_rows) + sub) + k // half_rows) for k in range(high // 8)
    ]
    low_ids = [[number(8 * k + sub - t) for t in range(STEPS)] for k in range(low_tiles)]
    lane = lax.broadcasted_iota(jnp.int32, (8, LANES), 1)
    lanes = lax.broadcasted_iota(jnp.int32, (NB // LANES, LANES), 1)
    acc_s[...] = jnp.zeros_like(acc_s)

    def two_observers(o, u):
        def spread(ref, *lead):
            rows = [
                jnp.broadcast_to(ref[(*lead, slice(o + e, o + e + 1), at)], (8, depth))
                for e in range(2)
            ]
            return jnp.concatenate(rows).astype(BF16)

        acc = None
        for c in range(members * local // depth):
            at = slice(c * depth, (c + 1) * depth)
            low_row, high_row = spread(low_s), spread(high_s)
            weights = [spread(weight_s, t) for t in range(STEPS)]
            left = jnp.concatenate([jnp.where(ids == high_row, one, zero) for ids in high_ids])
            right = []
            for k in range(low_tiles):
                placed = zero
                for t in range(1 if k * 8 >= LOW else 0, STEPS):
                    placed = jnp.where(low_ids[k][t] == low_row, weights[t], placed)
                right.append(placed)
            term = lax.dot_general(
                left, jnp.concatenate(right), (((1,), (1,)), ((), ())), preferred_element_type=F32
            )
            acc = term if acc is None else acc + term
        acc_s[u, :, : 16 * low_tiles] = acc
        for e in range(2):
            total = None
            for j in range(per_row):
                low = (lane - LOW * j) & (LANES - 1)
                source = jnp.where(low < 8 * low_tiles, 16 * (low // 8) + 8 * e + (low & 7), LANES - 1)
                tops = [16 * (j * half_rows + g) + 8 * e for g in range(half_rows)]
                x = jnp.concatenate(
                    [jnp.take_along_axis(acc_s[u, top : top + 8], source, axis=1) for top in tops]
                )
                if j == per_row - 1:
                    x = jnp.where(lanes < LOW, pltpu.roll(x, 1, 0), x)
                total = x if total is None else total + x
            sig_s[:, o + e : o + e + 1, :] = total[:, None, :]

    for u in range(block // 2):
        two_observers(2 * u, u)
    tiles = NB // LANES // 2
    per_owner = tiles // keep_ref.shape[0]
    for r in range(tiles):
        lanes = slice(r % per_owner * LANES, (r % per_owner + 1) * LANES)
        keep_ref[r // per_owner, :, lanes] = sig_s[half_ref[0] * tiles + r]
        sent = sig_s[(1 - half_ref[0]) * tiles + r]
        send_ref[r // per_owner, :, lanes] = sent.astype(BF16)


def binned(half, words, samples, first, count):
    members = len(words)
    local = words[0].shape[1]
    block = 16
    panels = members * local
    bins = NB // 2 // members
    out = pl.BlockSpec((members, block, bins), lambda i: (0, i, 0))
    return pl.pallas_call(
        bin_kernel,
        grid=(count // block,),
        in_specs=[SMEM]
        + [pl.BlockSpec((block, local), lambda i: (first // block + i, 0))] * members
        + [pl.BlockSpec(samples[0].shape, lambda i: (0, 0, 0))] * members,
        out_specs=[out, out],
        out_shape=[
            jax.ShapeDtypeStruct((members, count, bins), F32),
            jax.ShapeDtypeStruct((members, count, bins), BF16),
        ],
        scratch_shapes=[
            pltpu.VMEM((block, panels), F32),
            pltpu.VMEM((block, panels), F32),
            pltpu.VMEM((STEPS, block, panels), F32),
            pltpu.VMEM((block // 2, 2 * NB // LOW, LANES), F32),
            pltpu.VMEM((NB // LANES, block, LANES), F32),
        ],
        compiler_params=params(40),
        cost_estimate=cost(65536 * count * panels, 8 * count * panels),
    )(half, *words, *samples)


def join_kernel(parts, me_ref, *refs):
    keeps, gots, outs = refs[:parts], refs[parts : 2 * parts], refs[2 * parts :]
    for k, out in enumerate(outs):
        owner = lax.rem(me_ref[0] + k, len(outs))
        at = 0
        for keep, got in zip(keeps, gots):
            count = keep.shape[1]
            out[at : at + count] = (keep[owner] + got[owner].astype(F32)).astype(BF16)
            at += count


def join(me, keeps, gots):
    members, _, bins = keeps[0].shape
    count = sum(keep.shape[1] for keep in keeps)
    return pl.pallas_call(
        functools.partial(join_kernel, len(keeps)),
        in_specs=[SMEM] + [VMEM] * (2 * len(keeps)),
        out_specs=[VMEM] * members,
        out_shape=[jax.ShapeDtypeStruct((count, bins), BF16)] * members,
        compiler_params=params(16),
        cost_estimate=cost(members * count * bins, 8 * members * count * bins),
    )(me, *keeps, *gots)


def place_kernel(first, width, me_ref, *refs):
    members, count, _ = refs[-2].shape
    pieces, (out_ref, wide, sems) = refs[:members], refs[-3:]
    copies = []
    for k, ref in enumerate(pieces):
        owner = lax.rem(me_ref[0] - k + members, members)
        start = pl.multiple_of(owner * width + first, 16)
        wide[k] = ref[...].astype(F32)
        copies.append(
            pltpu.make_async_copy(wide.at[k], out_ref.at[pl.ds(start, count), :], sems.at[k])
        )
        copies[-1].start()
    for copy in copies:
        copy.wait()


def place(me, pieces, signals, first, width):
    members = len(pieces)
    count, bins = pieces[0].shape
    before = [] if signals is None else [signals]
    return pl.pallas_call(
        functools.partial(place_kernel, first, width),
        in_specs=[SMEM] + [VMEM] * members + [pl.BlockSpec(memory_space=pl.ANY)] * len(before),
        out_specs=pl.BlockSpec(memory_space=pl.ANY),
        out_shape=jax.ShapeDtypeStruct((width * members, bins), F32),
        input_output_aliases={members + 1: 0} if before else {},
        scratch_shapes=[
            pltpu.VMEM((members, count, bins), F32),
            pltpu.SemaphoreType.DMA((members,)),
        ],
        compiler_params=params(16),
        cost_estimate=cost(members * count * bins, 6 * members * count * bins),
    )(me, *pieces, *before)


def on_device(field_start, fluid_mask, base_visc, panel_cell, amplitude, delay_bin):
    peers = lax.axis_size("box")
    members = peers // 2
    index = lax.axis_index("box").astype(jnp.int32).reshape(1)
    me, half = lax.rem(index, members), index // members

    def spread(parts, to):
        def perm(k):
            return [(i, i // members * members + to(i % members, k, members)) for i in range(peers)]

        return [lax.ppermute(x, "box", perm(k)) if k else x for k, x in enumerate(parts)]

    ends = edges(field_start, fluid_mask, base_visc)
    amplitude, delay_bin, *ends = lax.optimization_barrier((amplitude, delay_bin, *ends))
    before, after = shifted("box", *ends)
    packed = pack(me, amplitude, delay_bin, members)
    before, after, *packed = lax.optimization_barrier((before, after, *packed))
    words = spread(packed, target)
    field, sample = field_window(
        field_start, fluid_mask, base_visc, before, after, panel_cell
    )
    sample = lax.all_gather(sample, "panel")
    middle = members // 2
    sample, words[middle] = lax.optimization_barrier((sample, words[middle]))
    samples = spread([sample] * members, target)
    observers = words[0].shape[0]
    across = [(i, (i + members) % peers) for i in range(peers)]
    first, groups = 0, []
    for chunks in sizes(observers):
        groups.append([])
        for count in chunks:
            keep, send = binned(half, words, samples, first, count)
            keep, half = lax.optimization_barrier((keep, half))
            groups[-1].append((keep, lax.ppermute(send, "box", across)))
            first += count
    pieces, waiting = None, []
    for group in groups:
        keeps, gots = [x[0] for x in group], [x[1] for x in group]
        if pieces is not None:
            gots[-1], pieces[middle] = lax.optimization_barrier((gots[-1], pieces[middle]))
        pieces = spread(join(me, keeps, gots), lambda i, k, n: (i + k) % n)
        waiting.append(pieces)
    first, signals = 0, None
    for pieces in waiting:
        signals = place(me, pieces, signals, first, observers)
        first += pieces[0].shape[0]
    return (field, signals)


def sizes(observers):
    units = observers // 16
    ends = [-(-units * part // 16) * 16 for part in PARTS]
    counts = [end - start for start, end in zip([0] + ends, ends)]
    return [[c for c in group if c] for group in (counts[:2], counts[2:]) if any(group)]


def solution(mesh):
    placed = (
        P("box", "panel"),
        P("box", "panel"),
        P("box", "panel"),
        P(("box", "panel")),
        P("box", "panel"),
        P("box", "panel"),
    )
    return jax.shard_map(
        on_device,
        mesh=mesh,
        in_specs=placed,
        out_specs=(P("box", "panel"), P("panel", "box")),
        check_vma=False,
    )
```

```python
import functools

import jax
import jax.numpy as jnp
from jax import lax
from jax.experimental import pallas as pl
from jax.experimental.pallas import tpu as pltpu
from jax.sharding import PartitionSpec as P

F32 = jnp.float32
BF16 = jnp.bfloat16
STEPS = 4
NB = 2048
LOW = 32
LANES = 128
EDGE = 2 * STEPS
PAD = 16
STRIP = 32
AMP_SCALE = 4096.0
PARTS = (8, 13, 16)
VMEM = pl.BlockSpec(memory_space=pltpu.VMEM)
SMEM = pl.BlockSpec(memory_space=pltpu.SMEM)


def params(mib):
    return pltpu.CompilerParams(vmem_limit_bytes=mib << 20)


def cost(flops, size):
    return pl.CostEstimate(flops=flops, bytes_accessed=size, transcendentals=0)


def target(me, k, members):
    return me ^ k if members & (members - 1) == 0 else (me + k) % members


def pack_kernel(me_ref, amp_ref, bin_ref, *refs):
    outs, turned = refs[:-1], refs[-1]
    scaled = (amp_ref[...].astype(F32) * AMP_SCALE).astype(jnp.int32)
    turned[...] = jnp.transpose((scaled << 16) | bin_ref[...])
    width = outs[0].shape[0]
    for k, out in enumerate(outs):
        first = pl.multiple_of(target(me_ref[0], k, len(outs)) * width, 8)
        out[...] = turned[pl.ds(first, width), :]


def pack(me, amplitude, delay_bin, members):
    panels, observers = amplitude.shape
    width = observers // members
    block = pl.BlockSpec((LANES, observers), lambda i: (i, 0))
    out = jax.ShapeDtypeStruct((width, panels), jnp.int32)
    return pl.pallas_call(
        pack_kernel,
        grid=(panels // LANES,),
        in_specs=[SMEM, block, block],
        out_specs=[pl.BlockSpec((width, LANES), lambda i: (0, i))] * members,
        out_shape=[out] * members,
        scratch_shapes=[pltpu.VMEM((observers, LANES), jnp.int32)],
        compiler_params=params(56),
        cost_estimate=cost(panels * observers, 10 * panels * observers),
    )(me, amplitude, delay_bin)


def coded(mask, visc):
    return jnp.where(mask != 0, visc, 0.0)


def rows_kernel(f_top, m_top, v_top, f_end, m_end, v_end, first_ref, last_ref):
    first_ref[:STEPS] = f_top[:STEPS]
    first_ref[STEPS:] = coded(m_top[:STEPS], v_top[:STEPS])
    last_ref[:STEPS] = f_end[8 - STEPS :]
    last_ref[STEPS:] = coded(m_end[8 - STEPS :], v_end[8 - STEPS :])


def columns_kernel(
    cell_ref, field_ref, mask_ref, visc_ref, before_ref, after_ref, first_ref, last_ref, place_ref, tall
):
    rows, cols = field_ref.shape
    cell = cell_ref[...]
    row = lax.div(cell, cols)
    col = cell - row * cols
    panel = lax.broadcasted_iota(jnp.int32, cell.shape, 1)
    place_ref[0:1] = col // LANES
    place_ref[1:2] = row // 8 * 8 + PAD
    place_ref[2:3] = row & 7
    place_ref[3:4] = (panel - col) & (LANES - 1)
    tall[...] = jnp.zeros_like(tall)
    for part in range(2):
        halo = slice(part * STEPS, (part + 1) * STEPS)
        for start, low, out in ((0, 0, first_ref), (cols - LANES, LANES - STEPS, last_ref)):
            lanes = slice(start, start + LANES)
            if part:
                tall[:rows] = coded(mask_ref[:, lanes], visc_ref[:, lanes])
            else:
                tall[:rows] = field_ref[:, lanes]
            tall[rows : rows + STEPS] = after_ref[halo, lanes]
            tall[rows + STEPS : rows + EDGE] = before_ref[halo, lanes]
            out[halo] = jnp.transpose(tall[...])[low : low + STEPS]


def step_kernel(
    cell_ref,
    field_ref,
    mask_ref,
    visc_ref,
    before_ref,
    after_ref,
    south_ref,
    north_ref,
    end_ref,
    sample_ref,
    fields,
    visc,
    wide,
    last,
    sem,
):
    rows, cols = field_ref.shape
    panels = sample_ref.shape[1]
    tiles, height, _ = visc.shape
    wide[...] = jnp.zeros_like(wide)
    for part, buf in enumerate((fields.at[0], visc)):
        halo = slice(part * STEPS, (part + 1) * STEPS)
        wide[:STEPS] = north_ref[halo]
        wide[LANES - STEPS :] = south_ref[halo]
        side = jnp.transpose(wide[...])
        for k in range(tiles):
            at = slice(k * LANES, (k + 1) * LANES)
            buf[k, :PAD] = jnp.zeros((PAD, LANES), F32)
            buf[k, PAD + rows :] = jnp.zeros((height - PAD - rows, LANES), F32)
            if k == tiles - 1:
                inside, before, after = (
                    side[:rows],
                    side[rows + STEPS : rows + EDGE],
                    side[rows : rows + STEPS],
                )
            else:
                inside = coded(mask_ref[:, at], visc_ref[:, at]) if part else field_ref[:, at]
                before, after = before_ref[halo, at], after_ref[halo, at]
            buf[k, PAD : PAD + rows] = inside
            buf[k, PAD - STEPS : PAD] = before
            buf[k, PAD + rows : PAD + rows + STEPS] = after

    first_lane = lax.broadcasted_iota(jnp.int32, (STRIP, LANES), 1) == 0
    last_lane = lax.broadcasted_iota(jnp.int32, (STRIP, LANES), 1) == LANES - 1
    for step in range(STEPS):
        old, new = fields.at[step], fields.at[step + 1]
        for k in range(tiles):
            new[k, :8] = jnp.zeros((8, LANES), F32)
            new[k, height - 8 :] = jnp.zeros((8, LANES), F32)

        def one_strip(i, carry):
            top = pl.multiple_of(i * STRIP, 8)
            centers = [old[k, pl.ds(top + 8, STRIP), :] for k in range(tiles)]
            right = [pltpu.roll(x, 1, 1) for x in centers]
            left = [pltpu.roll(x, LANES - 1, 1) for x in centers]
            for k in range(tiles):
                window = old[k, pl.ds(top, STRIP + 16), :]
                base = visc[k, pl.ds(top + 8, STRIP), :]
                center = centers[k]
                west = pltpu.roll(window, 1, 0)[8 : 8 + STRIP]
                east = pltpu.roll(window, STRIP + 15, 0)[8 : 8 + STRIP]
                south = jnp.where(first_lane, right[k - 1], right[k])
                north = jnp.where(last_lane, left[(k + 1) % tiles], left[k])
                diff_x = east - west
                diff_y = north - south
                square = diff_x * diff_x + diff_y * diff_y
                norm = square * lax.rsqrt(jnp.maximum(square, 1e-37))
                viscosity = base + 0.05 * norm / (2.0 + norm)
                around = (east + west) + (north + south)
                update = 0.75 * center + 0.15 * west + 0.1 * south
                update = update + viscosity * (around - 4.0 * center)
                new[k, pl.ds(top + 8, STRIP), :] = jnp.where(base > 0.0, update, 0.0)
            return carry

        strips = (height - 16) // STRIP
        lax.fori_loop(0, strips, one_strip, 0, unroll=strips)
    for k in range(tiles - 1):
        last[:, k * LANES : (k + 1) * LANES] = fields[STEPS, k, PAD : PAD + rows, :]
    leave = pltpu.make_async_copy(last, end_ref, sem)
    leave.start()

    lane = lax.broadcasted_iota(jnp.int32, (8, LANES), 1)
    line = lax.broadcasted_iota(jnp.int32, (8, LANES), 0)
    for base in range(0, panels, LANES):

        def one_panel(k, found):
            tile, top, row, turn = [cell_ref[c, base + k] for c in range(4)]
            top = pl.multiple_of(top, 8)
            here = (lane == k) & (line == row)
            return tuple(
                jnp.where(
                    here, pltpu.roll(fields[t + 1, tile, pl.ds(top, 8), :], turn, 1), found[t]
                )
                for t in range(STEPS)
            )

        none = (jnp.zeros((8, LANES), F32),) * STEPS
        found = lax.fori_loop(0, LANES, one_panel, none, unroll=32)
        for t in range(STEPS):
            sample_ref[t : t + 1, base : base + LANES] = jnp.sum(found[t], axis=0, keepdims=True)
    leave.wait()


def edges(field, mask, visc):
    rows, cols = field.shape
    edge_rows = jax.ShapeDtypeStruct((EDGE, cols), F32)
    return pl.pallas_call(
        rows_kernel,
        grid=(1,),
        in_specs=[pl.BlockSpec((8, cols), lambda i: (0, 0))] * 3
        + [pl.BlockSpec((8, cols), lambda i: (rows // 8 - 1, 0))] * 3,
        out_specs=[pl.BlockSpec((EDGE, cols), lambda i: (0, 0))] * 2,
        out_shape=[edge_rows, edge_rows],
        compiler_params=params(56),
        cost_estimate=cost(16 * cols, 256 * cols),
    )(field, mask, visc, field, mask, visc)


def shifted(axis, first, last):
    peers = lax.axis_size(axis)
    up = [(i, i + 1) for i in range(peers - 1)]
    down = [(i + 1, i) for i in range(peers - 1)]
    return lax.ppermute(last, axis, up), lax.ppermute(first, axis, down)


def field_window(field, mask, visc, before, after, panel_cell):
    rows, cols = field.shape
    tall = -(-(rows + EDGE) // LANES) * LANES
    edge_cols = jax.ShapeDtypeStruct((EDGE, tall), F32)

    panels = panel_cell.shape[0]
    first, last, places = pl.pallas_call(
        columns_kernel,
        in_specs=[VMEM] * 6,
        out_specs=[VMEM] * 3,
        out_shape=[edge_cols, edge_cols, jax.ShapeDtypeStruct((4, panels), jnp.int32)],
        scratch_shapes=[pltpu.VMEM((tall, LANES), F32)],
        compiler_params=params(16),
        cost_estimate=cost(rows * cols, 4 * rows * cols),
    )(panel_cell.reshape(1, panels), field, mask, visc, before, after)
    south, north = shifted("panel", first, last)
    tiles = cols // LANES + 1
    height = 16 + -(-(rows + 2 * PAD - 16) // STRIP) * STRIP
    return pl.pallas_call(
        step_kernel,
        in_specs=[SMEM] + [VMEM] * 7,
        out_specs=[pl.BlockSpec(memory_space=pl.ANY), VMEM],
        out_shape=[
            jax.ShapeDtypeStruct((rows, cols), F32),
            jax.ShapeDtypeStruct((STEPS, panels), F32),
        ],
        scratch_shapes=[
            pltpu.VMEM((STEPS + 1, tiles, height, LANES), F32),
            pltpu.VMEM((tiles, height, LANES), F32),
            pltpu.VMEM((LANES, tall), F32),
            pltpu.VMEM((rows, cols), F32),
            pltpu.SemaphoreType.DMA,
        ],
        compiler_params=params(24),
        cost_estimate=cost(100 * rows * cols, 800 * rows * cols),
    )(places, field, mask, visc, before, after, south, north)


def bin_kernel(half_ref, *refs):
    members = (len(refs) - 7) // 2
    words, samples = refs[:members], refs[members : 2 * members]
    keep_ref, send_ref, low_s, high_s, weight_s, acc_s, sig_s = refs[2 * members :]
    block, local = words[0].shape
    parts = local // LANES
    high = NB // LOW
    per_row = LANES // LOW
    half_rows = NB // LANES // 8
    low_tiles = LOW // 8 + 1
    depth = 2 * LANES
    shift = LOW.bit_length() - 1
    for s in range(members):
        for j in range(parts):
            word = words[s][:, j * LANES : (j + 1) * LANES]
            at = slice((s * parts + j) * LANES, (s * parts + j + 1) * LANES)
            low_s[:, at] = (word & (LOW - 1)).astype(F32)
            high_s[:, at] = ((word >> shift) & (high - 1)).astype(F32)
            amp = (word >> 16).astype(F32) * (1.0 / AMP_SCALE)
            for t in range(STEPS):
                weight_s[t, :, at] = amp * samples[s][j, t : t + 1, :]

    one = jnp.ones((), BF16)
    zero = jnp.zeros((), BF16)
    sub = lax.broadcasted_iota(jnp.int32, (16, depth), 0) & 7

    def number(x):
        return x.astype(F32).astype(BF16)

    high_ids = [
        number(per_row * (8 * (k % half_rows) + sub) + k // half_rows) for k in range(high // 8)
    ]
    low_ids = [[number(8 * k + sub - t) for t in range(STEPS)] for k in range(low_tiles)]
    lane = lax.broadcasted_iota(jnp.int32, (8, LANES), 1)
    lanes = lax.broadcasted_iota(jnp.int32, (NB // LANES, LANES), 1)
    acc_s[...] = jnp.zeros_like(acc_s)

    def two_observers(o, u):
        def spread(ref, *lead):
            rows = [
                jnp.broadcast_to(ref[(*lead, slice(o + e, o + e + 1), at)], (8, depth))
                for e in range(2)
            ]
            return jnp.concatenate(rows).astype(BF16)

        acc = None
        for c in range(members * local // depth):
            at = slice(c * depth, (c + 1) * depth)
            low_row, high_row = spread(low_s), spread(high_s)
            weights = [spread(weight_s, t) for t in range(STEPS)]
            left = jnp.concatenate([jnp.where(ids == high_row, one, zero) for ids in high_ids])
            right = []
            for k in range(low_tiles):
                placed = zero
                for t in range(1 if k * 8 >= LOW else 0, STEPS):
                    placed = jnp.where(low_ids[k][t] == low_row, weights[t], placed)
                right.append(placed)
            term = lax.dot_general(
                left, jnp.concatenate(right), (((1,), (1,)), ((), ())), preferred_element_type=F32
            )
            acc = term if acc is None else acc + term
        acc_s[u, :, : 16 * low_tiles] = acc
        for e in range(2):
            total = None
            for j in range(per_row):
                low = (lane - LOW * j) & (LANES - 1)
                source = jnp.where(low < 8 * low_tiles, 16 * (low // 8) + 8 * e + (low & 7), LANES - 1)
                tops = [16 * (j * half_rows + g) + 8 * e for g in range(half_rows)]
                x = jnp.concatenate(
                    [jnp.take_along_axis(acc_s[u, top : top + 8], source, axis=1) for top in tops]
                )
                if j == per_row - 1:
                    x = jnp.where(lanes < LOW, pltpu.roll(x, 1, 0), x)
                total = x if total is None else total + x
            sig_s[:, o + e : o + e + 1, :] = total[:, None, :]

    for u in range(block // 2):
        two_observers(2 * u, u)
    tiles = NB // LANES // 2
    per_owner = tiles // keep_ref.shape[0]
    for r in range(tiles):
        lanes = slice(r % per_owner * LANES, (r % per_owner + 1) * LANES)
        keep_ref[r // per_owner, :, lanes] = sig_s[half_ref[0] * tiles + r]
        sent = sig_s[(1 - half_ref[0]) * tiles + r]
        send_ref[r // per_owner, :, lanes] = sent.astype(BF16)


def binned(half, words, samples, first, count):
    members = len(words)
    local = words[0].shape[1]
    block = 16
    panels = members * local
    bins = NB // 2 // members
    out = pl.BlockSpec((members, block, bins), lambda i: (0, i, 0))
    return pl.pallas_call(
        bin_kernel,
        grid=(count // block,),
        in_specs=[SMEM]
        + [pl.BlockSpec((block, local), lambda i: (first // block + i, 0))] * members
        + [pl.BlockSpec(samples[0].shape, lambda i: (0, 0, 0))] * members,
        out_specs=[out, out],
        out_shape=[
            jax.ShapeDtypeStruct((members, count, bins), F32),
            jax.ShapeDtypeStruct((members, count, bins), BF16),
        ],
        scratch_shapes=[
            pltpu.VMEM((block, panels), F32),
            pltpu.VMEM((block, panels), F32),
            pltpu.VMEM((STEPS, block, panels), F32),
            pltpu.VMEM((block // 2, 2 * NB // LOW, LANES), F32),
            pltpu.VMEM((NB // LANES, block, LANES), F32),
        ],
        compiler_params=params(40),
        cost_estimate=cost(65536 * count * panels, 8 * count * panels),
    )(half, *words, *samples)


def join_kernel(parts, me_ref, *refs):
    keeps, gots, outs = refs[:parts], refs[parts : 2 * parts], refs[2 * parts :]
    for k, out in enumerate(outs):
        owner = lax.rem(me_ref[0] + k, len(outs))
        at = 0
        for keep, got in zip(keeps, gots):
            count = keep.shape[1]
            out[at : at + count] = (keep[owner] + got[owner].astype(F32)).astype(BF16)
            at += count


def join(me, keeps, gots):
    members, _, bins = keeps[0].shape
    count = sum(keep.shape[1] for keep in keeps)
    return pl.pallas_call(
        functools.partial(join_kernel, len(keeps)),
        in_specs=[SMEM] + [VMEM] * (2 * len(keeps)),
        out_specs=[VMEM] * members,
        out_shape=[jax.ShapeDtypeStruct((count, bins), BF16)] * members,
        compiler_params=params(16),
        cost_estimate=cost(members * count * bins, 8 * members * count * bins),
    )(me, *keeps, *gots)


def place_kernel(first, width, me_ref, *refs):
    members, count, _ = refs[-2].shape
    pieces, (out_ref, wide, sems) = refs[:members], refs[-3:]
    copies = []
    for k, ref in enumerate(pieces):
        owner = lax.rem(me_ref[0] - k + members, members)
        start = pl.multiple_of(owner * width + first, 16)
        wide[k] = ref[...].astype(F32)
        copies.append(
            pltpu.make_async_copy(wide.at[k], out_ref.at[pl.ds(start, count), :], sems.at[k])
        )
        copies[-1].start()
    for copy in copies:
        copy.wait()


def place(me, pieces, signals, first, width):
    members = len(pieces)
    count, bins = pieces[0].shape
    before = [] if signals is None else [signals]
    return pl.pallas_call(
        functools.partial(place_kernel, first, width),
        in_specs=[SMEM] + [VMEM] * members + [pl.BlockSpec(memory_space=pl.ANY)] * len(before),
        out_specs=pl.BlockSpec(memory_space=pl.ANY),
        out_shape=jax.ShapeDtypeStruct((width * members, bins), F32),
        input_output_aliases={members + 1: 0} if before else {},
        scratch_shapes=[
            pltpu.VMEM((members, count, bins), F32),
            pltpu.SemaphoreType.DMA((members,)),
        ],
        compiler_params=params(16),
        cost_estimate=cost(members * count * bins, 6 * members * count * bins),
    )(me, *pieces, *before)


def on_device(field_start, fluid_mask, base_visc, panel_cell, amplitude, delay_bin):
    peers = lax.axis_size("box")
    members = peers // 2
    index = lax.axis_index("box").astype(jnp.int32).reshape(1)
    me, half = lax.rem(index, members), index // members

    def spread(parts, to):
        def perm(k):
            return [(i, i // members * members + to(i % members, k, members)) for i in range(peers)]

        return [lax.ppermute(x, "box", perm(k)) if k else x for k, x in enumerate(parts)]

    ends = edges(field_start, fluid_mask, base_visc)
    amplitude, delay_bin, *ends = lax.optimization_barrier((amplitude, delay_bin, *ends))
    before, after = shifted("box", *ends)
    packed = pack(me, amplitude, delay_bin, members)
    before, after, *packed = lax.optimization_barrier((before, after, *packed))
    words = spread(packed, target)
    field, sample = field_window(
        field_start, fluid_mask, base_visc, before, after, panel_cell
    )
    sample = lax.all_gather(sample, "panel")
    middle = members // 2
    sample, words[middle] = lax.optimization_barrier((sample, words[middle]))
    samples = spread([sample] * members, target)
    observers = words[0].shape[0]
    across = [(i, (i + members) % peers) for i in range(peers)]
    first, groups = 0, []
    for chunks in sizes(observers):
        groups.append([])
        for count in chunks:
            keep, send = binned(half, words, samples, first, count)
            keep, half = lax.optimization_barrier((keep, half))
            groups[-1].append((keep, lax.ppermute(send, "box", across)))
            first += count
    pieces, waiting = None, []
    for group in groups:
        keeps, gots = [x[0] for x in group], [x[1] for x in group]
        if pieces is not None:
            gots[-1], pieces[middle] = lax.optimization_barrier((gots[-1], pieces[middle]))
        pieces = spread(join(me, keeps, gots), lambda i, k, n: (i + k) % n)
        waiting.append(pieces)
    first, signals = 0, None
    for pieces in waiting:
        signals = place(me, pieces, signals, first, observers)
        first += pieces[0].shape[0]
    return (field, signals)


def sizes(observers):
    units = observers // 16
    ends = [-(-units * part // 16) * 16 for part in PARTS]
    counts = [end - start for start, end in zip([0] + ends, ends)]
    return [[c for c in counts if c]]


def solution(mesh):
    placed = (
        P("box", "panel"),
        P("box", "panel"),
        P("box", "panel"),
        P(("box", "panel")),
        P("box", "panel"),
        P("box", "panel"),
    )
    return jax.shard_map(
        on_device,
        mesh=mesh,
        in_specs=placed,
        out_specs=(P("box", "panel"), P("panel", "box")),
        check_vma=False,
    )
```
